256 devices in a mesh: pts: 128 (over z, y, x), rep: 2 (over core).
Axes of the slice: x: 4, y: 4, z: 8, core: 2. Of those that a mesh axis runs over, the one named last changes fastest.
Arguments:
- feats: bfloat16 [2, 64, 131072], P('rep', None, 'pts'), may hold values from -6 to 6
- hilbert_of_z: int32 [2, 131072], P('rep', 'pts'), may hold values from 0 to 131071, as said below
- pool_owner: int32 [2, 131072, 1], P('rep', 'pts'), may hold values from 0 to 127; in each aligned block of 1024 rows (0 to 1023, 1024 to 2047, ..., all dimensions but the last counted through in order) at most 16 rows name the same one
- pool_slot: int32 [2, 131072], P('rep', 'pts'), may hold values from 0 to 255
- qkv_weight: bfloat16 [192, 64], replicated, may hold values from -0.75 to 0.75
- out_weight: bfloat16 [64, 64], replicated, may hold values from -0.75 to 0.75
- pool_weight: bfloat16 [128, 64], replicated, may hold values from -0.75 to 0.75
- norm_gain: float32 [64], replicated, may hold values from 0.1 to 1.9
- pooled_grad: bfloat16 [2, 128, 32768], P('rep', None, 'pts'), may hold values from -6 to 6
Outputs:
- pooled: bfloat16 [2, 128, 32768], P('rep', None, 'pts')
- feat_grad: bfloat16 [2, 64, 131072], P('rep', None, 'pts')
- qkv_grad: float32 [192, 64], replicated
- out_grad: float32 [64, 64], replicated
- pool_grad: float32 [128, 64], replicated
- gain_grad: float32 [64], replicated
The draws below stay inside these ranges and needn't reach their ends.
Inputs may be any that keep to these rules, and one draw needn't show every extreme that they name: For each window, hilbert_of_z is a permutation of the 131072 positions; the 1024 z-order points of each shard land on each Hilbert shard of 1024 positions exactly 1024 // 128 times. `pool_owner`: within the 1024 points of one device, no owner is named more than 16 times, a bound that some block reaches.
All inputs are finite; a program needn't handle non-finite values.
Results may differ from the reference program's by a relative error of at most 0.0084.
Values may be sent and summed in bfloat16 or wider, within the bound.
No kernel may reach another device: no remote copies, remote signals or barrier semaphores. Data moves between devices by JAX's collectives and lax.ppermute only.
A program may use at most 64 MiB of HBM per device.

```python
import math
import jax
import jax.numpy as jnp
import numpy as np
from jax import lax

C = 64
HEADS = 4
PATCH = 1024
C2 = 128
P_DEV = 1024
HEAD_DIM = 16
SHARDS = 128
WINDOWS = 2
NPTS = 131072
CAP = 16
CL_DEV = 256
CLUSTERS = 32768


def draw_hilbert_of_z(key, part):
    key = jax.random.fold_in(key, 11)
    shard_count = NPTS // P_DEV
    per_peer = P_DEV // shard_count

    def one_window(window_key):
        first_key, second_key = jax.random.split(window_key)
        source_perm = jax.vmap(lambda k: jax.random.permutation(k, P_DEV))(jax.random.split(first_key, shard_count))
        target_perm = jax.vmap(lambda k: jax.random.permutation(k, P_DEV))(jax.random.split(second_key, shard_count))
        grouped = source_perm.reshape(shard_count, shard_count, per_peer).astype(jnp.int32)
        placed = target_perm.reshape(shard_count, shard_count, per_peer).transpose(1, 0, 2).astype(jnp.int32)
        shard_ids = jnp.arange(shard_count, dtype=jnp.int32)
        z_index = shard_ids[:, None, None] * P_DEV + grouped
        h_index = shard_ids[None, :, None] * P_DEV + placed
        return jnp.zeros((NPTS,), jnp.int32).at[z_index.reshape(-1)].set(h_index.reshape(-1))
    return jax.vmap(one_window)(jax.random.split(key, WINDOWS))


def touch_ends(values, stream_key, least, high):
    shape = values.shape
    place = [jax.random.randint(jax.random.fold_in(stream_key, axis), (), 0, shape[axis]) for axis in range(len(shape))]
    values = values.at[tuple(place)].set(least)
    longest = shape.index(max(shape))
    place[longest] = (place[longest] + 1) % shape[longest]
    return values.at[tuple(place)].set(high)


def block_levels(rng, shape, cuts, least, top_value):
    loudness, own = 1.0, jax.random.fold_in(rng, 6)
    for position, parts in cuts:
        steps = jnp.exp(jax.random.uniform(jax.random.fold_in(own, position), (parts,), jnp.float32, least / len(cuts), top_value / len(cuts)))
        loudness = loudness * jnp.repeat(steps, shape[position] // parts).reshape([-1 if axis == position else 1 for axis in range(len(shape))])
    return loudness


def shared_out(stream_key, own, number, rows, count, top, reach, lean):
    order = jax.random.permutation(stream_key, count)
    packed, ordinary = load_shares(count, rows * top, reach, lean, True), load_shares(count, rows * top, reach, lean, False)
    places = jnp.arange(count)

    def named(lengths, rotation):
        used = int((lengths > 0).sum())
        fixed = max(1, used // 4)
        passed = fixed + (places - fixed + rotation * (used - fixed)) % max(1, count - fixed)
        return jnp.zeros((count,), jnp.int32).at[order[jnp.where(places < fixed, places, passed)]].set(jnp.asarray(lengths, jnp.int32))

    lengths = jnp.where(number % 4 == 0, named(packed, number // 4), named(ordinary, number - number // 4 - 1))
    mixed = jax.random.permutation(jax.random.fold_in(own, 3), count)
    giver, taker = mixed[0:count // 2 * 2:2], mixed[1:count // 2 * 2:2]
    margin = jnp.minimum(lengths[giver] - 1, reach - lengths[taker]) // 2
    margin = jnp.where((giver == order[0]) | (taker == order[0]) | (lengths[taker] == 0), 0, jnp.maximum(margin, 0))
    passed = jax.random.randint(jax.random.fold_in(own, 4), (count // 2,), 0, 1 << 20) % (margin + 1)
    lengths = lengths.at[giver].add(-passed).at[taker].add(passed)
    labels = jnp.searchsorted(jnp.cumsum(lengths), jnp.arange(rows * top), side="right").astype(jnp.int32)
    table = labels.reshape(top, rows).T
    table = table[jax.random.permutation(jax.random.fold_in(own, 1), rows)]
    rotation = jax.random.randint(jax.random.fold_in(own, 2), (rows, 1), 0, top)
    return jnp.take_along_axis(table, (jnp.arange(top)[None, :] + rotation) % top, axis=1)


def load_shares(amount, total, bound, lean, full):
    weights = [(1 << 20) // math.isqrt(standing ** lean) + 1 for standing in range(1, amount + 1)]
    largest = bound if full else min(bound, max(-(-total // amount), total * weights[0] // sum(weights)))
    least = 1 if total - largest >= amount - 1 else 0
    given, surplus = [largest] + [least] * (amount - 1), total - largest - least * (amount - 1)
    while surplus > 0:
        movable = [i for i in range(1, amount) if given[i] < largest] or [i for i in range(1, amount) if given[i] < bound]
        pool, remaining = sum([weights[i] for i in movable]), surplus
        for i in movable:
            more = min(bound - given[i], max(1, remaining * weights[i] // pool), surplus)
            given[i] = given[i] + more
            surplus = surplus - more
    return np.array(given)


def gaussian(key, shape, deviation, limit, cuts=(), held_as=jnp.bfloat16):
    result = jax.random.normal(key, shape, jnp.float32) * deviation
    if len(cuts) > 0:
        result = block_levels(key, shape, cuts, -0.22, 0.18) * result
    return jnp.clip(result, min=-limit, max=limit).astype(held_as)


def setup_inputs(seed: int = 0) -> dict:
    seeds = jax.random.split(jax.random.key(seed), 10)
    feats = gaussian(seeds[0], (WINDOWS, C, NPTS), 1.0, 6.0, ((0, 2), (2, 128)))
    hilbert_of_z = draw_hilbert_of_z(jax.random.fold_in(seeds[9], 71), 0)
    pool_owner_keys = jax.random.split(jax.random.fold_in(seeds[2], 1), WINDOWS * NPTS // P_DEV)
    pool_owner_turns = jax.random.permutation(jax.random.fold_in(seeds[2], 3), WINDOWS * NPTS // P_DEV)
    pool_owner = jax.vmap(lambda own, number: shared_out(jax.random.fold_in(seeds[2], 2), own, number, P_DEV, SHARDS, 1, CAP, 2))(pool_owner_keys, pool_owner_turns).reshape((WINDOWS, NPTS, 1))
    pool_slot = touch_ends(jax.random.randint(seeds[3], (WINDOWS, NPTS), 0, CL_DEV), jax.random.fold_in(seeds[3], 1), 0, CL_DEV - 1).astype(jnp.int32)
    qkv_weight = gaussian(seeds[4], (3 * C, C), C ** -0.5, 0.75)
    out_weight = gaussian(seeds[5], (C, C), C ** -0.5, 0.75)
    pool_weight = gaussian(seeds[6], (C2, C), C ** -0.5, 0.75)
    norm_gain = jnp.clip(1.0 + 0.18 * jax.random.normal(seeds[7], (C,), jnp.float32), 0.1, 1.9)
    pooled_grad = gaussian(seeds[8], (WINDOWS, C2, CLUSTERS), 1.0, 6.0, ((0, 2), (2, 128)))
    return dict(feats=feats, hilbert_of_z=hilbert_of_z, pool_owner=pool_owner, pool_slot=pool_slot, qkv_weight=qkv_weight, out_weight=out_weight, pool_weight=pool_weight, norm_gain=norm_gain, pooled_grad=pooled_grad)


NORM_EPS = 1e-05

def layer_norm(inputs, norm_gain):
    floats = inputs.astype(jnp.float32)
    centred = floats - lax.optimization_barrier(jnp.mean(floats, axis=0, keepdims=True))
    inverse_std = lax.rsqrt(lax.optimization_barrier(jnp.mean(centred * centred, axis=0, keepdims=True)) + NORM_EPS)
    normed = centred * inverse_std
    hidden = (norm_gain[:, None] * normed).astype(jnp.bfloat16)
    return (floats, normed, inverse_std, hidden)

def probabilities(queries, key_rows):
    scores = jnp.dot(queries.T, key_rows, preferred_element_type=jnp.float32) * HEAD_DIM ** (-0.5)
    weights = jnp.exp(scores)
    return weights / lax.optimization_barrier(jnp.sum(weights, axis=1, keepdims=True))

def attend_forward(triple):
    rounded = probabilities(triple[0], triple[1]).astype(jnp.bfloat16)
    return jnp.dot(triple[2], rounded.T, preferred_element_type=jnp.float32).astype(jnp.bfloat16)

def attend_backward(inputs):
    triple, upstream = inputs
    queries, key_rows, values = (triple[0], triple[1], triple[2])
    probs = probabilities(queries, key_rows)
    rounded = probs.astype(jnp.bfloat16)
    grad_values = jnp.dot(upstream, rounded, preferred_element_type=jnp.float32)
    grad_probs = jnp.dot(upstream.T, values, preferred_element_type=jnp.float32)
    grad_scores = probs * (grad_probs - lax.optimization_barrier(jnp.sum(probs * grad_probs, axis=1, keepdims=True))) * HEAD_DIM ** (-0.5)
    grad_scores = grad_scores.astype(jnp.bfloat16)
    grad_queries = jnp.dot(key_rows, grad_scores.T, preferred_element_type=jnp.float32)
    grad_keys = jnp.dot(queries, grad_scores, preferred_element_type=jnp.float32)
    return jnp.stack([grad_queries, grad_keys, grad_values]).astype(jnp.bfloat16)

def split_heads(qkv_rows):
    patches = qkv_rows.shape[1] // PATCH
    shaped = qkv_rows.reshape(3, HEADS, HEAD_DIM, patches, PATCH).transpose(3, 1, 0, 2, 4)
    return shaped.reshape(patches * HEADS, 3, HEAD_DIM, PATCH)

def split_single(head_rows):
    patches = head_rows.shape[1] // PATCH
    shaped = head_rows.reshape(HEADS, HEAD_DIM, patches, PATCH).transpose(2, 0, 1, 3)
    return shaped.reshape(patches * HEADS, HEAD_DIM, PATCH)

def merge_heads(items, length):
    patches = length // PATCH
    return items.reshape(patches, HEADS, HEAD_DIM, PATCH).transpose(1, 2, 0, 3).reshape(HEADS * HEAD_DIM, length)

def merge_triples(items, length):
    patches = length // PATCH
    shaped = items.reshape(patches, HEADS, 3, HEAD_DIM, PATCH).transpose(2, 1, 3, 0, 4)
    return shaped.reshape(3 * HEADS * HEAD_DIM, length)

def block_forward(hilbert_rows, qkv_weight, out_weight, norm_gain):
    floats, normed, inverse_std, hidden = layer_norm(hilbert_rows, norm_gain)
    qkv_rows = jnp.dot(qkv_weight, hidden, preferred_element_type=jnp.float32).astype(jnp.bfloat16)
    triples = split_heads(qkv_rows)
    attended = merge_heads(lax.map(attend_forward, triples), hilbert_rows.shape[1])
    mixed = (floats + jnp.dot(out_weight, attended, preferred_element_type=jnp.float32)).astype(jnp.bfloat16)
    return (mixed, (normed, inverse_std, hidden, triples, attended))

def block_backward(upstream, saved, qkv_weight, out_weight, norm_gain):
    normed, inverse_std, hidden, triples, attended = saved
    length = upstream.shape[1]
    grad_out_weight = jnp.dot(upstream, attended.T, preferred_element_type=jnp.float32)
    grad_attended = jnp.dot(out_weight.T, upstream, preferred_element_type=jnp.float32).astype(jnp.bfloat16)
    grad_triples = lax.map(attend_backward, (triples, split_single(grad_attended)))
    grad_qkv = merge_triples(grad_triples, length)
    grad_qkv_weight = jnp.dot(grad_qkv, hidden.T, preferred_element_type=jnp.float32)
    grad_hidden = jnp.dot(qkv_weight.T, grad_qkv, preferred_element_type=jnp.float32)
    grad_gain = lax.optimization_barrier(jnp.sum(grad_hidden * normed, axis=1))
    grad_normed = grad_hidden * norm_gain[:, None]
    grad_norm_in = inverse_std * (grad_normed - lax.optimization_barrier(jnp.mean(grad_normed, axis=0, keepdims=True)) - normed * lax.optimization_barrier(jnp.mean(grad_normed * normed, axis=0, keepdims=True)))
    grad_rows = (upstream.astype(jnp.float32) + grad_norm_in).astype(jnp.bfloat16)
    return (grad_rows, grad_qkv_weight, grad_out_weight, grad_gain)

def reference(feats, hilbert_of_z, pool_owner, pool_slot, qkv_weight, out_weight, pool_weight, norm_gain, pooled_grad):
    pooled_list = []
    grad_list = []
    qkv_total = jnp.zeros((3 * C, C), jnp.float32)
    out_total = jnp.zeros((C, C), jnp.float32)
    pool_total = jnp.zeros((C2, C), jnp.float32)
    gain_total = jnp.zeros((C,), jnp.float32)
    for window in range(WINDOWS):
        source_rows = feats[window]
        positions = hilbert_of_z[window]
        hilbert_rows = jnp.zeros_like(source_rows).at[:, positions].set(source_rows)
        mixed, saved = block_forward(hilbert_rows, qkv_weight, out_weight, norm_gain)
        cluster = pool_owner[window, :, 0] * CL_DEV + pool_slot[window]
        sums = jax.ops.segment_sum(mixed.T.astype(jnp.float32), cluster, num_segments=CLUSTERS)
        counts = jax.ops.segment_sum(jnp.ones(cluster.shape, jnp.float32), cluster, num_segments=CLUSTERS)
        denom = jnp.maximum(counts, 1.0)
        pooled_mean = (sums / denom[:, None]).T.astype(jnp.bfloat16)
        pooled_list.append(jnp.dot(pool_weight, pooled_mean, preferred_element_type=jnp.float32).astype(jnp.bfloat16))
        upstream_pool = pooled_grad[window]
        pool_total = pool_total + jnp.dot(upstream_pool, pooled_mean.T, preferred_element_type=jnp.float32)
        grad_mean = (jnp.dot(pool_weight.T, upstream_pool, preferred_element_type=jnp.float32) / denom[None, :]).astype(jnp.bfloat16)
        grad_mixed = grad_mean[:, cluster]
        grad_rows, grad_qkv_weight, grad_out_weight, grad_gain = block_backward(grad_mixed, saved, qkv_weight, out_weight, norm_gain)
        grad_list.append(grad_rows[:, positions])
        qkv_total = qkv_total + grad_qkv_weight
        out_total = out_total + grad_out_weight
        gain_total = gain_total + grad_gain
    factor = float(WINDOWS * NPTS) ** (-0.5)
    return (jnp.stack(pooled_list), jnp.stack(grad_list), qkv_total * factor, out_total * factor, pool_total * factor, gain_total * factor)
```

```python
import functools

import jax
import jax.numpy as jnp
from jax import lax
from jax.experimental import pallas as pl
from jax.experimental.pallas import tpu as pltpu
from jax.sharding import PartitionSpec as P

HEADS = 4
HEAD_DIM = 16
CHANNELS = 64
NORM_EPS = 1e-05
CHUNK = 256

F32 = jnp.float32
BF16 = jnp.bfloat16
I32 = jnp.int32


def dot(a, b):
    return lax.dot_general(a, b, (((1,), (0,)), ((), ())), preferred_element_type=F32)


def dot_nt(a, b):
    return lax.dot_general(a, b, (((1,), (1,)), ((), ())), preferred_element_type=F32)


def dot_tn(a, b):
    return lax.dot_general(a, b, (((0,), (0,)), ((), ())), preferred_element_type=F32)


def turned(a):
    return a.astype(F32).T


def iota(shape, dim):
    return lax.broadcasted_iota(I32, shape, dim)


def onehot(mask):
    return jnp.where(mask, 1.0, 0.0).astype(BF16)


def on_rows(row, count):
    return onehot(iota((count, row.shape[1]), 0) == row)


def on_columns(column, count):
    return onehot(iota((column.shape[0], count), 1) == column)


def rank_in_group(groups, count):
    length = groups.shape[1]
    member = on_rows(groups, count)
    upto = onehot(iota((128, 128), 0) <= iota((128, 128), 1))
    seen = jnp.zeros((count, 1), F32)
    ranks = []
    for start in range(0, length, 128):
        block = member[:, start : start + 128]
        running = dot(block, upto) + seen
        seen = running[:, 127:128]
        ranks.append(jnp.sum(block.astype(F32) * running, axis=0, keepdims=True) - 1.0)
    return jnp.concatenate(ranks, axis=1).astype(I32)


def send_kernel(pos_ref, owner_ref, cell_ref, feats_ref, out_ref, z_slot_ref, o_slot_ref):
    length = pos_ref.shape[1]
    shards = out_ref.shape[0]
    per_peer = length // shards
    positions = pos_ref[...]
    owners = owner_ref[...]
    shift = length.bit_length() - 1
    target = lax.shift_right_logical(positions, shift)
    local = lax.bitwise_and(positions, length - 1)
    z_slot = target * per_peer + rank_in_group(target, shards)
    o_slot = owners * (2 * per_peer) + rank_in_group(owners, shards)
    z_slot_ref[...] = z_slot
    o_slot_ref[...] = o_slot
    row = iota((CHANNELS, length), 0)
    high = lax.shift_right_logical(local, 5).astype(F32)
    low = lax.bitwise_and(local, 31).astype(F32)
    place = jnp.where(row == 0, high, jnp.where(row == 1, low, 0.0)).astype(BF16)
    cell = (cell_ref[...] + 1).astype(F32)
    odd = lax.bitwise_and(o_slot, 1)
    cells = jnp.where(row - 2 == odd, cell, 0.0).astype(BF16)
    first = jnp.concatenate([feats_ref[...], place], axis=0)
    second = jnp.concatenate([jnp.zeros((CHANNELS, length), BF16), cells], axis=0)
    out = dot_nt(on_rows(z_slot, length), first)
    out = out + dot_nt(on_rows(lax.shift_right_logical(o_slot, 1), length), second)
    out_ref[...] = out.astype(BF16).reshape(out_ref.shape)


def arrived_columns(arrived):
    side = arrived[:, CHANNELS:].astype(F32)
    place = (side[:, 0:1] * 32.0 + side[:, 1:2]).astype(I32)
    return place, side[:, 2:3].astype(I32) - 1, side[:, 3:4].astype(I32) - 1


def gain_column(gain_ref):
    gain = gain_ref[...]
    eye = iota((CHANNELS, CHANNELS), 0) == iota((CHANNELS, CHANNELS), 1)
    return jnp.sum(jnp.where(eye, gain, 0.0), axis=1, keepdims=True)


def layer_norm(floats, gain):
    centred = floats - jnp.mean(floats, axis=0, keepdims=True)
    inverse_std = lax.rsqrt(jnp.mean(centred * centred, axis=0, keepdims=True) + NORM_EPS)
    normed = centred * inverse_std
    return normed, inverse_std, (gain * normed).astype(BF16)


def cluster_counts(first, second):
    return jnp.maximum(
        jnp.sum(first.astype(F32) + second.astype(F32), axis=0, keepdims=True), 1.0
    )


def head_lanes(shape, head):
    return lax.shift_right_logical(iota(shape, 1), 4) == head


def forward_kernel(
    arrived_ref,
    o_slot_ref,
    qkv_t_ref,
    out_w_ref,
    pool_t_ref,
    gain_ref,
    pool_grad_ref,
    out_ref,
    hilbert_ref,
    attended_ref,
    probs_ref,
    query_ref,
    key_ref,
    value_ref,
    rows_ref,
):
    shards = out_ref.shape[0]
    length = arrived_ref.shape[0]
    clusters = pool_grad_ref.shape[1]
    arrived = arrived_ref[...]
    place, first_cell, second_cell = arrived_columns(arrived)
    first = on_columns(first_cell, clusters)
    second = on_columns(second_cell, clusters)
    denom = cluster_counts(first, second)
    grad_mean = (dot(pool_t_ref[...], pool_grad_ref[...]) / denom).astype(BF16)
    blank = jnp.zeros_like(grad_mean)
    back = dot_nt(first, jnp.concatenate([grad_mean, blank], axis=0))
    back = back + dot_nt(second, jnp.concatenate([blank, grad_mean], axis=0))
    per_peer = length // shards
    out_ref[:, per_peer:, :] = back.astype(BF16).reshape(shards, per_peer, 2 * CHANNELS)
    turned_rows = turned(arrived)[:CHANNELS].astype(BF16)
    floats = dot(turned_rows, on_columns(place, length))
    hilbert_ref[...] = floats.astype(BF16)
    _, _, hidden = layer_norm(floats, gain_column(gain_ref))
    qkv = dot_tn(qkv_t_ref[...], hidden).astype(BF16)
    query_ref[...] = (turned(qkv[:CHANNELS]) * HEAD_DIM ** (-0.5)).astype(BF16)
    key_ref[...] = qkv[CHANNELS : 2 * CHANNELS]
    values = turned(qkv[2 * CHANNELS :])
    for head in range(HEADS):
        mask = head_lanes((length, CHANNELS), head)
        value_ref[head] = jnp.where(mask, values, 0.0).astype(BF16)

    def one_chunk(index, carry):
        rows = pl.ds(pl.multiple_of(index * CHUNK, CHUNK), CHUNK)
        queries = query_ref[rows, :].astype(F32)
        total = jnp.zeros((CHUNK, CHANNELS), F32)
        for head in range(HEADS):
            mask = head_lanes((CHUNK, CHANNELS), head)
            mine = jnp.where(mask, queries, 0.0).astype(BF16)
            weights = jnp.exp(dot(mine, key_ref[...]))
            share = 1.0 / jnp.sum(weights, axis=1, keepdims=True)
            probs = (weights * share).astype(BF16)
            probs_ref[head, rows, :] = probs
            total = total + dot(probs, value_ref[head])
        rows_ref[rows, :] = total
        return carry

    lax.fori_loop(0, length // CHUNK, one_chunk, 0)
    attended = rows_ref[...].T
    attended_ref[...] = attended
    mixed = (floats + dot(out_w_ref[...], attended.astype(BF16))).astype(BF16).astype(F32)
    o_slot = o_slot_ref[...]
    odd = lax.bitwise_and(o_slot, 1) == 1
    pair = jnp.concatenate([jnp.where(odd, 0.0, mixed), jnp.where(odd, mixed, 0.0)], axis=0)
    picked = dot_nt(on_rows(lax.shift_right_logical(o_slot, 1), length), pair.astype(BF16))
    out_ref[:, :per_peer, :] = picked.astype(BF16).reshape(shards, per_peer, 2 * CHANNELS)


def backward_kernel(
    returned_ref,
    arrived_ref,
    o_slot_ref,
    qkv_t_ref,
    out_w_ref,
    pool_t_ref,
    gain_ref,
    pool_grad_ref,
    hilbert_ref,
    attended_ref,
    probs_ref,
    out_ref,
    pooled_ref,
    key_rows_ref,
    upstream_ref,
    value_ref,
    query_ref,
    grad_out_ref,
    grad_query_ref,
    grad_key_ref,
    grad_value_ref,
):
    shards = out_ref.shape[0]
    length = arrived_ref.shape[0]
    clusters = pool_grad_ref.shape[1]
    per_peer = length // shards
    place, first_cell, second_cell = arrived_columns(arrived_ref[...])
    blank = jnp.zeros((CHANNELS, length), BF16)
    blank_clusters = jnp.zeros((CHANNELS, clusters), BF16)

    first = on_columns(first_cell, clusters)
    second = on_columns(second_cell, clusters)
    denom = cluster_counts(first, second)
    mixed_rows = turned(returned_ref[:, :per_peer, :].reshape(length, 2 * CHANNELS)).astype(BF16)
    sums = dot(mixed_rows[:CHANNELS], first) + dot(mixed_rows[CHANNELS:], second)
    pooled_mean = (sums / denom).astype(BF16)
    pooled_ref[...] = dot_tn(pool_t_ref[...], pooled_mean).astype(BF16)
    pool_grad = pool_grad_ref[...]
    pool_parts = [
        dot_nt(pooled_mean, jnp.concatenate([blank_clusters, pool_grad[start : start + CHANNELS]], axis=0))
        for start in (0, CHANNELS)
    ]

    gain = gain_column(gain_ref)
    normed, inverse_std, hidden = layer_norm(hilbert_ref[...].astype(F32), gain)
    qkv = dot_tn(qkv_t_ref[...], hidden).astype(BF16)
    query_ref[...] = qkv[:CHANNELS]
    key_rows = turned(qkv[CHANNELS : 2 * CHANNELS])
    for head in range(HEADS):
        mask = head_lanes((length, CHANNELS), head)
        key_rows_ref[head] = jnp.where(mask, key_rows, 0.0).astype(BF16)
    value_ref[:CHANNELS, :] = qkv[2 * CHANNELS :]
    value_ref[CHANNELS:, :] = jnp.ones((CHANNELS, length), BF16)

    o_slot = o_slot_ref[...]
    odd = lax.bitwise_and(o_slot, 1) == 1
    slots = turned(returned_ref[:, per_peer:, :].reshape(length, 2 * CHANNELS)).astype(BF16)
    both = dot(slots, on_rows(lax.shift_right_logical(o_slot, 1), length))
    grad_mixed = jnp.where(odd, both[CHANNELS:], both[:CHANNELS])
    grad_mixed_low = grad_mixed.astype(BF16)
    attended = attended_ref[...]
    attended_low = attended.astype(BF16)
    out_part = dot_nt(grad_mixed_low, jnp.concatenate([blank, attended_low], axis=0))
    grad_attended = dot_tn(out_w_ref[...], grad_mixed_low).astype(BF16)
    grad_out_ref[...] = grad_attended
    scaled = grad_attended.astype(F32) * HEAD_DIM ** (-0.5)
    delta = -jnp.sum((scaled * attended).reshape(HEADS, HEAD_DIM, length), axis=1)
    delta_high = delta.astype(BF16).astype(F32)
    rest = jnp.concatenate(
        [delta_high, delta - delta_high, jnp.zeros((CHANNELS - 2 * HEADS, length), F32)], axis=0
    )
    upstream_ref[...] = jnp.concatenate([scaled, rest], axis=0).T.astype(BF16)
    grad_key_ref[...] = jnp.zeros_like(grad_key_ref)
    grad_value_ref[...] = jnp.zeros_like(grad_value_ref)

    def one_chunk(index, carry):
        rows = pl.ds(pl.multiple_of(index * CHUNK, CHUNK), CHUNK)
        upstream = upstream_ref[rows, :].astype(F32)
        total = jnp.zeros((CHUNK, CHANNELS), F32)
        lane = iota((CHUNK, 2 * CHANNELS), 1)
        for head in range(HEADS):
            own = slice(head * HEAD_DIM, (head + 1) * HEAD_DIM)
            mask = (
                (lax.shift_right_logical(lane, 4) == head)
                | (lane == CHANNELS + head)
                | (lane == CHANNELS + HEADS + head)
            )
            mine = jnp.where(mask, upstream, 0.0).astype(BF16)
            probs = probs_ref[head, rows, :]
            grad_value_ref[own, :] += dot(grad_out_ref[own, rows], probs)
            change = dot(mine, value_ref[...])
            grad_scores = (probs.astype(F32) * change).astype(BF16)
            total = total + dot(grad_scores, key_rows_ref[head])
            grad_key_ref[own, :] += dot(query_ref[own, rows], grad_scores)
        grad_query_ref[rows, :] = total
        return carry

    lax.fori_loop(0, length // CHUNK, one_chunk, 0)
    grad_qkv = jnp.concatenate(
        [grad_query_ref[...].T, grad_key_ref[...], grad_value_ref[...]], axis=0
    ).astype(BF16)
    qkv_parts = [
        dot_nt(hidden, jnp.concatenate([blank, grad_qkv[start : start + CHANNELS]], axis=0))
        for start in (0, CHANNELS, 2 * CHANNELS)
    ]
    grad_hidden = dot(qkv_t_ref[...], grad_qkv)
    grad_gain = jnp.sum(grad_hidden * normed, axis=1, keepdims=True)
    grad_normed = grad_hidden * gain
    grad_norm_in = inverse_std * (
        grad_normed
        - jnp.mean(grad_normed, axis=0, keepdims=True)
        - normed * jnp.mean(grad_normed * normed, axis=0, keepdims=True)
    )
    grad_rows = (grad_mixed + grad_norm_in).astype(BF16)
    eye = iota((CHANNELS, 2 * CHANNELS), 0) + CHANNELS == iota((CHANNELS, 2 * CHANNELS), 1)
    gain_row = jnp.sum(jnp.where(eye, grad_gain, 0.0), axis=0, keepdims=True)
    back = dot_nt(on_columns(place, length), jnp.concatenate([grad_rows, blank], axis=0))
    parts = jnp.concatenate(qkv_parts + [out_part] + pool_parts, axis=0)
    high = parts.astype(BF16).astype(F32)
    gain_high = gain_row.astype(BF16).astype(F32)
    row = iota((8, 2 * CHANNELS), 0)
    gain_rows = jnp.where(row == 0, gain_high, jnp.where(row == 1, gain_row - gain_high, 0.0))
    count = parts.shape[0]
    used = 2 * count + 8
    side = jnp.concatenate(
        [high, parts - high, gain_rows, jnp.zeros((length - used, 2 * CHANNELS), F32)], axis=0
    )
    out_ref[...] = (back + side).astype(BF16).reshape(out_ref.shape)


def total_kernel(arrived_ref, out_ref):
    shards, per_peer, lanes = arrived_ref.shape
    total = jnp.sum(arrived_ref[...].astype(F32), axis=0)
    high = total.astype(BF16).astype(F32)
    low = pltpu.roll(total - high, CHANNELS, 1)
    chosen = jnp.where(iota((per_peer, lanes), 1) >= CHANNELS, high, low)
    out_ref[...] = jnp.broadcast_to(chosen[None], (shards, per_peer, lanes)).astype(BF16)


def feat_grad_kernel(arrived_ref, z_slot_ref, out_ref):
    length = arrived_ref.shape[0]
    rows = turned(arrived_ref[...])[:CHANNELS].astype(BF16)
    out_ref[...] = dot(rows, on_rows(z_slot_ref[...], length)).astype(BF16)


def finish_kernel(factor, own_ref, other_ref, qkv_ref, out_ref, pool_ref, gain_ref):
    both = own_ref[...].astype(F32) + other_ref[...].astype(F32)
    count = 6 * CHANNELS
    halves = both[:count] + both[count : 2 * count]
    halves = (halves[:, CHANNELS:] + halves[:, :CHANNELS]) * factor
    piece = [halves[k * CHANNELS : (k + 1) * CHANNELS] for k in range(6)]
    qkv_ref[...] = jnp.concatenate(piece[:3], axis=1)
    out_ref[...] = piece[3]
    pool_ref[...] = jnp.concatenate(piece[4:], axis=1)
    gain = both[2 * count : 2 * count + 1] + both[2 * count + 1 : 2 * count + 2]
    gain_ref[...] = (gain[:, CHANNELS:] + gain[:, :CHANNELS]) * factor


def shape(dims, dtype):
    return jax.ShapeDtypeStruct(dims, dtype)


def call(kernel, outs, scratch=(), flops=0):
    return pl.pallas_call(
        kernel,
        out_shape=outs,
        scratch_shapes=list(scratch),
        compiler_params=pltpu.CompilerParams(vmem_limit_bytes=48 * 1024 * 1024),
        cost_estimate=pl.CostEstimate(flops=flops, bytes_accessed=1 << 20, transcendentals=0),
    )


def exchange(blocks):
    return lax.all_to_all(blocks, "pts", split_axis=0, concat_axis=0, tiled=True)


def body(
    feats,
    hilbert_of_z,
    pool_owner,
    pool_slot,
    qkv_weight,
    out_weight,
    pool_weight,
    norm_gain,
    pooled_grad,
):
    length = feats.shape[2]
    shards = lax.axis_size("pts")
    per_peer = length // shards
    clusters = pooled_grad.shape[2]
    lanes = 2 * CHANNELS
    qkv_t = qkv_weight.T
    pool_t = pool_weight.T
    gain = norm_gain.reshape(1, CHANNELS)
    upstream_pool = pooled_grad[0]

    outgoing, z_slot, o_slot = call(
        send_kernel,
        (
            shape((shards, per_peer, lanes), BF16),
            shape((1, length), I32),
            shape((1, length), I32),
        ),
        flops=1 << 30,
    )(hilbert_of_z, pool_owner.reshape(1, length), pool_slot, feats[0])
    arrived = exchange(outgoing).reshape(length, lanes)

    both_ways, hilbert_rows, attended, probs = call(
        forward_kernel,
        (
            shape((shards, 2 * per_peer, lanes), BF16),
            shape((CHANNELS, length), BF16),
            shape((CHANNELS, length), F32),
            shape((HEADS, length, length), BF16),
        ),
        scratch=(
            pltpu.VMEM((length, CHANNELS), BF16),
            pltpu.VMEM((CHANNELS, length), BF16),
            pltpu.VMEM((HEADS, length, CHANNELS), BF16),
            pltpu.VMEM((length, CHANNELS), F32),
        ),
        flops=1 << 32,
    )(arrived, o_slot, qkv_t, out_weight, pool_t, gain, upstream_pool)
    returned = exchange(both_ways)

    last, pooled = call(
        backward_kernel,
        (shape((shards, per_peer, lanes), BF16), shape((2 * CHANNELS, clusters), BF16)),
        scratch=(
            pltpu.VMEM((HEADS, length, CHANNELS), BF16),
            pltpu.VMEM((length, lanes), BF16),
            pltpu.VMEM((lanes, length), BF16),
            pltpu.VMEM((CHANNELS, length), BF16),
            pltpu.VMEM((CHANNELS, length), BF16),
            pltpu.VMEM((length, CHANNELS), F32),
            pltpu.VMEM((CHANNELS, length), F32),
            pltpu.VMEM((CHANNELS, length), F32),
        ),
        flops=1 << 33,
    )(
        returned,
        arrived,
        o_slot,
        qkv_t,
        out_weight,
        pool_t,
        gain,
        upstream_pool,
        hilbert_rows,
        attended,
        probs,
    )
    final = exchange(last)

    chunk = call(total_kernel, shape((shards, per_peer, lanes), BF16))(final)
    gathered = exchange(chunk).reshape(length, lanes)
    feat_grad = call(feat_grad_kernel, shape((CHANNELS, length), BF16), flops=1 << 28)(
        final.reshape(length, lanes), z_slot
    )
    other = lax.ppermute(gathered, "rep", [(0, 1), (1, 0)])
    factor = float(lax.axis_size("rep") * shards * length) ** (-0.5)
    qkv_total, out_total, pool_total, gain_total = call(
        functools.partial(finish_kernel, factor),
        (
            shape((CHANNELS, 3 * CHANNELS), F32),
            shape((CHANNELS, CHANNELS), F32),
            shape((CHANNELS, lanes), F32),
            shape((1, CHANNELS), F32),
        ),
    )(gathered, other)
    return (
        pooled[None],
        feat_grad[None],
        qkv_total.T,
        out_total,
        pool_total.T,
        gain_total.reshape(CHANNELS),
    )


def solution(mesh):
    return jax.shard_map(
        body,
        mesh=mesh,
        in_specs=(
            P("rep", None, "pts"),
            P("rep", "pts"),
            P("rep", "pts", None),
            P("rep", "pts"),
            P(),
            P(),
            P(),
            P(),
            P("rep", None, "pts"),
        ),
        out_specs=(P("rep", None, "pts"), P("rep", None, "pts"), P(), P(), P(), P()),
        check_vma=False,
    )
```

```python
import functools

import jax
import jax.numpy as jnp
from jax import lax
from jax.experimental import pallas as pl
from jax.experimental.pallas import tpu as pltpu
from jax.sharding import PartitionSpec as P

HEADS = 4
HEAD_DIM = 16
CHANNELS = 64
NORM_EPS = 1e-05
CHUNK = 256
PLANE = 16

F32 = jnp.float32
BF16 = jnp.bfloat16
I32 = jnp.int32


def dot(a, b):
    return lax.dot_general(a, b, (((1,), (0,)), ((), ())), preferred_element_type=F32)


def dot_nt(a, b):
    return lax.dot_general(a, b, (((1,), (1,)), ((), ())), preferred_element_type=F32)


def dot_tn(a, b):
    return lax.dot_general(a, b, (((0,), (0,)), ((), ())), preferred_element_type=F32)


def turned(a):
    return a.astype(F32).T


def iota(shape, dim):
    return lax.broadcasted_iota(I32, shape, dim)


def onehot(mask):
    return jnp.where(mask, 1.0, 0.0).astype(BF16)


def on_rows(row, count):
    return onehot(iota((count, row.shape[1]), 0) == row)


def on_columns(column, count):
    return onehot(iota((column.shape[0], count), 1) == column)


def rank_in_group(groups, count):
    length = groups.shape[1]
    member = on_rows(groups, count)
    upto = onehot(iota((128, 128), 0) <= iota((128, 128), 1))
    seen = jnp.zeros((count, 1), F32)
    ranks = []
    for start in range(0, length, 128):
        block = member[:, start : start + 128]
        running = dot(block, upto) + seen
        seen = running[:, 127:128]
        ranks.append(jnp.sum(block.astype(F32) * running, axis=0, keepdims=True) - 1.0)
    return jnp.concatenate(ranks, axis=1).astype(I32)


def send_kernel(
    pos_hbm,
    owner_hbm,
    cell_hbm,
    feats_hbm,
    pool_grad_hbm,
    qkv_t_hbm,
    out_w_hbm,
    pool_t_hbm,
    gain_hbm,
    out_ref,
    z_slot_ref,
    o_slot_ref,
    pool_grad_ref,
    qkv_t_ref,
    out_w_ref,
    pool_t_ref,
    gain_ref,
    pos_ref,
    owner_ref,
    cell_ref,
    feats_ref,
    sems,
):
    loads = [
        pltpu.make_async_copy(source, target, sems.at[number])
        for number, (source, target) in enumerate(
            (
                (pos_hbm, pos_ref),
                (owner_hbm, owner_ref),
                (cell_hbm, cell_ref),
                (feats_hbm, feats_ref),
                (pool_grad_hbm, pool_grad_ref),
                (qkv_t_hbm, qkv_t_ref),
                (out_w_hbm, out_w_ref),
                (pool_t_hbm, pool_t_ref),
                (gain_hbm, gain_ref),
            )
        )
    ]
    for load in loads:
        load.start()
    for load in loads[:3]:
        load.wait()
    length = pos_ref.shape[1]
    shards = out_ref.shape[0]
    per_peer = length // shards
    positions = pos_ref[...]
    owners = owner_ref[...]
    shift = length.bit_length() - 1
    target = lax.shift_right_logical(positions, shift)
    local = lax.bitwise_and(positions, length - 1)
    z_slot = target * per_peer + rank_in_group(target, shards)
    o_slot = owners * (2 * per_peer) + rank_in_group(owners, shards)
    z_slot_ref[...] = z_slot
    o_slot_ref[...] = o_slot
    row = iota((CHANNELS, length), 0)
    high = lax.shift_right_logical(local, 5).astype(F32)
    low = lax.bitwise_and(local, 31).astype(F32)
    place = jnp.where(row == 0, high, jnp.where(row == 1, low, 0.0)).astype(BF16)
    cell = (cell_ref[...] + 1).astype(F32)
    odd = lax.bitwise_and(o_slot, 1)
    cells = jnp.where(row - 2 == odd, cell, 0.0).astype(BF16)
    loads[3].wait()
    first = jnp.concatenate([feats_ref[...], place], axis=0)
    second = jnp.concatenate([jnp.zeros((CHANNELS, length), BF16), cells], axis=0)
    out = dot_nt(on_rows(z_slot, length), first)
    out = out + dot_nt(on_rows(lax.shift_right_logical(o_slot, 1), length), second)
    out_ref[...] = out.astype(BF16).reshape(out_ref.shape)
    for load in loads[4:]:
        load.wait()


def arrived_columns(arrived):
    side = arrived[:, CHANNELS:].astype(F32)
    place = (side[:, 0:1] * 32.0 + side[:, 1:2]).astype(I32)
    return place, side[:, 2:3].astype(I32) - 1, side[:, 3:4].astype(I32) - 1


def gain_column(gain_ref):
    gain = gain_ref[...]
    eye = iota((CHANNELS, CHANNELS), 0) == iota((CHANNELS, CHANNELS), 1)
    return jnp.sum(jnp.where(eye, gain, 0.0), axis=1, keepdims=True)


def layer_norm(floats, gain):
    centred = floats - jnp.mean(floats, axis=0, keepdims=True)
    inverse_std = lax.rsqrt(jnp.mean(centred * centred, axis=0, keepdims=True) + NORM_EPS)
    normed = centred * inverse_std
    return normed, inverse_std, (gain * normed).astype(BF16)


def cluster_counts(first, second):
    return jnp.maximum(
        jnp.sum(first.astype(F32) + second.astype(F32), axis=0, keepdims=True), 1.0
    )


def head_lanes(shape, head):
    return lax.shift_right_logical(iota(shape, 1), 4) == head


def forward_kernel(
    arrived_ref,
    o_slot_ref,
    qkv_t_ref,
    out_w_ref,
    pool_t_ref,
    gain_ref,
    pool_grad_ref,
    out_ref,
    hilbert_ref,
    attended_ref,
    probs_ref,
    query_ref,
    key_ref,
    value_ref,
    rows_ref,
):
    shards = out_ref.shape[0]
    length = arrived_ref.shape[0]
    clusters = pool_grad_ref.shape[1]
    arrived = arrived_ref[...]
    place, first_cell, second_cell = arrived_columns(arrived)
    first = on_columns(first_cell, clusters)
    second = on_columns(second_cell, clusters)
    denom = cluster_counts(first, second)
    grad_mean = (dot(pool_t_ref[...], pool_grad_ref[...]) / denom).astype(BF16)
    blank = jnp.zeros_like(grad_mean)
    back = dot_nt(first, jnp.concatenate([grad_mean, blank], axis=0))
    back = back + dot_nt(second, jnp.concatenate([blank, grad_mean], axis=0))
    per_peer = length // shards
    out_ref[:, per_peer:, :] = back.astype(BF16).reshape(shards, per_peer, 2 * CHANNELS)
    turned_rows = turned(arrived)[:CHANNELS].astype(BF16)
    floats = dot(turned_rows, on_columns(place, length))
    hilbert_ref[...] = floats.astype(BF16)
    _, _, hidden = layer_norm(floats, gain_column(gain_ref))
    qkv = dot_tn(qkv_t_ref[...], hidden).astype(BF16)
    query_ref[...] = (turned(qkv[:CHANNELS]) * HEAD_DIM ** (-0.5)).astype(BF16)
    key_ref[...] = qkv[CHANNELS : 2 * CHANNELS]
    values = turned(qkv[2 * CHANNELS :])
    for head in range(HEADS):
        mask = head_lanes((length, CHANNELS), head)
        value_ref[head] = jnp.where(mask, values, 0.0).astype(BF16)

    def one_chunk(index, carry):
        rows = pl.ds(pl.multiple_of(index * CHUNK, CHUNK), CHUNK)
        queries = query_ref[rows, :].astype(F32)
        total = jnp.zeros((CHUNK, CHANNELS), F32)
        for head in range(HEADS):
            mask = head_lanes((CHUNK, CHANNELS), head)
            mine = jnp.where(mask, queries, 0.0).astype(BF16)
            weights = jnp.exp(dot(mine, key_ref[...]))
            share = 1.0 / jnp.sum(weights, axis=1, keepdims=True)
            probs = (weights * share).astype(BF16)
            probs_ref[head, rows, :] = probs
            total = total + dot(probs, value_ref[head])
        rows_ref[rows, :] = total
        return carry

    lax.fori_loop(0, length // CHUNK, one_chunk, 0)
    attended = rows_ref[...].T
    attended_ref[...] = attended
    mixed = (floats + dot(out_w_ref[...], attended.astype(BF16))).astype(BF16).astype(F32)
    o_slot = o_slot_ref[...]
    odd = lax.bitwise_and(o_slot, 1) == 1
    pair = jnp.concatenate([jnp.where(odd, 0.0, mixed), jnp.where(odd, mixed, 0.0)], axis=0)
    picked = dot_nt(on_rows(lax.shift_right_logical(o_slot, 1), length), pair.astype(BF16))
    out_ref[:, :per_peer, :] = picked.astype(BF16).reshape(shards, per_peer, 2 * CHANNELS)


def backward_kernel(
    returned_ref,
    arrived_ref,
    o_slot_ref,
    qkv_t_ref,
    out_w_ref,
    pool_t_ref,
    gain_ref,
    pool_grad_ref,
    hilbert_ref,
    attended_ref,
    probs_ref,
    out_ref,
    pooled_ref,
    key_rows_ref,
    upstream_ref,
    value_ref,
    query_ref,
    grad_out_ref,
    grad_query_ref,
    grad_key_ref,
    grad_value_ref,
):
    shards = out_ref.shape[0]
    length = arrived_ref.shape[0]
    clusters = pool_grad_ref.shape[1]
    per_peer = length // shards
    place, first_cell, second_cell = arrived_columns(arrived_ref[...])
    blank = jnp.zeros((CHANNELS, length), BF16)

    first = on_columns(first_cell, clusters)
    second = on_columns(second_cell, clusters)
    denom = cluster_counts(first, second)
    mixed_rows = turned(returned_ref[:, :per_peer, :].reshape(length, 2 * CHANNELS)).astype(BF16)
    sums = dot(mixed_rows[:CHANNELS], first) + dot(mixed_rows[CHANNELS:], second)
    pooled_mean = (sums / denom).astype(BF16)
    pooled_ref[...] = dot_tn(pool_t_ref[...], pooled_mean).astype(BF16)
    pool_part = dot_nt(pooled_mean, pool_grad_ref[...])

    gain = gain_column(gain_ref)
    normed, inverse_std, hidden = layer_norm(hilbert_ref[...].astype(F32), gain)
    qkv = dot_tn(qkv_t_ref[...], hidden).astype(BF16)
    query_ref[...] = qkv[:CHANNELS]
    key_rows = turned(qkv[CHANNELS : 2 * CHANNELS])
    for head in range(HEADS):
        mask = head_lanes((length, CHANNELS), head)
        key_rows_ref[head] = jnp.where(mask, key_rows, 0.0).astype(BF16)
    value_ref[:CHANNELS, :] = qkv[2 * CHANNELS :]
    value_ref[CHANNELS:, :] = jnp.ones((CHANNELS, length), BF16)

    o_slot = o_slot_ref[...]
    odd = lax.bitwise_and(o_slot, 1) == 1
    slots = turned(returned_ref[:, per_peer:, :].reshape(length, 2 * CHANNELS)).astype(BF16)
    both = dot(slots, on_rows(lax.shift_right_logical(o_slot, 1), length))
    grad_mixed = jnp.where(odd, both[CHANNELS:], both[:CHANNELS])
    grad_mixed_low = grad_mixed.astype(BF16)
    attended = attended_ref[...]
    attended_low = attended.astype(BF16)
    out_part = dot_nt(grad_mixed_low, jnp.concatenate([blank, attended_low], axis=0))
    grad_attended = dot_tn(out_w_ref[...], grad_mixed_low).astype(BF16)
    grad_out_ref[...] = grad_attended
    scaled = grad_attended.astype(F32) * HEAD_DIM ** (-0.5)
    delta = -jnp.sum((scaled * attended).reshape(HEADS, HEAD_DIM, length), axis=1)
    delta_high = delta.astype(BF16).astype(F32)
    rest = jnp.concatenate(
        [delta_high, delta - delta_high, jnp.zeros((CHANNELS - 2 * HEADS, length), F32)], axis=0
    )
    upstream_ref[...] = jnp.concatenate([scaled, rest], axis=0).T.astype(BF16)
    grad_key_ref[...] = jnp.zeros_like(grad_key_ref)
    grad_value_ref[...] = jnp.zeros_like(grad_value_ref)

    def one_chunk(index, carry):
        rows = pl.ds(pl.multiple_of(index * CHUNK, CHUNK), CHUNK)
        upstream = upstream_ref[rows, :].astype(F32)
        total = jnp.zeros((CHUNK, CHANNELS), F32)
        lane = iota((CHUNK, 2 * CHANNELS), 1)
        for head in range(HEADS):
            own = slice(head * HEAD_DIM, (head + 1) * HEAD_DIM)
            mask = (
                (lax.shift_right_logical(lane, 4) == head)
                | (lane == CHANNELS + head)
                | (lane == CHANNELS + HEADS + head)
            )
            mine = jnp.where(mask, upstream, 0.0).astype(BF16)
            probs = probs_ref[head, rows, :]
            grad_value_ref[own, :] += dot(grad_out_ref[own, rows], probs)
            change = dot(mine, value_ref[...])
            grad_scores = (probs.astype(F32) * change).astype(BF16)
            total = total + dot(grad_scores, key_rows_ref[head])
            grad_key_ref[own, :] += dot(query_ref[own, rows], grad_scores)
        grad_query_ref[rows, :] = total
        return carry

    lax.fori_loop(0, length // CHUNK, one_chunk, 0)
    grad_qkv = jnp.concatenate(
        [grad_query_ref[...].T, grad_key_ref[...], grad_value_ref[...]], axis=0
    ).astype(BF16)
    query_key_part = dot_nt(hidden, grad_qkv[: 2 * CHANNELS])
    value_part = dot_nt(hidden, jnp.concatenate([blank, grad_qkv[2 * CHANNELS :]], axis=0))
    grad_hidden = dot(qkv_t_ref[...], grad_qkv)
    grad_normed = grad_hidden * gain
    grad_norm_in = inverse_std * (
        grad_normed
        - jnp.mean(grad_normed, axis=0, keepdims=True)
        - normed * jnp.mean(grad_normed * normed, axis=0, keepdims=True)
    )
    grad_rows = (grad_mixed + grad_norm_in).astype(BF16)
    back = dot_nt(on_columns(place, length), jnp.concatenate([grad_rows, blank], axis=0))
    beside = jnp.concatenate([value_part, out_part], axis=0)
    below = jnp.concatenate([query_key_part, pool_part], axis=0).astype(BF16)
    below = below.reshape(PLANE, per_peer, 2 * CHANNELS)
    span = PLANE * per_peer
    for start in range(0, shards, PLANE):
        rows = back[start * per_peer : start * per_peer + span] + beside
        out_ref[start : start + PLANE, :per_peer, :] = rows.astype(BF16).reshape(below.shape)
        out_ref[start : start + PLANE, per_peer:, :] = below


def total_kernel(arrived_ref, out_ref):
    out_ref[...] = jnp.sum(arrived_ref[...].astype(F32), axis=0)


def feat_grad_kernel(arrived_ref, z_slot_ref, out_ref):
    shards, rows_per_peer, lanes = arrived_ref.shape
    length = shards * rows_per_peer // 2
    arrived = arrived_ref[:, : rows_per_peer // 2, :].reshape(length, lanes)
    rows = turned(arrived)[:CHANNELS].astype(BF16)
    out_ref[...] = dot(rows, on_rows(z_slot_ref[...], length)).astype(BF16)


def finish_kernel(factor, total_ref, qkv_t_ref, gain_in_ref, qkv_ref, out_ref, pool_ref, gain_ref):
    chunks, rows, lanes = total_ref.shape
    half = rows // 2
    beside = total_ref[:, :half, :].reshape(chunks * half, lanes)[:, CHANNELS:] * factor
    below = total_ref[:, half:, :].reshape(chunks * half, lanes) * factor
    qkv = jnp.concatenate([below[:CHANNELS], beside[:CHANNELS]], axis=1)
    qkv_ref[...] = qkv
    out_ref[...] = beside[CHANNELS:]
    pool_ref[...] = below[CHANNELS:]
    column = jnp.sum(qkv * qkv_t_ref[...].astype(F32), axis=1, keepdims=True)
    eye = iota((CHANNELS, CHANNELS), 0) == iota((CHANNELS, CHANNELS), 1)
    gain_ref[...] = jnp.sum(jnp.where(eye, column, 0.0), axis=0, keepdims=True) / gain_in_ref[...]


def shape(dims, dtype):
    return jax.ShapeDtypeStruct(dims, dtype)


def call(kernel, outs, scratch=(), flops=0, **more):
    return pl.pallas_call(
        kernel,
        out_shape=outs,
        **more,
        scratch_shapes=list(scratch),
        compiler_params=pltpu.CompilerParams(vmem_limit_bytes=48 * 1024 * 1024),
        cost_estimate=pl.CostEstimate(flops=flops, bytes_accessed=1 << 20, transcendentals=0),
    )


def exchange(blocks):
    return lax.all_to_all(blocks, "pts", split_axis=0, concat_axis=0, tiled=True)


def body(
    feats,
    hilbert_of_z,
    pool_owner,
    pool_slot,
    qkv_weight,
    out_weight,
    pool_weight,
    norm_gain,
    pooled_grad,
):
    length = feats.shape[2]
    shards = lax.axis_size("pts")
    per_peer = length // shards
    clusters = pooled_grad.shape[2]
    lanes = 2 * CHANNELS
    qkv_t = qkv_weight.T
    pool_t = pool_weight.T
    gain = norm_gain.reshape(1, CHANNELS)
    upstream_pool = pooled_grad[0]

    arguments = (
        hilbert_of_z,
        pool_owner.reshape(1, length),
        pool_slot,
        feats[0],
        upstream_pool,
        qkv_t,
        out_weight,
        pool_t,
        gain,
    )
    outgoing, z_slot, o_slot, upstream_pool, qkv_t, out_weight, pool_t, gain = call(
        send_kernel,
        (
            shape((shards, per_peer, lanes), BF16),
            shape((1, length), I32),
            shape((1, length), I32),
        )
        + tuple(shape(one.shape, one.dtype) for one in arguments[4:]),
        scratch=tuple(pltpu.VMEM(one.shape, one.dtype) for one in arguments[:4])
        + (pltpu.SemaphoreType.DMA((len(arguments),)),),
        flops=1 << 30,
        in_specs=[pl.BlockSpec(memory_space=pltpu.HBM)] * len(arguments),
    )(*arguments)
    arrived = exchange(outgoing).reshape(length, lanes)

    both_ways, hilbert_rows, attended, probs = call(
        forward_kernel,
        (
            shape((shards, 2 * per_peer, lanes), BF16),
            shape((CHANNELS, length), BF16),
            shape((CHANNELS, length), F32),
            shape((HEADS, length, length), BF16),
        ),
        scratch=(
            pltpu.VMEM((length, CHANNELS), BF16),
            pltpu.VMEM((CHANNELS, length), BF16),
            pltpu.VMEM((HEADS, length, CHANNELS), BF16),
            pltpu.VMEM((length, CHANNELS), F32),
        ),
        flops=1 << 32,
    )(arrived, o_slot, qkv_t, out_weight, pool_t, gain, upstream_pool)
    returned = exchange(both_ways)

    last, pooled = call(
        backward_kernel,
        (shape((shards, 2 * per_peer, lanes), BF16), shape((2 * CHANNELS, clusters), BF16)),
        scratch=(
            pltpu.VMEM((HEADS, length, CHANNELS), BF16),
            pltpu.VMEM((length, lanes), BF16),
            pltpu.VMEM((lanes, length), BF16),
            pltpu.VMEM((CHANNELS, length), BF16),
            pltpu.VMEM((CHANNELS, length), BF16),
            pltpu.VMEM((length, CHANNELS), F32),
            pltpu.VMEM((CHANNELS, length), F32),
            pltpu.VMEM((CHANNELS, length), F32),
        ),
        flops=1 << 33,
    )(
        returned,
        arrived,
        o_slot,
        qkv_t,
        out_weight,
        pool_t,
        gain,
        upstream_pool,
        hilbert_rows,
        attended,
        probs,
    )
    final = exchange(last)

    own = call(total_kernel, shape((2 * per_peer, lanes), F32))(final)
    other = lax.ppermute(own, "rep", [(0, 1), (1, 0)])
    feat_grad = call(feat_grad_kernel, shape((CHANNELS, length), BF16), flops=1 << 28)(
        final, z_slot
    )
    total = jnp.broadcast_to((own + other)[None], (PLANE, 2 * per_peer, lanes))
    gathered = lax.all_to_all(
        total,
        "pts",
        split_axis=0,
        concat_axis=0,
        tiled=True,
        axis_index_groups=[
            list(range(start, start + PLANE)) for start in range(0, shards, PLANE)
        ],
    )
    factor = float(lax.axis_size("rep") * shards * length) ** (-0.5)
    qkv_total, out_total, pool_total, gain_total = call(
        functools.partial(finish_kernel, factor),
        (
            shape((CHANNELS, 3 * CHANNELS), F32),
            shape((CHANNELS, CHANNELS), F32),
            shape((CHANNELS, lanes), F32),
            shape((1, CHANNELS), F32),
        ),
    )(gathered, qkv_t, gain)
    return (
        pooled[None],
        feat_grad[None],
        qkv_total.T,
        out_total,
        pool_total.T,
        gain_total.reshape(CHANNELS),
    )


def solution(mesh):
    return jax.shard_map(
        body,
        mesh=mesh,
        in_specs=(
            P("rep", None, "pts"),
            P("rep", "pts"),
            P("rep", "pts", None),
            P("rep", "pts"),
            P(),
            P(),
            P(),
            P(),
            P("rep", None, "pts"),
        ),
        out_specs=(P("rep", None, "pts"), P("rep", None, "pts"), P(), P(), P(), P()),
        check_vma=False,
    )
```

```python
import functools

import jax
import jax.numpy as jnp
from jax import lax
from jax.experimental import pallas as pl
from jax.experimental.pallas import tpu as pltpu
from jax.sharding import PartitionSpec as P

HEADS = 4
HEAD_DIM = 16
CHANNELS = 64
NORM_EPS = 1e-05
CHUNK = 256
GROUP = 64

F32 = jnp.float32
BF16 = jnp.bfloat16
I32 = jnp.int32


def dot(a, b):
    return lax.dot_general(a, b, (((1,), (0,)), ((), ())), preferred_element_type=F32)


def dot_nt(a, b):
    return lax.dot_general(a, b, (((1,), (1,)), ((), ())), preferred_element_type=F32)


def dot_tn(a, b):
    return lax.dot_general(a, b, (((0,), (0,)), ((), ())), preferred_element_type=F32)


def turned(a):
    return a.astype(F32).T


def iota(shape, dim):
    return lax.broadcasted_iota(I32, shape, dim)


def onehot(mask):
    return jnp.where(mask, 1.0, 0.0).astype(BF16)


def on_rows(row, count):
    return onehot(iota((count, row.shape[1]), 0) == row)


def on_columns(column, count):
    return onehot(iota((column.shape[0], count), 1) == column)


def rank_in_group(groups, count):
    length = groups.shape[1]
    member = on_rows(groups, count)
    upto = onehot(iota((128, 128), 0) <= iota((128, 128), 1))
    seen = jnp.zeros((count, 1), F32)
    ranks = []
    for start in range(0, length, 128):
        block = member[:, start : start + 128]
        running = dot(block, upto) + seen
        seen = running[:, 127:128]
        ranks.append(jnp.sum(block.astype(F32) * running, axis=0, keepdims=True) - 1.0)
    return jnp.concatenate(ranks, axis=1).astype(I32)


def send_kernel(
    pos_hbm,
    owner_hbm,
    cell_hbm,
    feats_hbm,
    pool_grad_hbm,
    qkv_t_hbm,
    out_w_hbm,
    pool_t_hbm,
    gain_hbm,
    out_ref,
    z_slot_ref,
    o_slot_ref,
    pool_grad_ref,
    qkv_t_ref,
    out_w_ref,
    pool_t_ref,
    gain_ref,
    pos_ref,
    owner_ref,
    cell_ref,
    feats_ref,
    sems,
):
    loads = [
        pltpu.make_async_copy(source, target, sems.at[number])
        for number, (source, target) in enumerate(
            (
                (pos_hbm, pos_ref),
                (owner_hbm, owner_ref),
                (cell_hbm, cell_ref),
                (feats_hbm, feats_ref),
                (pool_grad_hbm, pool_grad_ref),
                (qkv_t_hbm, qkv_t_ref),
                (out_w_hbm, out_w_ref),
                (pool_t_hbm, pool_t_ref),
                (gain_hbm, gain_ref),
            )
        )
    ]
    for load in loads:
        load.start()
    for load in loads[:3]:
        load.wait()
    length = pos_ref.shape[1]
    shards = out_ref.shape[0]
    per_peer = length // shards
    positions = pos_ref[...]
    owners = owner_ref[...]
    shift = length.bit_length() - 1
    target = lax.shift_right_logical(positions, shift)
    local = lax.bitwise_and(positions, length - 1)
    z_slot = target * per_peer + rank_in_group(target, shards)
    o_slot = owners * (2 * per_peer) + rank_in_group(owners, shards)
    z_slot_ref[...] = z_slot
    o_slot_ref[...] = o_slot
    row = iota((CHANNELS, length), 0)
    high = lax.shift_right_logical(local, 5).astype(F32)
    low = lax.bitwise_and(local, 31).astype(F32)
    place = jnp.where(row == 0, high, jnp.where(row == 1, low, 0.0)).astype(BF16)
    cell = (cell_ref[...] + 1).astype(F32)
    odd = lax.bitwise_and(o_slot, 1)
    cells = jnp.where(row - 2 == odd, cell, 0.0).astype(BF16)
    loads[3].wait()
    first = jnp.concatenate([feats_ref[...], place], axis=0)
    second = jnp.concatenate([jnp.zeros((CHANNELS, length), BF16), cells], axis=0)
    out = dot_nt(on_rows(z_slot, length), first)
    out = out + dot_nt(on_rows(lax.shift_right_logical(o_slot, 1), length), second)
    out_ref[...] = out.astype(BF16).reshape(out_ref.shape)
    for load in loads[4:]:
        load.wait()


def arrived_columns(arrived):
    side = arrived[:, CHANNELS:].astype(F32)
    place = (side[:, 0:1] * 32.0 + side[:, 1:2]).astype(I32)
    return place, side[:, 2:3].astype(I32) - 1, side[:, 3:4].astype(I32) - 1


def gain_column(gain_ref):
    gain = gain_ref[...]
    eye = iota((CHANNELS, CHANNELS), 0) == iota((CHANNELS, CHANNELS), 1)
    return jnp.sum(jnp.where(eye, gain, 0.0), axis=1, keepdims=True)


def layer_norm(floats, gain):
    centred = floats - jnp.mean(floats, axis=0, keepdims=True)
    inverse_std = lax.rsqrt(jnp.mean(centred * centred, axis=0, keepdims=True) + NORM_EPS)
    normed = centred * inverse_std
    return normed, inverse_std, (gain * normed).astype(BF16)


def cluster_counts(first, second):
    return jnp.maximum(
        jnp.sum(first.astype(F32) + second.astype(F32), axis=0, keepdims=True), 1.0
    )


def head_lanes(shape, head):
    return lax.shift_right_logical(iota(shape, 1), 4) == head


def forward_kernel(
    arrived_ref,
    o_slot_ref,
    qkv_t_ref,
    out_w_ref,
    pool_t_ref,
    gain_ref,
    pool_grad_ref,
    out_ref,
    hilbert_ref,
    attended_ref,
    probs_ref,
    query_ref,
    key_ref,
    value_ref,
    rows_ref,
):
    shards = out_ref.shape[0]
    length = arrived_ref.shape[0]
    clusters = pool_grad_ref.shape[1]
    arrived = arrived_ref[...]
    place, first_cell, second_cell = arrived_columns(arrived)
    first = on_columns(first_cell, clusters)
    second = on_columns(second_cell, clusters)
    denom = cluster_counts(first, second)
    grad_mean = (dot(pool_t_ref[...], pool_grad_ref[...]) / denom).astype(BF16)
    blank = jnp.zeros_like(grad_mean)
    back = dot_nt(first, jnp.concatenate([grad_mean, blank], axis=0))
    back = back + dot_nt(second, jnp.concatenate([blank, grad_mean], axis=0))
    per_peer = length // shards
    out_ref[:, per_peer:, :] = back.astype(BF16).reshape(shards, per_peer, 2 * CHANNELS)
    turned_rows = turned(arrived)[:CHANNELS].astype(BF16)
    floats = dot(turned_rows, on_columns(place, length))
    hilbert_ref[...] = floats.astype(BF16)
    _, _, hidden = layer_norm(floats, gain_column(gain_ref))
    qkv = dot_tn(qkv_t_ref[...], hidden).astype(BF16)
    query_ref[...] = (turned(qkv[:CHANNELS]) * HEAD_DIM ** (-0.5)).astype(BF16)
    key_ref[...] = qkv[CHANNELS : 2 * CHANNELS]
    values = turned(qkv[2 * CHANNELS :])
    for head in range(HEADS):
        mask = head_lanes((length, CHANNELS), head)
        value_ref[head] = jnp.where(mask, values, 0.0).astype(BF16)

    def one_chunk(index, carry):
        rows = pl.ds(pl.multiple_of(index * CHUNK, CHUNK), CHUNK)
        queries = query_ref[rows, :].astype(F32)
        total = jnp.zeros((CHUNK, CHANNELS), F32)
        for head in range(HEADS):
            mask = head_lanes((CHUNK, CHANNELS), head)
            mine = jnp.where(mask, queries, 0.0).astype(BF16)
            weights = jnp.exp(dot(mine, key_ref[...]))
            share = 1.0 / jnp.sum(weights, axis=1, keepdims=True)
            probs = (weights * share).astype(BF16)
            probs_ref[head, rows, :] = probs
            total = total + dot(probs, value_ref[head])
        rows_ref[rows, :] = total
        return carry

    lax.fori_loop(0, length // CHUNK, one_chunk, 0)
    attended = rows_ref[...].T
    attended_ref[...] = attended
    mixed = (floats + dot(out_w_ref[...], attended.astype(BF16))).astype(BF16).astype(F32)
    o_slot = o_slot_ref[...]
    odd = lax.bitwise_and(o_slot, 1) == 1
    pair = jnp.concatenate([jnp.where(odd, 0.0, mixed), jnp.where(odd, mixed, 0.0)], axis=0)
    picked = dot_nt(on_rows(lax.shift_right_logical(o_slot, 1), length), pair.astype(BF16))
    out_ref[:, :per_peer, :] = picked.astype(BF16).reshape(shards, per_peer, 2 * CHANNELS)


def backward_kernel(
    returned_ref,
    arrived_ref,
    o_slot_ref,
    qkv_t_ref,
    out_w_ref,
    pool_t_ref,
    gain_ref,
    pool_grad_ref,
    hilbert_ref,
    attended_ref,
    probs_ref,
    out_ref,
    pooled_ref,
    key_rows_ref,
    upstream_ref,
    value_ref,
    query_ref,
    grad_out_ref,
    grad_query_ref,
    grad_key_ref,
    grad_value_ref,
):
    shards = out_ref.shape[0]
    length = arrived_ref.shape[0]
    clusters = pool_grad_ref.shape[1]
    per_peer = length // shards
    place, first_cell, second_cell = arrived_columns(arrived_ref[...])
    blank = jnp.zeros((CHANNELS, length), BF16)
    blank_clusters = jnp.zeros((CHANNELS, clusters), BF16)

    first = on_columns(first_cell, clusters)
    second = on_columns(second_cell, clusters)
    denom = cluster_counts(first, second)
    mixed_rows = turned(returned_ref[:, :per_peer, :].reshape(length, 2 * CHANNELS)).astype(BF16)
    sums = dot(mixed_rows[:CHANNELS], first) + dot(mixed_rows[CHANNELS:], second)
    pooled_mean = (sums / denom).astype(BF16)
    pooled_ref[...] = dot_tn(pool_t_ref[...], pooled_mean).astype(BF16)
    pool_parts = [
        dot_nt(pooled_mean, jnp.concatenate([blank_clusters, half], axis=0))
        for half in (pool_grad_ref[:CHANNELS, :], pool_grad_ref[CHANNELS:, :])
    ]

    gain = gain_column(gain_ref)
    normed, inverse_std, hidden = layer_norm(hilbert_ref[...].astype(F32), gain)
    qkv = dot_tn(qkv_t_ref[...], hidden).astype(BF16)
    query_ref[...] = qkv[:CHANNELS]
    key_rows = turned(qkv[CHANNELS : 2 * CHANNELS])
    for head in range(HEADS):
        mask = head_lanes((length, CHANNELS), head)
        key_rows_ref[head] = jnp.where(mask, key_rows, 0.0).astype(BF16)
    value_ref[:CHANNELS, :] = qkv[2 * CHANNELS :]
    value_ref[CHANNELS:, :] = jnp.ones((CHANNELS, length), BF16)

    o_slot = o_slot_ref[...]
    odd = lax.bitwise_and(o_slot, 1) == 1
    slots = turned(returned_ref[:, per_peer:, :].reshape(length, 2 * CHANNELS)).astype(BF16)
    both = dot(slots, on_rows(lax.shift_right_logical(o_slot, 1), length))
    grad_mixed = jnp.where(odd, both[CHANNELS:], both[:CHANNELS])
    grad_mixed_low = grad_mixed.astype(BF16)
    attended = attended_ref[...]
    attended_low = attended.astype(BF16)
    out_part = dot_nt(grad_mixed_low, jnp.concatenate([blank, attended_low], axis=0))
    grad_attended = dot_tn(out_w_ref[...], grad_mixed_low).astype(BF16)
    grad_out_ref[...] = grad_attended
    scaled = grad_attended.astype(F32) * HEAD_DIM ** (-0.5)
    delta = -jnp.sum((scaled * attended).reshape(HEADS, HEAD_DIM, length), axis=1)
    delta_high = delta.astype(BF16).astype(F32)
    rest = jnp.concatenate(
        [delta_high, delta - delta_high, jnp.zeros((CHANNELS - 2 * HEADS, length), F32)], axis=0
    )
    upstream_ref[...] = jnp.concatenate([scaled, rest], axis=0).T.astype(BF16)
    grad_key_ref[...] = jnp.zeros_like(grad_key_ref)
    grad_value_ref[...] = jnp.zeros_like(grad_value_ref)

    def one_chunk(index, carry):
        rows = pl.ds(pl.multiple_of(index * CHUNK, CHUNK), CHUNK)
        upstream = upstream_ref[rows, :].astype(F32)
        total = jnp.zeros((CHUNK, CHANNELS), F32)
        lane = iota((CHUNK, 2 * CHANNELS), 1)
        for head in range(HEADS):
            own = slice(head * HEAD_DIM, (head + 1) * HEAD_DIM)
            mask = (
                (lax.shift_right_logical(lane, 4) == head)
                | (lane == CHANNELS + head)
                | (lane == CHANNELS + HEADS + head)
            )
            mine = jnp.where(mask, upstream, 0.0).astype(BF16)
            probs = probs_ref[head, rows, :]
            grad_value_ref[own, :] += dot(grad_out_ref[own, rows], probs)
            change = dot(mine, value_ref[...])
            grad_scores = (probs.astype(F32) * change).astype(BF16)
            total = total + dot(grad_scores, key_rows_ref[head])
            grad_key_ref[own, :] += dot(query_ref[own, rows], grad_scores)
        grad_query_ref[rows, :] = total
        return carry

    lax.fori_loop(0, length // CHUNK, one_chunk, 0)
    grad_qkv = jnp.concatenate(
        [grad_query_ref[...].T, grad_key_ref[...], grad_value_ref[...]], axis=0
    ).astype(BF16)
    qkv_parts = [
        dot_nt(hidden, jnp.concatenate([blank, grad_qkv[start : start + CHANNELS]], axis=0))
        for start in (0, CHANNELS, 2 * CHANNELS)
    ]
    grad_hidden = dot(qkv_t_ref[...], grad_qkv)
    grad_normed = grad_hidden * gain
    grad_norm_in = inverse_std * (
        grad_normed
        - jnp.mean(grad_normed, axis=0, keepdims=True)
        - normed * jnp.mean(grad_normed * normed, axis=0, keepdims=True)
    )
    grad_rows = (grad_mixed + grad_norm_in).astype(BF16)
    back = dot_nt(on_columns(place, length), jnp.concatenate([grad_rows, blank], axis=0))
    parts = qkv_parts + [out_part] + pool_parts
    unused = jnp.zeros((GROUP * per_peer - len(parts) * CHANNELS, 2 * CHANNELS), F32)
    side = jnp.concatenate(parts + [unused], axis=0)
    span = GROUP * per_peer
    for start in range(0, shards, GROUP):
        rows = back[start * per_peer : start * per_peer + span] + side
        out_ref[start : start + GROUP] = rows.astype(BF16).reshape(GROUP, per_peer, 2 * CHANNELS)


def total_kernel(arrived_ref, out_ref):
    out_ref[...] = jnp.sum(arrived_ref[...].astype(F32), axis=0)


def spread_kernel(own_ref, other_ref, out_ref):
    total = own_ref[...] + other_ref[...]
    high = total.astype(BF16).astype(F32)
    low = pltpu.roll(total - high, CHANNELS, 1)
    chosen = jnp.where(iota(total.shape, 1) >= CHANNELS, high, low)
    out_ref[...] = jnp.broadcast_to(chosen[None], out_ref.shape).astype(BF16)


def feat_grad_kernel(arrived_ref, z_slot_ref, out_ref):
    length = arrived_ref.shape[0]
    rows = turned(arrived_ref[...])[:CHANNELS].astype(BF16)
    out_ref[...] = dot(rows, on_rows(z_slot_ref[...], length)).astype(BF16)


def finish_kernel(factor, total_ref, qkv_t_ref, gain_in_ref, qkv_ref, out_ref, pool_ref, gain_ref):
    both = total_ref[...].astype(F32)
    both = (both[:, CHANNELS:] + both[:, :CHANNELS]) * factor
    piece = [both[k * CHANNELS : (k + 1) * CHANNELS] for k in range(6)]
    qkv = jnp.concatenate(piece[:3], axis=1)
    qkv_ref[...] = qkv
    out_ref[...] = piece[3]
    pool_ref[...] = jnp.concatenate(piece[4:], axis=1)
    column = jnp.sum(qkv * qkv_t_ref[...].astype(F32), axis=1, keepdims=True)
    eye = iota((CHANNELS, CHANNELS), 0) == iota((CHANNELS, CHANNELS), 1)
    gain_ref[...] = jnp.sum(jnp.where(eye, column, 0.0), axis=0, keepdims=True) / gain_in_ref[...]


def shape(dims, dtype):
    return jax.ShapeDtypeStruct(dims, dtype)


def call(kernel, outs, scratch=(), flops=0, **more):
    return pl.pallas_call(
        kernel,
        out_shape=outs,
        **more,
        scratch_shapes=list(scratch),
        compiler_params=pltpu.CompilerParams(vmem_limit_bytes=48 * 1024 * 1024),
        cost_estimate=pl.CostEstimate(flops=flops, bytes_accessed=1 << 20, transcendentals=0),
    )


def exchange(blocks):
    return lax.all_to_all(blocks, "pts", split_axis=0, concat_axis=0, tiled=True)


def body(
    feats,
    hilbert_of_z,
    pool_owner,
    pool_slot,
    qkv_weight,
    out_weight,
    pool_weight,
    norm_gain,
    pooled_grad,
):
    length = feats.shape[2]
    shards = lax.axis_size("pts")
    per_peer = length // shards
    clusters = pooled_grad.shape[2]
    lanes = 2 * CHANNELS
    qkv_t = qkv_weight.T
    pool_t = pool_weight.T
    gain = norm_gain.reshape(1, CHANNELS)
    upstream_pool = pooled_grad[0]

    arguments = tuple(
        pltpu.with_memory_space_constraint(one, pltpu.HBM)
        for one in (
        hilbert_of_z,
        pool_owner.reshape(1, length),
        pool_slot,
        feats[0],
        upstream_pool,
        qkv_t,
        out_weight,
        pool_t,
        gain,
        )
    )
    outgoing, z_slot, o_slot, upstream_pool, qkv_t, out_weight, pool_t, gain = call(
        send_kernel,
        (
            shape((shards, per_peer, lanes), BF16),
            shape((1, length), I32),
            shape((1, length), I32),
        )
        + tuple(shape(one.shape, one.dtype) for one in arguments[4:]),
        scratch=tuple(pltpu.VMEM(one.shape, one.dtype) for one in arguments[:4])
        + (pltpu.SemaphoreType.DMA((len(arguments),)),),
        flops=1 << 30,
        in_specs=[pl.BlockSpec(memory_space=pltpu.HBM)] * len(arguments),
    )(*arguments)
    arrived = exchange(outgoing).reshape(length, lanes)

    both_ways, hilbert_rows, attended, probs = call(
        forward_kernel,
        (
            shape((shards, 2 * per_peer, lanes), BF16),
            shape((CHANNELS, length), BF16),
            shape((CHANNELS, length), F32),
            shape((HEADS, length, length), BF16),
        ),
        scratch=(
            pltpu.VMEM((length, CHANNELS), BF16),
            pltpu.VMEM((CHANNELS, length), BF16),
            pltpu.VMEM((HEADS, length, CHANNELS), BF16),
            pltpu.VMEM((length, CHANNELS), F32),
        ),
        flops=1 << 32,
    )(arrived, o_slot, qkv_t, out_weight, pool_t, gain, upstream_pool)
    returned = exchange(both_ways)

    last, pooled = call(
        backward_kernel,
        (shape((shards, per_peer, lanes), BF16), shape((2 * CHANNELS, clusters), BF16)),
        scratch=(
            pltpu.VMEM((HEADS, length, CHANNELS), BF16),
            pltpu.VMEM((length, lanes), BF16),
            pltpu.VMEM((lanes, length), BF16),
            pltpu.VMEM((CHANNELS, length), BF16),
            pltpu.VMEM((CHANNELS, length), BF16),
            pltpu.VMEM((length, CHANNELS), F32),
            pltpu.VMEM((CHANNELS, length), F32),
            pltpu.VMEM((CHANNELS, length), F32),
        ),
        flops=1 << 33,
    )(
        returned,
        arrived,
        o_slot,
        qkv_t,
        out_weight,
        pool_t,
        gain,
        upstream_pool,
        hilbert_rows,
        attended,
        probs,
    )
    final = exchange(last)

    own = call(total_kernel, shape((per_peer, lanes), F32))(final)
    other = lax.ppermute(own, "rep", [(0, 1), (1, 0)])
    feat_grad = call(feat_grad_kernel, shape((CHANNELS, length), BF16), flops=1 << 28)(
        final.reshape(length, lanes), z_slot
    )
    total = call(spread_kernel, shape((GROUP, per_peer, lanes), BF16))(own, other)
    gathered = lax.all_to_all(
        total,
        "pts",
        split_axis=0,
        concat_axis=0,
        tiled=True,
        axis_index_groups=[
            list(range(start, start + GROUP)) for start in range(0, shards, GROUP)
        ],
    ).reshape(GROUP * per_peer, lanes)
    factor = float(lax.axis_size("rep") * shards * length) ** (-0.5)
    qkv_total, out_total, pool_total, gain_total = call(
        functools.partial(finish_kernel, factor),
        (
            shape((CHANNELS, 3 * CHANNELS), F32),
            shape((CHANNELS, CHANNELS), F32),
            shape((CHANNELS, lanes), F32),
            shape((1, CHANNELS), F32),
        ),
    )(gathered, qkv_t, gain)
    return (
        pooled[None],
        feat_grad[None],
        qkv_total.T,
        out_total,
        pool_total.T,
        gain_total.reshape(CHANNELS),
    )


def solution(mesh):
    return jax.shard_map(
        body,
        mesh=mesh,
        in_specs=(
            P("rep", None, "pts"),
            P("rep", "pts"),
            P("rep", "pts", None),
            P("rep", "pts"),
            P(),
            P(),
            P(),
            P(),
            P("rep", None, "pts"),
        ),
        out_specs=(P("rep", None, "pts"), P("rep", None, "pts"), P(), P(), P(), P()),
        check_vma=False,
    )
```

```python
import functools

import jax
import jax.numpy as jnp
from jax import lax
from jax.experimental import pallas as pl
from jax.experimental.pallas import tpu as pltpu
from jax.sharding import PartitionSpec as P

HEADS = 4
HEAD_DIM = 16
CHANNELS = 64
NORM_EPS = 1e-05
CHUNK = 256
GROUP = 64

F32 = jnp.float32
BF16 = jnp.bfloat16
I32 = jnp.int32


def dot(a, b):
    return lax.dot_general(a, b, (((1,), (0,)), ((), ())), preferred_element_type=F32)


def dot_nt(a, b):
    return lax.dot_general(a, b, (((1,), (1,)), ((), ())), preferred_element_type=F32)


def dot_tn(a, b):
    return lax.dot_general(a, b, (((0,), (0,)), ((), ())), preferred_element_type=F32)


def turned(a):
    return a.astype(F32).T


def iota(shape, dim):
    return lax.broadcasted_iota(I32, shape, dim)


def onehot(mask):
    return jnp.where(mask, 1.0, 0.0).astype(BF16)


def on_rows(row, count):
    return onehot(iota((count, row.shape[1]), 0) == row)


def on_columns(column, count):
    return onehot(iota((column.shape[0], count), 1) == column)


def rank_in_group(groups, count):
    length = groups.shape[1]
    member = on_rows(groups, count)
    upto = onehot(iota((128, 128), 0) <= iota((128, 128), 1))
    seen = jnp.zeros((count, 1), F32)
    ranks = []
    for start in range(0, length, 128):
        block = member[:, start : start + 128]
        running = dot(block, upto) + seen
        seen = running[:, 127:128]
        ranks.append(jnp.sum(block.astype(F32) * running, axis=0, keepdims=True) - 1.0)
    return jnp.concatenate(ranks, axis=1).astype(I32)


def send_kernel(
    pos_hbm,
    owner_hbm,
    cell_hbm,
    feats_hbm,
    pool_grad_hbm,
    qkv_t_hbm,
    out_w_hbm,
    pool_t_hbm,
    gain_hbm,
    out_ref,
    z_slot_ref,
    o_slot_ref,
    pool_grad_ref,
    qkv_t_ref,
    out_w_ref,
    pool_t_ref,
    gain_ref,
    pos_ref,
    owner_ref,
    cell_ref,
    feats_ref,
    sems,
):
    loads = [
        pltpu.make_async_copy(source, target, sems.at[number])
        for number, (source, target) in enumerate(
            (
                (pos_hbm, pos_ref),
                (owner_hbm, owner_ref),
                (cell_hbm, cell_ref),
                (feats_hbm, feats_ref),
                (pool_grad_hbm, pool_grad_ref),
                (qkv_t_hbm, qkv_t_ref),
                (out_w_hbm, out_w_ref),
                (pool_t_hbm, pool_t_ref),
                (gain_hbm, gain_ref),
            )
        )
    ]
    for load in loads:
        load.start()
    for load in loads[:3]:
        load.wait()
    length = pos_ref.shape[1]
    shards = out_ref.shape[0]
    per_peer = length // shards
    positions = pos_ref[...]
    owners = owner_ref[...]
    shift = length.bit_length() - 1
    target = lax.shift_right_logical(positions, shift)
    local = lax.bitwise_and(positions, length - 1)
    z_slot = target * per_peer + rank_in_group(target, shards)
    o_slot = owners * (2 * per_peer) + rank_in_group(owners, shards)
    z_slot_ref[...] = z_slot
    o_slot_ref[...] = o_slot
    row = iota((CHANNELS, length), 0)
    high = lax.shift_right_logical(local, 5).astype(F32)
    low = lax.bitwise_and(local, 31).astype(F32)
    place = jnp.where(row == 0, high, jnp.where(row == 1, low, 0.0)).astype(BF16)
    cell = (cell_ref[...] + 1).astype(F32)
    odd = lax.bitwise_and(o_slot, 1)
    cells = jnp.where(row - 2 == odd, cell, 0.0).astype(BF16)
    loads[3].wait()
    first = jnp.concatenate([feats_ref[...], place], axis=0)
    second = jnp.concatenate([jnp.zeros((CHANNELS, length), BF16), cells], axis=0)
    out = dot_nt(on_rows(z_slot, length), first)
    out = out + dot_nt(on_rows(lax.shift_right_logical(o_slot, 1), length), second)
    out_ref[...] = out.astype(BF16).reshape(out_ref.shape)
    for load in loads[4:]:
        load.wait()


def arrived_columns(arrived):
    side = arrived[:, CHANNELS:].astype(F32)
    place = (side[:, 0:1] * 32.0 + side[:, 1:2]).astype(I32)
    return place, side[:, 2:3].astype(I32) - 1, side[:, 3:4].astype(I32) - 1


def gain_column(gain_ref):
    gain = gain_ref[...]
    eye = iota((CHANNELS, CHANNELS), 0) == iota((CHANNELS, CHANNELS), 1)
    return jnp.sum(jnp.where(eye, gain, 0.0), axis=1, keepdims=True)


def layer_norm(floats, gain):
    centred = floats - jnp.mean(floats, axis=0, keepdims=True)
    inverse_std = lax.rsqrt(jnp.mean(centred * centred, axis=0, keepdims=True) + NORM_EPS)
    normed = centred * inverse_std
    return normed, inverse_std, (gain * normed).astype(BF16)


def cluster_counts(first, second):
    return jnp.maximum(
        jnp.sum(first.astype(F32) + second.astype(F32), axis=0, keepdims=True), 1.0
    )


def head_lanes(shape, head):
    return lax.shift_right_logical(iota(shape, 1), 4) == head


def forward_kernel(
    arrived_ref,
    o_slot_ref,
    qkv_t_ref,
    out_w_ref,
    pool_t_ref,
    gain_ref,
    pool_grad_ref,
    out_ref,
    hilbert_ref,
    attended_ref,
    probs_ref,
    query_ref,
    key_ref,
    value_ref,
    rows_ref,
):
    shards = out_ref.shape[0]
    length = arrived_ref.shape[0]
    clusters = pool_grad_ref.shape[1]
    arrived = arrived_ref[...]
    place, first_cell, second_cell = arrived_columns(arrived)
    first = on_columns(first_cell, clusters)
    second = on_columns(second_cell, clusters)
    denom = cluster_counts(first, second)
    grad_mean = (dot(pool_t_ref[...], pool_grad_ref[...]) / denom).astype(BF16)
    blank = jnp.zeros_like(grad_mean)
    back = dot_nt(first, jnp.concatenate([grad_mean, blank], axis=0))
    back = back + dot_nt(second, jnp.concatenate([blank, grad_mean], axis=0))
    per_peer = length // shards
    out_ref[:, per_peer:, :] = back.astype(BF16).reshape(shards, per_peer, 2 * CHANNELS)
    turned_rows = turned(arrived)[:CHANNELS].astype(BF16)
    floats = dot(turned_rows, on_columns(place, length))
    hilbert_ref[...] = floats.astype(BF16)
    _, _, hidden = layer_norm(floats, gain_column(gain_ref))
    qkv = dot_tn(qkv_t_ref[...], hidden).astype(BF16)
    query_ref[...] = (turned(qkv[:CHANNELS]) * HEAD_DIM ** (-0.5)).astype(BF16)
    key_ref[...] = qkv[CHANNELS : 2 * CHANNELS]
    values = turned(qkv[2 * CHANNELS :])
    for head in range(HEADS):
        mask = head_lanes((length, CHANNELS), head)
        value_ref[head] = jnp.where(mask, values, 0.0).astype(BF16)

    units = [(start, head) for start in range(0, length, CHUNK) for head in range(HEADS)]

    def scores(unit):
        start, head = unit
        queries = query_ref[start : start + CHUNK, :].astype(F32)
        mask = head_lanes((CHUNK, CHANNELS), head)
        return dot(jnp.where(mask, queries, 0.0).astype(BF16), key_ref[...])

    def mix(unit):
        start, head = unit
        return dot(probs_ref[head, start : start + CHUNK, :], value_ref[head])

    totals = []
    ready = scores(units[0])
    for number, (start, head) in enumerate(units):
        now = ready
        if number + 1 < len(units):
            ready = scores(units[number + 1])
        if number > 0:
            totals.append(mix(units[number - 1]))
        weights = jnp.exp(now)
        share = 1.0 / jnp.sum(weights, axis=1, keepdims=True)
        probs_ref[head, start : start + CHUNK, :] = (weights * share).astype(BF16)
    totals.append(mix(units[-1]))
    for number in range(0, len(units), HEADS):
        start = units[number][0]
        rows_ref[start : start + CHUNK, :] = sum(totals[number : number + HEADS])
    attended = rows_ref[...].T
    attended_ref[...] = attended
    mixed = (floats + dot(out_w_ref[...], attended.astype(BF16))).astype(BF16).astype(F32)
    o_slot = o_slot_ref[...]
    odd = lax.bitwise_and(o_slot, 1) == 1
    pair = jnp.concatenate([jnp.where(odd, 0.0, mixed), jnp.where(odd, mixed, 0.0)], axis=0)
    picked = dot_nt(on_rows(lax.shift_right_logical(o_slot, 1), length), pair.astype(BF16))
    out_ref[:, :per_peer, :] = picked.astype(BF16).reshape(shards, per_peer, 2 * CHANNELS)


def backward_kernel(
    returned_ref,
    arrived_ref,
    o_slot_ref,
    qkv_t_ref,
    out_w_ref,
    pool_t_ref,
    gain_ref,
    pool_grad_ref,
    hilbert_ref,
    attended_ref,
    probs_ref,
    out_ref,
    pooled_ref,
    key_rows_ref,
    upstream_ref,
    value_ref,
    query_ref,
    grad_out_ref,
    grad_query_ref,
    grad_key_ref,
    grad_value_ref,
):
    shards = out_ref.shape[0]
    length = arrived_ref.shape[0]
    clusters = pool_grad_ref.shape[1]
    per_peer = length // shards
    place, first_cell, second_cell = arrived_columns(arrived_ref[...])
    blank = jnp.zeros((CHANNELS, length), BF16)
    blank_clusters = jnp.zeros((CHANNELS, clusters), BF16)

    first = on_columns(first_cell, clusters)
    second = on_columns(second_cell, clusters)
    denom = cluster_counts(first, second)
    mixed_rows = turned(returned_ref[:, :per_peer, :].reshape(length, 2 * CHANNELS)).astype(BF16)
    sums = dot(mixed_rows[:CHANNELS], first) + dot(mixed_rows[CHANNELS:], second)
    pooled_mean = (sums / denom).astype(BF16)
    pooled_ref[...] = dot_tn(pool_t_ref[...], pooled_mean).astype(BF16)
    pool_parts = [
        dot_nt(pooled_mean, jnp.concatenate([blank_clusters, half], axis=0))
        for half in (pool_grad_ref[:CHANNELS, :], pool_grad_ref[CHANNELS:, :])
    ]

    gain = gain_column(gain_ref)
    normed, inverse_std, hidden = layer_norm(hilbert_ref[...].astype(F32), gain)
    qkv = dot_tn(qkv_t_ref[...], hidden).astype(BF16)
    query_ref[...] = qkv[:CHANNELS]
    key_rows = turned(qkv[CHANNELS : 2 * CHANNELS])
    for head in range(HEADS):
        mask = head_lanes((length, CHANNELS), head)
        key_rows_ref[head] = jnp.where(mask, key_rows, 0.0).astype(BF16)
    value_ref[:CHANNELS, :] = qkv[2 * CHANNELS :]
    value_ref[CHANNELS:, :] = jnp.ones((CHANNELS, length), BF16)

    o_slot = o_slot_ref[...]
    odd = lax.bitwise_and(o_slot, 1) == 1
    slots = turned(returned_ref[:, per_peer:, :].reshape(length, 2 * CHANNELS)).astype(BF16)
    both = dot(slots, on_rows(lax.shift_right_logical(o_slot, 1), length))
    grad_mixed = jnp.where(odd, both[CHANNELS:], both[:CHANNELS])
    grad_mixed_low = grad_mixed.astype(BF16)
    attended = attended_ref[...]
    attended_low = attended.astype(BF16)
    out_part = dot_nt(grad_mixed_low, jnp.concatenate([blank, attended_low], axis=0))
    grad_attended = dot_tn(out_w_ref[...], grad_mixed_low).astype(BF16)
    grad_out_ref[...] = grad_attended
    scaled = grad_attended.astype(F32) * HEAD_DIM ** (-0.5)
    delta = -jnp.sum((scaled * attended).reshape(HEADS, HEAD_DIM, length), axis=1)
    delta_high = delta.astype(BF16).astype(F32)
    rest = jnp.concatenate(
        [delta_high, delta - delta_high, jnp.zeros((CHANNELS - 2 * HEADS, length), F32)], axis=0
    )
    upstream_ref[...] = jnp.concatenate([scaled, rest], axis=0).T.astype(BF16)
    grad_key_ref[...] = jnp.zeros_like(grad_key_ref)
    grad_value_ref[...] = jnp.zeros_like(grad_value_ref)

    units = [(start, head) for start in range(0, length, CHUNK) for head in range(HEADS)]
    lane = iota((CHUNK, 2 * CHANNELS), 1)

    def change(unit):
        start, head = unit
        mask = (
            (lax.shift_right_logical(lane, 4) == head)
            | (lane == CHANNELS + head)
            | (lane == CHANNELS + HEADS + head)
        )
        upstream = upstream_ref[start : start + CHUNK, :].astype(F32)
        return dot(jnp.where(mask, upstream, 0.0).astype(BF16), value_ref[...])

    totals = []
    ready = change(units[0])
    for number, (start, head) in enumerate(units):
        own = slice(head * HEAD_DIM, (head + 1) * HEAD_DIM)
        rows = slice(start, start + CHUNK)
        now = ready
        if number + 1 < len(units):
            ready = change(units[number + 1])
        probs = probs_ref[head, rows, :]
        grad_value_ref[own, :] += dot(grad_out_ref[own, rows], probs)
        grad_scores = (probs.astype(F32) * now).astype(BF16)
        totals.append(dot(grad_scores, key_rows_ref[head]))
        grad_key_ref[own, :] += dot(query_ref[own, rows], grad_scores)
    for number in range(0, len(units), HEADS):
        start = units[number][0]
        grad_query_ref[start : start + CHUNK, :] = sum(totals[number : number + HEADS])
    grad_qkv = jnp.concatenate(
        [grad_query_ref[...].T, grad_key_ref[...], grad_value_ref[...]], axis=0
    ).astype(BF16)
    qkv_parts = [
        dot_nt(hidden, jnp.concatenate([blank, grad_qkv[start : start + CHANNELS]], axis=0))
        for start in (0, CHANNELS, 2 * CHANNELS)
    ]
    grad_hidden = dot(qkv_t_ref[...], grad_qkv)
    grad_normed = grad_hidden * gain
    grad_norm_in = inverse_std * (
        grad_normed
        - jnp.mean(grad_normed, axis=0, keepdims=True)
        - normed * jnp.mean(grad_normed * normed, axis=0, keepdims=True)
    )
    grad_rows = (grad_mixed + grad_norm_in).astype(BF16)
    back = dot_nt(on_columns(place, length), jnp.concatenate([grad_rows, blank], axis=0))
    parts = qkv_parts + [out_part] + pool_parts
    unused = jnp.zeros((GROUP * per_peer - len(parts) * CHANNELS, 2 * CHANNELS), F32)
    side = jnp.concatenate(parts + [unused], axis=0)
    span = GROUP * per_peer
    for start in range(0, shards, GROUP):
        rows = back[start * per_peer : start * per_peer + span] + side
        out_ref[start : start + GROUP] = rows.astype(BF16).reshape(GROUP, per_peer, 2 * CHANNELS)


def total_kernel(arrived_ref, out_ref):
    out_ref[...] = jnp.sum(arrived_ref[...].astype(F32), axis=0)


def spread_kernel(own_ref, other_ref, out_ref):
    total = own_ref[...] + other_ref[...]
    high = total.astype(BF16).astype(F32)
    low = pltpu.roll(total - high, CHANNELS, 1)
    chosen = jnp.where(iota(total.shape, 1) >= CHANNELS, high, low)
    out_ref[...] = jnp.broadcast_to(chosen[None], out_ref.shape).astype(BF16)


def feat_grad_kernel(arrived_ref, z_slot_ref, out_ref):
    length = arrived_ref.shape[0]
    rows = turned(arrived_ref[...])[:CHANNELS].astype(BF16)
    out_ref[...] = dot(rows, on_rows(z_slot_ref[...], length)).astype(BF16)


def finish_kernel(factor, total_ref, qkv_t_ref, gain_in_ref, qkv_ref, out_ref, pool_ref, gain_ref):
    both = total_ref[...].astype(F32)
    both = (both[:, CHANNELS:] + both[:, :CHANNELS]) * factor
    piece = [both[k * CHANNELS : (k + 1) * CHANNELS] for k in range(6)]
    qkv = jnp.concatenate(piece[:3], axis=1)
    qkv_ref[...] = qkv
    out_ref[...] = piece[3]
    pool_ref[...] = jnp.concatenate(piece[4:], axis=1)
    column = jnp.sum(qkv * qkv_t_ref[...].astype(F32), axis=1, keepdims=True)
    eye = iota((CHANNELS, CHANNELS), 0) == iota((CHANNELS, CHANNELS), 1)
    gain_ref[...] = jnp.sum(jnp.where(eye, column, 0.0), axis=0, keepdims=True) / gain_in_ref[...]


def shape(dims, dtype):
    return jax.ShapeDtypeStruct(dims, dtype)


def call(kernel, outs, scratch=(), flops=0, **more):
    return pl.pallas_call(
        kernel,
        out_shape=outs,
        **more,
        scratch_shapes=list(scratch),
        compiler_params=pltpu.CompilerParams(vmem_limit_bytes=28 * 1024 * 1024),
        cost_estimate=pl.CostEstimate(flops=flops, bytes_accessed=1 << 20, transcendentals=0),
    )


def exchange(blocks):
    return lax.all_to_all(blocks, "pts", split_axis=0, concat_axis=0, tiled=True)


def body(
    feats,
    hilbert_of_z,
    pool_owner,
    pool_slot,
    qkv_weight,
    out_weight,
    pool_weight,
    norm_gain,
    pooled_grad,
):
    length = feats.shape[2]
    shards = lax.axis_size("pts")
    per_peer = length // shards
    clusters = pooled_grad.shape[2]
    lanes = 2 * CHANNELS
    qkv_t = qkv_weight.T
    pool_t = pool_weight.T
    gain = norm_gain.reshape(1, CHANNELS)
    upstream_pool = pooled_grad[0]

    arguments = tuple(
        pltpu.with_memory_space_constraint(one, pltpu.HBM)
        for one in (
        hilbert_of_z,
        pool_owner.reshape(1, length),
        pool_slot,
        feats[0],
        upstream_pool,
        qkv_t,
        out_weight,
        pool_t,
        gain,
        )
    )
    outgoing, z_slot, o_slot, upstream_pool, qkv_t, out_weight, pool_t, gain = call(
        send_kernel,
        (
            shape((shards, per_peer, lanes), BF16),
            shape((1, length), I32),
            shape((1, length), I32),
        )
        + tuple(shape(one.shape, one.dtype) for one in arguments[4:]),
        scratch=tuple(pltpu.VMEM(one.shape, one.dtype) for one in arguments[:4])
        + (pltpu.SemaphoreType.DMA((len(arguments),)),),
        flops=1 << 30,
        in_specs=[pl.BlockSpec(memory_space=pltpu.HBM)] * len(arguments),
    )(*arguments)
    arrived = exchange(outgoing).reshape(length, lanes)

    both_ways, hilbert_rows, attended, probs = call(
        forward_kernel,
        (
            shape((shards, 2 * per_peer, lanes), BF16),
            shape((CHANNELS, length), BF16),
            shape((CHANNELS, length), F32),
            shape((HEADS, length, length), BF16),
        ),
        scratch=(
            pltpu.VMEM((length, CHANNELS), BF16),
            pltpu.VMEM((CHANNELS, length), BF16),
            pltpu.VMEM((HEADS, length, CHANNELS), BF16),
            pltpu.VMEM((length, CHANNELS), F32),
        ),
        flops=1 << 32,
    )(arrived, o_slot, qkv_t, out_weight, pool_t, gain, upstream_pool)
    returned = exchange(both_ways)

    last, pooled = call(
        backward_kernel,
        (shape((shards, per_peer, lanes), BF16), shape((2 * CHANNELS, clusters), BF16)),
        scratch=(
            pltpu.VMEM((HEADS, length, CHANNELS), BF16),
            pltpu.VMEM((length, lanes), BF16),
            pltpu.VMEM((lanes, length), BF16),
            pltpu.VMEM((CHANNELS, length), BF16),
            pltpu.VMEM((CHANNELS, length), BF16),
            pltpu.VMEM((length, CHANNELS), F32),
            pltpu.VMEM((CHANNELS, length), F32),
            pltpu.VMEM((CHANNELS, length), F32),
        ),
        flops=1 << 33,
    )(
        returned,
        arrived,
        o_slot,
        qkv_t,
        out_weight,
        pool_t,
        gain,
        upstream_pool,
        hilbert_rows,
        attended,
        probs,
    )
    final = exchange(last)

    own = call(total_kernel, shape((per_peer, lanes), F32))(final)
    other = lax.ppermute(own, "rep", [(0, 1), (1, 0)])
    feat_grad = call(feat_grad_kernel, shape((CHANNELS, length), BF16), flops=1 << 28)(
        final.reshape(length, lanes), z_slot
    )
    total = call(spread_kernel, shape((GROUP, per_peer, lanes), BF16))(own, other)
    gathered = lax.all_to_all(
        total,
        "pts",
        split_axis=0,
        concat_axis=0,
        tiled=True,
        axis_index_groups=[
            list(range(start, start + GROUP)) for start in range(0, shards, GROUP)
        ],
    ).reshape(GROUP * per_peer, lanes)
    factor = float(lax.axis_size("rep") * shards * length) ** (-0.5)
    qkv_total, out_total, pool_total, gain_total = call(
        functools.partial(finish_kernel, factor),
        (
            shape((CHANNELS, 3 * CHANNELS), F32),
            shape((CHANNELS, CHANNELS), F32),
            shape((CHANNELS, lanes), F32),
            shape((1, CHANNELS), F32),
        ),
    )(gathered, qkv_t, gain)
    return (
        pooled[None],
        feat_grad[None],
        qkv_total.T,
        out_total,
        pool_total.T,
        gain_total.reshape(CHANNELS),
    )


def solution(mesh):
    return jax.shard_map(
        body,
        mesh=mesh,
        in_specs=(
            P("rep", None, "pts"),
            P("rep", "pts"),
            P("rep", "pts", None),
            P("rep", "pts"),
            P(),
            P(),
            P(),
            P(),
            P("rep", None, "pts"),
        ),
        out_specs=(P("rep", None, "pts"), P("rep", None, "pts"), P(), P(), P(), P()),
        check_vma=False,
    )
```

```python
import functools

import jax
import jax.numpy as jnp
from jax import lax
from jax.experimental import pallas as pl
from jax.experimental.pallas import tpu as pltpu
from jax.sharding import PartitionSpec as P

HEADS = 4
HEAD_DIM = 16
CHANNELS = 64
NORM_EPS = 1e-05
CHUNK = 256
GROUP = 64
PLANE = 16
LAYERS = 8

F32 = jnp.float32
BF16 = jnp.bfloat16
I32 = jnp.int32


def dot(a, b):
    return lax.dot_general(a, b, (((1,), (0,)), ((), ())), preferred_element_type=F32)


def dot_nt(a, b):
    return lax.dot_general(a, b, (((1,), (1,)), ((), ())), preferred_element_type=F32)


def dot_tn(a, b):
    return lax.dot_general(a, b, (((0,), (0,)), ((), ())), preferred_element_type=F32)


def turned(a):
    return a.astype(F32).T


def iota(shape, dim):
    return lax.broadcasted_iota(I32, shape, dim)


def onehot(mask):
    return jnp.where(mask, 1.0, 0.0).astype(BF16)


def on_rows(row, count):
    return onehot(iota((count, row.shape[1]), 0) == row)


def on_columns(column, count):
    return onehot(iota((column.shape[0], count), 1) == column)


def rank_in_group(groups, count):
    length = groups.shape[1]
    member = on_rows(groups, count)
    upto = onehot(iota((128, 128), 0) <= iota((128, 128), 1))
    seen = jnp.zeros((count, 1), F32)
    ranks = []
    for start in range(0, length, 128):
        block = member[:, start : start + 128]
        running = dot(block, upto) + seen
        seen = running[:, 127:128]
        ranks.append(jnp.sum(block.astype(F32) * running, axis=0, keepdims=True) - 1.0)
    return jnp.concatenate(ranks, axis=1).astype(I32)


def exchange_place(shard):
    plane_place = lax.bitwise_and(shard, PLANE - 1)
    layer = lax.shift_right_logical(shard, PLANE.bit_length() - 1)
    return plane_place * LAYERS + layer


def send_kernel(
    pos_hbm,
    owner_hbm,
    cell_hbm,
    feats_hbm,
    pool_grad_hbm,
    qkv_t_hbm,
    out_w_hbm,
    pool_t_hbm,
    gain_hbm,
    out_ref,
    z_slot_ref,
    o_slot_ref,
    pool_grad_ref,
    qkv_t_ref,
    out_w_ref,
    pool_t_ref,
    gain_ref,
    pos_ref,
    owner_ref,
    cell_ref,
    feats_ref,
    sems,
):
    loads = [
        pltpu.make_async_copy(source, target, sems.at[number])
        for number, (source, target) in enumerate(
            (
                (pos_hbm, pos_ref),
                (owner_hbm, owner_ref),
                (cell_hbm, cell_ref),
                (feats_hbm, feats_ref),
                (pool_grad_hbm, pool_grad_ref),
                (qkv_t_hbm, qkv_t_ref),
                (out_w_hbm, out_w_ref),
                (pool_t_hbm, pool_t_ref),
                (gain_hbm, gain_ref),
            )
        )
    ]
    for load in loads:
        load.start()
    for load in loads[:3]:
        load.wait()
    length = pos_ref.shape[1]
    shards = out_ref.shape[0]
    per_peer = length // shards
    positions = pos_ref[...]
    owners = exchange_place(owner_ref[...])
    shift = length.bit_length() - 1
    target = exchange_place(lax.shift_right_logical(positions, shift))
    local = lax.bitwise_and(positions, length - 1)
    z_slot = target * per_peer + rank_in_group(target, shards)
    o_slot = owners * (2 * per_peer) + rank_in_group(owners, shards)
    z_slot_ref[...] = z_slot
    o_slot_ref[...] = o_slot
    row = iota((CHANNELS, length), 0)
    high = lax.shift_right_logical(local, 5).astype(F32)
    low = lax.bitwise_and(local, 31).astype(F32)
    place = jnp.where(row == 0, high, jnp.where(row == 1, low, 0.0)).astype(BF16)
    cell = (cell_ref[...] + 1).astype(F32)
    odd = lax.bitwise_and(o_slot, 1)
    cells = jnp.where(row - 2 == odd, cell, 0.0).astype(BF16)
    loads[3].wait()
    first = jnp.concatenate([feats_ref[...], place], axis=0)
    second = jnp.concatenate([jnp.zeros((CHANNELS, length), BF16), cells], axis=0)
    out = dot_nt(on_rows(z_slot, length), first)
    out = out + dot_nt(on_rows(lax.shift_right_logical(o_slot, 1), length), second)
    out_ref[...] = out.astype(BF16).reshape(out_ref.shape)
    for load in loads[4:]:
        load.wait()


def arrived_columns(arrived):
    side = arrived[:, CHANNELS:].astype(F32)
    place = (side[:, 0:1] * 32.0 + side[:, 1:2]).astype(I32)
    return place, side[:, 2:3].astype(I32) - 1, side[:, 3:4].astype(I32) - 1


def gain_column(gain_ref):
    gain = gain_ref[...]
    eye = iota((CHANNELS, CHANNELS), 0) == iota((CHANNELS, CHANNELS), 1)
    return jnp.sum(jnp.where(eye, gain, 0.0), axis=1, keepdims=True)


def layer_norm(floats, gain):
    centred = floats - jnp.mean(floats, axis=0, keepdims=True)
    inverse_std = lax.rsqrt(jnp.mean(centred * centred, axis=0, keepdims=True) + NORM_EPS)
    normed = centred * inverse_std
    return normed, inverse_std, (gain * normed).astype(BF16)


def cluster_counts(first, second):
    return jnp.maximum(
        jnp.sum(first.astype(F32) + second.astype(F32), axis=0, keepdims=True), 1.0
    )


def head_lanes(shape, head):
    return lax.shift_right_logical(iota(shape, 1), 4) == head


def points_kernel(o_slot_ref, pool_t_ref, pool_grad_ref, slot_map_ref, cluster_grad_ref):
    rows = lax.shift_right_logical(o_slot_ref[...], 1)
    slot_map_ref[...] = on_rows(rows, slot_map_ref.shape[0])
    cluster_grad_ref[...] = dot(pool_t_ref[...], pool_grad_ref[...])


def forward_kernel(
    arrived_ref,
    o_slot_ref,
    slot_map_ref,
    qkv_t_ref,
    out_w_ref,
    gain_ref,
    cluster_grad_ref,
    out_ref,
    hilbert_ref,
    attended_ref,
    probs_ref,
    query_ref,
    key_ref,
    value_ref,
    rows_ref,
):
    shards = out_ref.shape[0]
    length = arrived_ref.shape[0]
    clusters = cluster_grad_ref.shape[1]
    arrived = arrived_ref[...]
    place, first_cell, second_cell = arrived_columns(arrived)
    first = on_columns(first_cell, clusters)
    second = on_columns(second_cell, clusters)
    denom = cluster_counts(first, second)
    grad_mean = (cluster_grad_ref[...] / denom).astype(BF16)
    blank = jnp.zeros_like(grad_mean)
    back = dot_nt(first, jnp.concatenate([grad_mean, blank], axis=0))
    back = back + dot_nt(second, jnp.concatenate([blank, grad_mean], axis=0))
    per_peer = length // shards
    out_ref[:, per_peer:, :] = back.astype(BF16).reshape(shards, per_peer, 2 * CHANNELS)
    turned_rows = turned(arrived)[:CHANNELS].astype(BF16)
    floats = dot(turned_rows, on_columns(place, length))
    hilbert_ref[...] = floats.astype(BF16)
    _, _, hidden = layer_norm(floats, gain_column(gain_ref))
    qkv = dot_tn(qkv_t_ref[...], hidden).astype(BF16)
    query_ref[...] = (turned(qkv[:CHANNELS]) * HEAD_DIM ** (-0.5)).astype(BF16)
    key_ref[...] = qkv[CHANNELS : 2 * CHANNELS]
    values = turned(qkv[2 * CHANNELS :])
    for head in range(HEADS):
        mask = head_lanes((length, CHANNELS), head)
        value_ref[head] = jnp.where(mask, values, 0.0).astype(BF16)

    units = [(start, head) for start in range(0, length, CHUNK) for head in range(HEADS)]

    def scores(unit):
        start, head = unit
        queries = query_ref[start : start + CHUNK, :].astype(F32)
        mask = head_lanes((CHUNK, CHANNELS), head)
        return dot(jnp.where(mask, queries, 0.0).astype(BF16), key_ref[...])

    def mix(unit):
        start, head = unit
        return dot(probs_ref[head, start : start + CHUNK, :], value_ref[head])

    totals = []
    ready = scores(units[0])
    for number, (start, head) in enumerate(units):
        now = ready
        if number + 1 < len(units):
            ready = scores(units[number + 1])
        if number > 0:
            totals.append(mix(units[number - 1]))
        weights = jnp.exp(now)
        share = 1.0 / jnp.sum(weights, axis=1, keepdims=True)
        probs_ref[head, start : start + CHUNK, :] = (weights * share).astype(BF16)
    totals.append(mix(units[-1]))
    for number in range(0, len(units), HEADS):
        start = units[number][0]
        rows_ref[start : start + CHUNK, :] = sum(totals[number : number + HEADS])
    attended = rows_ref[...].T
    attended_ref[...] = attended
    mixed = (floats + dot(out_w_ref[...], attended.astype(BF16))).astype(BF16).astype(F32)
    o_slot = o_slot_ref[...]
    odd = lax.bitwise_and(o_slot, 1) == 1
    pair = jnp.concatenate([jnp.where(odd, 0.0, mixed), jnp.where(odd, mixed, 0.0)], axis=0)
    picked = dot_nt(slot_map_ref[...], pair.astype(BF16))
    out_ref[:, :per_peer, :] = picked.astype(BF16).reshape(shards, per_peer, 2 * CHANNELS)


def ahead_kernel(
    arrived_ref,
    hilbert_ref,
    qkv_t_ref,
    gain_ref,
    place_ref,
    first_ref,
    second_ref,
    denom_ref,
    hidden_ref,
    normed_ref,
    inverse_std_ref,
    query_ref,
    key_rows_ref,
    value_ref,
):
    length = arrived_ref.shape[0]
    clusters = first_ref.shape[1]
    place, first_cell, second_cell = arrived_columns(arrived_ref[...])
    place_ref[...] = on_columns(place, length)
    first = on_columns(first_cell, clusters)
    second = on_columns(second_cell, clusters)
    first_ref[...] = first
    second_ref[...] = second
    denom_ref[...] = cluster_counts(first, second)
    normed, inverse_std, hidden = layer_norm(
        hilbert_ref[...].astype(F32), gain_column(gain_ref)
    )
    hidden_ref[...] = hidden
    normed_ref[...] = normed
    inverse_std_ref[...] = inverse_std
    qkv = dot_tn(qkv_t_ref[...], hidden).astype(BF16)
    query_ref[...] = qkv[:CHANNELS]
    key_rows = turned(qkv[CHANNELS : 2 * CHANNELS])
    for head in range(HEADS):
        mask = head_lanes((length, CHANNELS), head)
        key_rows_ref[head] = jnp.where(mask, key_rows, 0.0).astype(BF16)
    value_ref[:CHANNELS, :] = qkv[2 * CHANNELS :]
    value_ref[CHANNELS:, :] = jnp.ones((CHANNELS, length), BF16)


def backward_kernel(
    returned_ref,
    o_slot_ref,
    slot_map_ref,
    qkv_t_ref,
    out_w_ref,
    pool_t_ref,
    gain_ref,
    pool_grad_ref,
    attended_ref,
    probs_ref,
    place_ref,
    first_ref,
    second_ref,
    denom_ref,
    hidden_ref,
    normed_ref,
    inverse_std_ref,
    query_ref,
    key_rows_ref,
    value_ref,
    out_ref,
    pooled_ref,
    upstream_ref,
    grad_out_ref,
    grad_query_ref,
    grad_key_ref,
    grad_value_ref,
):
    shards = out_ref.shape[0]
    length = o_slot_ref.shape[1]
    clusters = pool_grad_ref.shape[1]
    per_peer = length // shards
    blank = jnp.zeros((CHANNELS, length), BF16)
    blank_clusters = jnp.zeros((CHANNELS, clusters), BF16)

    mixed_rows = turned(returned_ref[:, :per_peer, :].reshape(length, 2 * CHANNELS)).astype(BF16)
    sums = dot(mixed_rows[:CHANNELS], first_ref[...]) + dot(mixed_rows[CHANNELS:], second_ref[...])
    pooled_mean = (sums / denom_ref[...]).astype(BF16)
    pooled_ref[...] = dot_tn(pool_t_ref[...], pooled_mean).astype(BF16)
    pool_parts = [
        dot_nt(pooled_mean, jnp.concatenate([blank_clusters, half], axis=0))
        for half in (pool_grad_ref[:CHANNELS, :], pool_grad_ref[CHANNELS:, :])
    ]

    o_slot = o_slot_ref[...]
    odd = lax.bitwise_and(o_slot, 1) == 1
    slots = turned(returned_ref[:, per_peer:, :].reshape(length, 2 * CHANNELS)).astype(BF16)
    both = dot(slots, slot_map_ref[...])
    grad_mixed = jnp.where(odd, both[CHANNELS:], both[:CHANNELS])
    grad_mixed_low = grad_mixed.astype(BF16)
    attended = attended_ref[...]
    attended_low = attended.astype(BF16)
    out_part = dot_nt(grad_mixed_low, jnp.concatenate([blank, attended_low], axis=0))
    grad_attended = dot_tn(out_w_ref[...], grad_mixed_low).astype(BF16)
    grad_out_ref[...] = grad_attended
    scaled = grad_attended.astype(F32) * HEAD_DIM ** (-0.5)
    delta = -jnp.sum((scaled * attended).reshape(HEADS, HEAD_DIM, length), axis=1)
    delta_high = delta.astype(BF16).astype(F32)
    rest = jnp.concatenate(
        [delta_high, delta - delta_high, jnp.zeros((CHANNELS - 2 * HEADS, length), F32)], axis=0
    )
    upstream_ref[...] = jnp.concatenate([scaled, rest], axis=0).T.astype(BF16)
    grad_key_ref[...] = jnp.zeros_like(grad_key_ref)
    grad_value_ref[...] = jnp.zeros_like(grad_value_ref)

    units = [(start, head) for start in range(0, length, CHUNK) for head in range(HEADS)]
    lane = iota((CHUNK, 2 * CHANNELS), 1)

    def change(unit):
        start, head = unit
        mask = (
            (lax.shift_right_logical(lane, 4) == head)
            | (lane == CHANNELS + head)
            | (lane == CHANNELS + HEADS + head)
        )
        upstream = upstream_ref[start : start + CHUNK, :].astype(F32)
        return dot(jnp.where(mask, upstream, 0.0).astype(BF16), value_ref[...])

    totals = []
    ready = change(units[0])
    for number, (start, head) in enumerate(units):
        own = slice(head * HEAD_DIM, (head + 1) * HEAD_DIM)
        rows = slice(start, start + CHUNK)
        now = ready
        if number + 1 < len(units):
            ready = change(units[number + 1])
        probs = probs_ref[head, rows, :]
        grad_value_ref[own, :] += dot(grad_out_ref[own, rows], probs)
        grad_scores = (probs.astype(F32) * now).astype(BF16)
        totals.append(dot(grad_scores, key_rows_ref[head]))
        grad_key_ref[own, :] += dot(query_ref[own, rows], grad_scores)
    for number in range(0, len(units), HEADS):
        start = units[number][0]
        grad_query_ref[start : start + CHUNK, :] = sum(totals[number : number + HEADS])
    grad_qkv = jnp.concatenate(
        [grad_query_ref[...].T, grad_key_ref[...], grad_value_ref[...]], axis=0
    ).astype(BF16)
    hidden = hidden_ref[...]
    normed = normed_ref[...]
    inverse_std = inverse_std_ref[...]
    qkv_parts = [
        dot_nt(hidden, jnp.concatenate([blank, grad_qkv[start : start + CHANNELS]], axis=0))
        for start in (0, CHANNELS, 2 * CHANNELS)
    ]
    grad_hidden = dot(qkv_t_ref[...], grad_qkv)
    grad_normed = grad_hidden * gain_column(gain_ref)
    grad_norm_in = inverse_std * (
        grad_normed
        - jnp.mean(grad_normed, axis=0, keepdims=True)
        - normed * jnp.mean(grad_normed * normed, axis=0, keepdims=True)
    )
    grad_rows = (grad_mixed + grad_norm_in).astype(BF16)
    back = dot_nt(place_ref[...], jnp.concatenate([grad_rows, blank], axis=0))
    parts = qkv_parts + [out_part] + pool_parts
    unused = jnp.zeros((GROUP * per_peer - len(parts) * CHANNELS, 2 * CHANNELS), F32)
    side = jnp.concatenate(parts + [unused], axis=0)
    span = GROUP * per_peer
    for start in range(0, shards, GROUP):
        rows = back[start * per_peer : start * per_peer + span] + side
        out_ref[start : start + GROUP] = rows.astype(BF16).reshape(GROUP, per_peer, 2 * CHANNELS)


def total_kernel(arrived_ref, out_ref):
    total = jnp.sum(arrived_ref[...].astype(F32), axis=0)
    high = total.astype(BF16).astype(F32)
    low = pltpu.roll(total - high, CHANNELS, 1)
    chosen = jnp.where(iota(total.shape, 1) >= CHANNELS, high, low)
    out_ref[...] = jnp.broadcast_to(chosen[None], out_ref.shape).astype(BF16)


def feat_grad_kernel(arrived_ref, z_slot_ref, out_ref):
    length = arrived_ref.shape[0]
    rows = turned(arrived_ref[...])[:CHANNELS].astype(BF16)
    out_ref[...] = dot(rows, on_rows(z_slot_ref[...], length)).astype(BF16)


def finish_kernel(
    factor,
    own_ref,
    other_ref,
    qkv_t_ref,
    gain_in_ref,
    qkv_ref,
    out_ref,
    pool_ref,
    gain_ref,
):
    both = own_ref[...].astype(F32) + other_ref[...].astype(F32)
    both = (both[:, CHANNELS:] + both[:, :CHANNELS]) * factor
    piece = [both[k * CHANNELS : (k + 1) * CHANNELS] for k in range(6)]
    qkv = jnp.concatenate(piece[:3], axis=1)
    qkv_ref[...] = qkv
    out_ref[...] = piece[3]
    pool_ref[...] = jnp.concatenate(piece[4:], axis=1)
    column = jnp.sum(qkv * qkv_t_ref[...].astype(F32), axis=1, keepdims=True)
    eye = iota((CHANNELS, CHANNELS), 0) == iota((CHANNELS, CHANNELS), 1)
    gain_ref[...] = jnp.sum(jnp.where(eye, column, 0.0), axis=0, keepdims=True) / gain_in_ref[...]


def shape(dims, dtype):
    return jax.ShapeDtypeStruct(dims, dtype)


def call(kernel, outs, scratch=(), flops=0, **more):
    return pl.pallas_call(
        kernel,
        out_shape=outs,
        **more,
        scratch_shapes=list(scratch),
        compiler_params=pltpu.CompilerParams(vmem_limit_bytes=28 * 1024 * 1024),
        cost_estimate=pl.CostEstimate(flops=flops, bytes_accessed=1 << 20, transcendentals=0),
    )


def exchange(blocks, size):
    order = [layer * PLANE + place for place in range(PLANE) for layer in range(LAYERS)]
    return lax.all_to_all(
        blocks,
        "pts",
        split_axis=0,
        concat_axis=0,
        tiled=True,
        axis_index_groups=[order[start : start + size] for start in range(0, len(order), size)],
    )


def body(
    feats,
    hilbert_of_z,
    pool_owner,
    pool_slot,
    qkv_weight,
    out_weight,
    pool_weight,
    norm_gain,
    pooled_grad,
):
    length = feats.shape[2]
    shards = lax.axis_size("pts")
    per_peer = length // shards
    clusters = pooled_grad.shape[2]
    lanes = 2 * CHANNELS
    qkv_t = qkv_weight.T
    pool_t = pool_weight.T
    gain = norm_gain.reshape(1, CHANNELS)
    upstream_pool = pooled_grad[0]

    arguments = tuple(
        pltpu.with_memory_space_constraint(one, pltpu.HBM)
        for one in (
        hilbert_of_z,
        pool_owner.reshape(1, length),
        pool_slot,
        feats[0],
        upstream_pool,
        qkv_t,
        out_weight,
        pool_t,
        gain,
        )
    )
    outgoing, z_slot, o_slot, upstream_pool, qkv_t, out_weight, pool_t, gain = call(
        send_kernel,
        (
            shape((shards, per_peer, lanes), BF16),
            shape((1, length), I32),
            shape((1, length), I32),
        )
        + tuple(shape(one.shape, one.dtype) for one in arguments[4:]),
        scratch=tuple(pltpu.VMEM(one.shape, one.dtype) for one in arguments[:4])
        + (pltpu.SemaphoreType.DMA((len(arguments),)),),
        flops=1 << 30,
        in_specs=[pl.BlockSpec(memory_space=pltpu.HBM)] * len(arguments),
    )(*arguments)
    arrived = exchange(outgoing, shards).reshape(length, lanes)
    slot_map, cluster_grad = call(
        points_kernel,
        (shape((length, length), BF16), shape((CHANNELS, clusters), F32)),
        flops=1 << 31,
    )(o_slot, pool_t, upstream_pool)

    both_ways, hilbert_rows, attended, probs = call(
        forward_kernel,
        (
            shape((shards, 2 * per_peer, lanes), BF16),
            shape((CHANNELS, length), BF16),
            shape((CHANNELS, length), F32),
            shape((HEADS, length, length), BF16),
        ),
        scratch=(
            pltpu.VMEM((length, CHANNELS), BF16),
            pltpu.VMEM((CHANNELS, length), BF16),
            pltpu.VMEM((HEADS, length, CHANNELS), BF16),
            pltpu.VMEM((length, CHANNELS), F32),
        ),
        flops=1 << 32,
    )(arrived, o_slot, slot_map, qkv_t, out_weight, gain, cluster_grad)
    returned = exchange(both_ways, shards)
    ahead = call(
        ahead_kernel,
        (
            shape((length, length), BF16),
            shape((length, clusters), BF16),
            shape((length, clusters), BF16),
            shape((1, clusters), F32),
            shape((CHANNELS, length), BF16),
            shape((CHANNELS, length), F32),
            shape((1, length), F32),
            shape((CHANNELS, length), BF16),
            shape((HEADS, length, CHANNELS), BF16),
            shape((lanes, length), BF16),
        ),
        flops=1 << 31,
    )(arrived, hilbert_rows, qkv_t, gain)

    last, pooled = call(
        backward_kernel,
        (shape((shards, per_peer, lanes), BF16), shape((2 * CHANNELS, clusters), BF16)),
        scratch=(
            pltpu.VMEM((length, lanes), BF16),
            pltpu.VMEM((CHANNELS, length), BF16),
            pltpu.VMEM((length, CHANNELS), F32),
            pltpu.VMEM((CHANNELS, length), F32),
            pltpu.VMEM((CHANNELS, length), F32),
        ),
        flops=1 << 33,
    )(
        returned,
        o_slot,
        slot_map,
        qkv_t,
        out_weight,
        pool_t,
        gain,
        upstream_pool,
        attended,
        probs,
        *ahead,
    )
    final = exchange(last, shards)

    total = call(total_kernel, shape((GROUP, per_peer, lanes), BF16))(final)
    gathered = exchange(total, GROUP).reshape(GROUP * per_peer, lanes)
    feat_grad = call(feat_grad_kernel, shape((CHANNELS, length), BF16), flops=1 << 30)(
        final.reshape(length, lanes), z_slot
    )
    other = lax.ppermute(gathered, "rep", [(0, 1), (1, 0)])
    factor = float(lax.axis_size("rep") * shards * length) ** (-0.5)
    qkv_total, out_total, pool_total, gain_total = call(
        functools.partial(finish_kernel, factor),
        (
            shape((CHANNELS, 3 * CHANNELS), F32),
            shape((CHANNELS, CHANNELS), F32),
            shape((CHANNELS, lanes), F32),
            shape((1, CHANNELS), F32),
        ),
    )(gathered, other, qkv_t, gain)
    return (
        pooled[None],
        feat_grad[None],
        qkv_total.T,
        out_total,
        pool_total.T,
        gain_total.reshape(CHANNELS),
    )


def solution(mesh):
    return jax.shard_map(
        body,
        mesh=mesh,
        in_specs=(
            P("rep", None, "pts"),
            P("rep", "pts"),
            P("rep", "pts", None),
            P("rep", "pts"),
            P(),
            P(),
            P(),
            P(),
            P("rep", None, "pts"),
        ),
        out_specs=(P("rep", None, "pts"), P("rep", None, "pts"), P(), P(), P(), P()),
        check_vma=False,
    )
```

```python
import functools

import jax
import jax.numpy as jnp
from jax import lax
from jax.experimental import pallas as pl
from jax.experimental.pallas import tpu as pltpu
from jax.sharding import PartitionSpec as P

HEADS = 4
HEAD_DIM = 16
CHANNELS = 64
NORM_EPS = 1e-05
CHUNK = 256
GROUP = 32
PLANE = 16
LAYERS = 8

F32 = jnp.float32
BF16 = jnp.bfloat16
I32 = jnp.int32


def dot(a, b):
    return lax.dot_general(a, b, (((1,), (0,)), ((), ())), preferred_element_type=F32)


def dot_nt(a, b):
    return lax.dot_general(a, b, (((1,), (1,)), ((), ())), preferred_element_type=F32)


def dot_tn(a, b):
    return lax.dot_general(a, b, (((0,), (0,)), ((), ())), preferred_element_type=F32)


def turned(a):
    return a.astype(F32).T


def iota(shape, dim):
    return lax.broadcasted_iota(I32, shape, dim)


def onehot(mask):
    return jnp.where(mask, 1.0, 0.0).astype(BF16)


def on_rows(row, count):
    return onehot(iota((count, row.shape[1]), 0) == row)


def on_columns(column, count):
    return onehot(iota((column.shape[0], count), 1) == column)


def rank_in_group(groups, count):
    length = groups.shape[1]
    member = on_rows(groups, count)
    upto = onehot(iota((128, 128), 0) <= iota((128, 128), 1))
    seen = jnp.zeros((count, 1), F32)
    ranks = []
    for start in range(0, length, 128):
        block = member[:, start : start + 128]
        running = dot(block, upto) + seen
        seen = running[:, 127:128]
        ranks.append(jnp.sum(block.astype(F32) * running, axis=0, keepdims=True) - 1.0)
    return jnp.concatenate(ranks, axis=1).astype(I32)


def exchange_place(shard):
    plane_place = lax.bitwise_and(shard, PLANE - 1)
    layer = lax.shift_right_logical(shard, PLANE.bit_length() - 1)
    return plane_place * LAYERS + layer


def send_kernel(
    pos_hbm,
    owner_hbm,
    cell_hbm,
    feats_hbm,
    pool_grad_hbm,
    qkv_t_hbm,
    out_w_hbm,
    pool_t_hbm,
    gain_hbm,
    out_ref,
    z_slot_ref,
    o_slot_ref,
    pool_grad_ref,
    qkv_t_ref,
    out_w_ref,
    pool_t_ref,
    gain_ref,
    pos_ref,
    owner_ref,
    cell_ref,
    feats_ref,
    sems,
):
    loads = [
        pltpu.make_async_copy(source, target, sems.at[number])
        for number, (source, target) in enumerate(
            (
                (pos_hbm, pos_ref),
                (owner_hbm, owner_ref),
                (cell_hbm, cell_ref),
                (feats_hbm, feats_ref),
                (pool_grad_hbm, pool_grad_ref),
                (qkv_t_hbm, qkv_t_ref),
                (out_w_hbm, out_w_ref),
                (pool_t_hbm, pool_t_ref),
                (gain_hbm, gain_ref),
            )
        )
    ]
    for load in loads:
        load.start()
    for load in loads[:3]:
        load.wait()
    length = pos_ref.shape[1]
    shards = out_ref.shape[0]
    per_peer = length // shards
    positions = pos_ref[...]
    owners = exchange_place(owner_ref[...])
    shift = length.bit_length() - 1
    target = exchange_place(lax.shift_right_logical(positions, shift))
    local = lax.bitwise_and(positions, length - 1)
    z_slot = target * per_peer + rank_in_group(target, shards)
    o_slot = owners * (2 * per_peer) + rank_in_group(owners, shards)
    z_slot_ref[...] = z_slot
    o_slot_ref[...] = o_slot
    row = iota((CHANNELS, length), 0)
    high = lax.shift_right_logical(local, 5).astype(F32)
    low = lax.bitwise_and(local, 31).astype(F32)
    place = jnp.where(row == 0, high, jnp.where(row == 1, low, 0.0)).astype(BF16)
    cell = (cell_ref[...] + 1).astype(F32)
    odd = lax.bitwise_and(o_slot, 1)
    cells = jnp.where(row - 2 == odd, cell, 0.0).astype(BF16)
    loads[3].wait()
    first = jnp.concatenate([feats_ref[...], place], axis=0)
    second = jnp.concatenate([jnp.zeros((CHANNELS, length), BF16), cells], axis=0)
    out = dot_nt(on_rows(z_slot, length), first)
    out = out + dot_nt(on_rows(lax.shift_right_logical(o_slot, 1), length), second)
    out_ref[...] = out.astype(BF16).reshape(out_ref.shape)
    for load in loads[4:]:
        load.wait()


def arrived_columns(arrived):
    side = arrived[:, CHANNELS:].astype(F32)
    place = (side[:, 0:1] * 32.0 + side[:, 1:2]).astype(I32)
    return place, side[:, 2:3].astype(I32) - 1, side[:, 3:4].astype(I32) - 1


def gain_column(gain_ref):
    gain = gain_ref[...]
    eye = iota((CHANNELS, CHANNELS), 0) == iota((CHANNELS, CHANNELS), 1)
    return jnp.sum(jnp.where(eye, gain, 0.0), axis=1, keepdims=True)


def layer_norm(floats, gain):
    centred = floats - jnp.mean(floats, axis=0, keepdims=True)
    inverse_std = lax.rsqrt(jnp.mean(centred * centred, axis=0, keepdims=True) + NORM_EPS)
    normed = centred * inverse_std
    return normed, inverse_std, (gain * normed).astype(BF16)


def cluster_counts(first, second):
    return jnp.maximum(
        jnp.sum(first.astype(F32) + second.astype(F32), axis=0, keepdims=True), 1.0
    )


def head_lanes(shape, head):
    return lax.shift_right_logical(iota(shape, 1), 4) == head


def forward_kernel(
    arrived_ref,
    o_slot_ref,
    qkv_t_ref,
    out_w_ref,
    pool_t_ref,
    gain_ref,
    pool_grad_ref,
    out_ref,
    hilbert_ref,
    attended_ref,
    probs_ref,
    query_ref,
    key_ref,
    value_ref,
    rows_ref,
):
    shards = out_ref.shape[0]
    length = arrived_ref.shape[0]
    clusters = pool_grad_ref.shape[1]
    arrived = arrived_ref[...]
    place, first_cell, second_cell = arrived_columns(arrived)
    first = on_columns(first_cell, clusters)
    second = on_columns(second_cell, clusters)
    denom = cluster_counts(first, second)
    grad_mean = (dot(pool_t_ref[...], pool_grad_ref[...]) / denom).astype(BF16)
    blank = jnp.zeros_like(grad_mean)
    back = dot_nt(first, jnp.concatenate([grad_mean, blank], axis=0))
    back = back + dot_nt(second, jnp.concatenate([blank, grad_mean], axis=0))
    per_peer = length // shards
    out_ref[:, per_peer:, :] = back.astype(BF16).reshape(shards, per_peer, 2 * CHANNELS)
    turned_rows = turned(arrived)[:CHANNELS].astype(BF16)
    floats = dot(turned_rows, on_columns(place, length))
    hilbert_ref[...] = floats.astype(BF16)
    _, _, hidden = layer_norm(floats, gain_column(gain_ref))
    qkv = dot_tn(qkv_t_ref[...], hidden).astype(BF16)
    query_ref[...] = (turned(qkv[:CHANNELS]) * HEAD_DIM ** (-0.5)).astype(BF16)
    key_ref[...] = qkv[CHANNELS : 2 * CHANNELS]
    values = turned(qkv[2 * CHANNELS :])
    for head in range(HEADS):
        mask = head_lanes((length, CHANNELS), head)
        value_ref[head] = jnp.where(mask, values, 0.0).astype(BF16)

    units = [(start, head) for start in range(0, length, CHUNK) for head in range(HEADS)]

    def scores(unit):
        start, head = unit
        queries = query_ref[start : start + CHUNK, :].astype(F32)
        mask = head_lanes((CHUNK, CHANNELS), head)
        return dot(jnp.where(mask, queries, 0.0).astype(BF16), key_ref[...])

    def mix(unit):
        start, head = unit
        return dot(probs_ref[head, start : start + CHUNK, :], value_ref[head])

    totals = []
    ready = scores(units[0])
    for number, (start, head) in enumerate(units):
        now = ready
        if number + 1 < len(units):
            ready = scores(units[number + 1])
        if number > 0:
            totals.append(mix(units[number - 1]))
        weights = jnp.exp(now)
        share = 1.0 / jnp.sum(weights, axis=1, keepdims=True)
        probs_ref[head, start : start + CHUNK, :] = (weights * share).astype(BF16)
    totals.append(mix(units[-1]))
    for number in range(0, len(units), HEADS):
        start = units[number][0]
        rows_ref[start : start + CHUNK, :] = sum(totals[number : number + HEADS])
    attended = rows_ref[...].T
    attended_ref[...] = attended
    mixed = (floats + dot(out_w_ref[...], attended.astype(BF16))).astype(BF16).astype(F32)
    o_slot = o_slot_ref[...]
    odd = lax.bitwise_and(o_slot, 1) == 1
    pair = jnp.concatenate([jnp.where(odd, 0.0, mixed), jnp.where(odd, mixed, 0.0)], axis=0)
    picked = dot_nt(on_rows(lax.shift_right_logical(o_slot, 1), length), pair.astype(BF16))
    out_ref[:, :per_peer, :] = picked.astype(BF16).reshape(shards, per_peer, 2 * CHANNELS)


def backward_kernel(
    core_ref,
    returned_ref,
    arrived_ref,
    o_slot_ref,
    qkv_t_ref,
    out_w_ref,
    pool_t_ref,
    gain_ref,
    pool_grad_ref,
    hilbert_ref,
    attended_ref,
    probs_ref,
    keep_ref,
    give_ref,
    pooled_ref,
    grad_qkv_ref,
    grad_mixed_ref,
    normed_ref,
    inverse_std_ref,
    key_rows_ref,
    upstream_ref,
    value_ref,
    query_ref,
    grad_out_ref,
    grad_query_ref,
    grad_key_ref,
    grad_value_ref,
):
    shards = returned_ref.shape[0]
    length = arrived_ref.shape[0]
    clusters = pool_grad_ref.shape[1]
    per_peer = length // shards
    _, first_cell, second_cell = arrived_columns(arrived_ref[...])
    blank = jnp.zeros((CHANNELS, length), BF16)
    blank_clusters = jnp.zeros((CHANNELS, clusters), BF16)

    first = on_columns(first_cell, clusters)
    second = on_columns(second_cell, clusters)
    denom = cluster_counts(first, second)
    mixed_rows = turned(returned_ref[:, :per_peer, :].reshape(length, 2 * CHANNELS)).astype(BF16)
    sums = dot(mixed_rows[:CHANNELS], first) + dot(mixed_rows[CHANNELS:], second)
    pooled_mean = (sums / denom).astype(BF16)
    pooled_ref[...] = dot_tn(pool_t_ref[...], pooled_mean).astype(BF16)
    pool_parts = [
        dot_nt(pooled_mean, jnp.concatenate([blank_clusters, half], axis=0))
        for half in (pool_grad_ref[:CHANNELS, :], pool_grad_ref[CHANNELS:, :])
    ]

    gain = gain_column(gain_ref)
    normed, inverse_std, hidden = layer_norm(hilbert_ref[...].astype(F32), gain)
    normed_ref[...] = normed
    inverse_std_ref[...] = inverse_std
    qkv = dot_tn(qkv_t_ref[...], hidden).astype(BF16)
    query_ref[...] = qkv[:CHANNELS]
    key_rows = turned(qkv[CHANNELS : 2 * CHANNELS])
    for head in range(HEADS):
        mask = head_lanes((length, CHANNELS), head)
        key_rows_ref[head] = jnp.where(mask, key_rows, 0.0).astype(BF16)
    value_ref[:CHANNELS, :] = qkv[2 * CHANNELS :]
    value_ref[CHANNELS:, :] = jnp.ones((CHANNELS, length), BF16)

    o_slot = o_slot_ref[...]
    odd = lax.bitwise_and(o_slot, 1) == 1
    slots = turned(returned_ref[:, per_peer:, :].reshape(length, 2 * CHANNELS)).astype(BF16)
    both = dot(slots, on_rows(lax.shift_right_logical(o_slot, 1), length))
    grad_mixed = jnp.where(odd, both[CHANNELS:], both[:CHANNELS])
    grad_mixed_low = grad_mixed.astype(BF16)
    grad_mixed_ref[...] = grad_mixed_low
    attended = attended_ref[...]
    attended_low = attended.astype(BF16)
    out_part = dot_nt(grad_mixed_low, jnp.concatenate([blank, attended_low], axis=0))
    grad_attended = dot_tn(out_w_ref[...], grad_mixed_low).astype(BF16)
    grad_out_ref[...] = grad_attended
    scaled = grad_attended.astype(F32) * HEAD_DIM ** (-0.5)
    delta = -jnp.sum((scaled * attended).reshape(HEADS, HEAD_DIM, length), axis=1)
    delta_high = delta.astype(BF16).astype(F32)
    rest = jnp.concatenate(
        [delta_high, delta - delta_high, jnp.zeros((CHANNELS - 2 * HEADS, length), F32)], axis=0
    )
    upstream_ref[...] = jnp.concatenate([scaled, rest], axis=0).T.astype(BF16)
    grad_key_ref[...] = jnp.zeros_like(grad_key_ref)
    grad_value_ref[...] = jnp.zeros_like(grad_value_ref)

    units = [(start, head) for start in range(0, length, CHUNK) for head in range(HEADS)]
    lane = iota((CHUNK, 2 * CHANNELS), 1)

    def change(unit):
        start, head = unit
        mask = (
            (lax.shift_right_logical(lane, 4) == head)
            | (lane == CHANNELS + head)
            | (lane == CHANNELS + HEADS + head)
        )
        upstream = upstream_ref[start : start + CHUNK, :].astype(F32)
        return dot(jnp.where(mask, upstream, 0.0).astype(BF16), value_ref[...])

    totals = []
    ready = change(units[0])
    for number, (start, head) in enumerate(units):
        own = slice(head * HEAD_DIM, (head + 1) * HEAD_DIM)
        rows = slice(start, start + CHUNK)
        now = ready
        if number + 1 < len(units):
            ready = change(units[number + 1])
        probs = probs_ref[head, rows, :]
        grad_value_ref[own, :] += dot(grad_out_ref[own, rows], probs)
        grad_scores = (probs.astype(F32) * now).astype(BF16)
        totals.append(dot(grad_scores, key_rows_ref[head]))
        grad_key_ref[own, :] += dot(query_ref[own, rows], grad_scores)
    for number in range(0, len(units), HEADS):
        start = units[number][0]
        grad_query_ref[start : start + CHUNK, :] = sum(totals[number : number + HEADS])
    grad_qkv = jnp.concatenate(
        [grad_query_ref[...].T, grad_key_ref[...], grad_value_ref[...]], axis=0
    ).astype(BF16)
    qkv_parts = [
        dot_nt(hidden, jnp.concatenate([blank, grad_qkv[start : start + CHANNELS]], axis=0))
        for start in (0, CHANNELS, 2 * CHANNELS)
    ]
    grad_qkv_ref[...] = grad_qkv
    projections = jnp.concatenate(qkv_parts, axis=0)
    others = jnp.concatenate([out_part] + pool_parts, axis=0)
    leads = core_ref[0] == 0
    keep_ref[...] = jnp.where(leads, projections, others)
    give_ref[...] = jnp.where(leads, others, projections)


def input_grad_kernel(
    arrived_ref,
    qkv_t_ref,
    gain_ref,
    grad_qkv_ref,
    grad_mixed_ref,
    normed_ref,
    inverse_std_ref,
    out_ref,
):
    length = arrived_ref.shape[0]
    place, _, _ = arrived_columns(arrived_ref[...])
    normed = normed_ref[...]
    grad_hidden = dot(qkv_t_ref[...], grad_qkv_ref[...])
    grad_normed = grad_hidden * gain_column(gain_ref)
    grad_norm_in = inverse_std_ref[...] * (
        grad_normed
        - jnp.mean(grad_normed, axis=0, keepdims=True)
        - normed * jnp.mean(grad_normed * normed, axis=0, keepdims=True)
    )
    grad_rows = (grad_mixed_ref[...].astype(F32) + grad_norm_in).astype(BF16)
    blank = jnp.zeros((CHANNELS, length), BF16)
    back = dot_nt(on_columns(place, length), jnp.concatenate([grad_rows, blank], axis=0))
    out_ref[...] = back.astype(BF16)


def pack_kernel(back_ref, keep_ref, other_ref, out_ref):
    per_peer = out_ref.shape[1]
    parts = keep_ref[...] + other_ref[...]
    span = GROUP * per_peer
    unused = jnp.zeros((span - parts.shape[0], 2 * CHANNELS), F32)
    side = jnp.concatenate([parts, unused], axis=0)
    for start in range(0, out_ref.shape[0], GROUP):
        rows = back_ref[start * per_peer : start * per_peer + span, :].astype(F32) + side
        out_ref[start : start + GROUP] = rows.astype(BF16).reshape(GROUP, per_peer, 2 * CHANNELS)


def total_kernel(arrived_ref, out_ref):
    total = jnp.sum(arrived_ref[...].astype(F32), axis=0)
    high = total.astype(BF16).astype(F32)
    low = pltpu.roll(total - high, CHANNELS, 1)
    chosen = jnp.where(iota(total.shape, 1) >= CHANNELS, high, low)
    out_ref[...] = jnp.broadcast_to(chosen[None], out_ref.shape).astype(BF16)


def feat_grad_kernel(arrived_ref, z_slot_ref, out_ref):
    length = arrived_ref.shape[0]
    rows = turned(arrived_ref[...])[:CHANNELS].astype(BF16)
    out_ref[...] = dot(rows, on_rows(z_slot_ref[...], length)).astype(BF16)


def finish_kernel(
    factor,
    core_ref,
    own_ref,
    other_ref,
    qkv_t_ref,
    gain_in_ref,
    qkv_ref,
    out_ref,
    pool_ref,
    gain_ref,
):
    own = own_ref[...].astype(F32)
    other = other_ref[...].astype(F32)
    own = (own[:, CHANNELS:] + own[:, :CHANNELS]) * factor
    other = (other[:, CHANNELS:] + other[:, :CHANNELS]) * factor
    leads = core_ref[0] == 0
    first = jnp.where(leads, own, other)
    second = jnp.where(leads, other, own)
    both = (first, second)
    piece = [one[k * CHANNELS : (k + 1) * CHANNELS] for one in both for k in range(3)]
    qkv = jnp.concatenate(piece[:3], axis=1)
    qkv_ref[...] = qkv
    out_ref[...] = piece[3]
    pool_ref[...] = jnp.concatenate(piece[4:], axis=1)
    column = jnp.sum(qkv * qkv_t_ref[...].astype(F32), axis=1, keepdims=True)
    eye = iota((CHANNELS, CHANNELS), 0) == iota((CHANNELS, CHANNELS), 1)
    gain_ref[...] = jnp.sum(jnp.where(eye, column, 0.0), axis=0, keepdims=True) / gain_in_ref[...]


def shape(dims, dtype):
    return jax.ShapeDtypeStruct(dims, dtype)


def call(kernel, outs, scratch=(), flops=0, **more):
    return pl.pallas_call(
        kernel,
        out_shape=outs,
        **more,
        scratch_shapes=list(scratch),
        compiler_params=pltpu.CompilerParams(vmem_limit_bytes=28 * 1024 * 1024),
        cost_estimate=pl.CostEstimate(flops=flops, bytes_accessed=1 << 20, transcendentals=0),
    )


def exchange(blocks, size):
    order = [layer * PLANE + place for place in range(PLANE) for layer in range(LAYERS)]
    return lax.all_to_all(
        blocks,
        "pts",
        split_axis=0,
        concat_axis=0,
        tiled=True,
        axis_index_groups=[order[start : start + size] for start in range(0, len(order), size)],
    )


def body(
    feats,
    hilbert_of_z,
    pool_owner,
    pool_slot,
    qkv_weight,
    out_weight,
    pool_weight,
    norm_gain,
    pooled_grad,
):
    length = feats.shape[2]
    shards = lax.axis_size("pts")
    per_peer = length // shards
    clusters = pooled_grad.shape[2]
    lanes = 2 * CHANNELS
    qkv_t = qkv_weight.T
    pool_t = pool_weight.T
    gain = norm_gain.reshape(1, CHANNELS)
    upstream_pool = pooled_grad[0]

    arguments = tuple(
        pltpu.with_memory_space_constraint(one, pltpu.HBM)
        for one in (
        hilbert_of_z,
        pool_owner.reshape(1, length),
        pool_slot,
        feats[0],
        upstream_pool,
        qkv_t,
        out_weight,
        pool_t,
        gain,
        )
    )
    outgoing, z_slot, o_slot, upstream_pool, qkv_t, out_weight, pool_t, gain = call(
        send_kernel,
        (
            shape((shards, per_peer, lanes), BF16),
            shape((1, length), I32),
            shape((1, length), I32),
        )
        + tuple(shape(one.shape, one.dtype) for one in arguments[4:]),
        scratch=tuple(pltpu.VMEM(one.shape, one.dtype) for one in arguments[:4])
        + (pltpu.SemaphoreType.DMA((len(arguments),)),),
        flops=1 << 30,
        in_specs=[pl.BlockSpec(memory_space=pltpu.HBM)] * len(arguments),
    )(*arguments)
    arrived = exchange(outgoing, shards).reshape(length, lanes)

    both_ways, hilbert_rows, attended, probs = call(
        forward_kernel,
        (
            shape((shards, 2 * per_peer, lanes), BF16),
            shape((CHANNELS, length), BF16),
            shape((CHANNELS, length), F32),
            shape((HEADS, length, length), BF16),
        ),
        scratch=(
            pltpu.VMEM((length, CHANNELS), BF16),
            pltpu.VMEM((CHANNELS, length), BF16),
            pltpu.VMEM((HEADS, length, CHANNELS), BF16),
            pltpu.VMEM((length, CHANNELS), F32),
        ),
        flops=1 << 32,
    )(arrived, o_slot, qkv_t, out_weight, pool_t, gain, upstream_pool)
    returned = exchange(both_ways, shards)

    core = lax.axis_index("rep").astype(I32).reshape(1)
    scalar = pl.BlockSpec(memory_space=pltpu.SMEM)
    block = pl.BlockSpec(memory_space=pltpu.VMEM)
    swap = [(0, 1), (1, 0)]

    keep, give, pooled, grad_qkv, grad_mixed, normed, inverse_std = call(
        backward_kernel,
        (
            shape((3 * CHANNELS, lanes), F32),
            shape((3 * CHANNELS, lanes), F32),
            shape((2 * CHANNELS, clusters), BF16),
            shape((3 * CHANNELS, length), BF16),
            shape((CHANNELS, length), BF16),
            shape((CHANNELS, length), F32),
            shape((1, length), F32),
        ),
        scratch=(
            pltpu.VMEM((HEADS, length, CHANNELS), BF16),
            pltpu.VMEM((length, lanes), BF16),
            pltpu.VMEM((lanes, length), BF16),
            pltpu.VMEM((CHANNELS, length), BF16),
            pltpu.VMEM((CHANNELS, length), BF16),
            pltpu.VMEM((length, CHANNELS), F32),
            pltpu.VMEM((CHANNELS, length), F32),
            pltpu.VMEM((CHANNELS, length), F32),
        ),
        flops=1 << 33,
        in_specs=[scalar] + [block] * 11,
    )(
        core,
        returned,
        arrived,
        o_slot,
        qkv_t,
        out_weight,
        pool_t,
        gain,
        upstream_pool,
        hilbert_rows,
        attended,
        probs,
    )
    taken = lax.ppermute(give, "rep", swap)
    back = call(input_grad_kernel, shape((length, lanes), BF16), flops=1 << 31)(
        arrived, qkv_t, gain, grad_qkv, grad_mixed, normed, inverse_std
    )
    last = call(pack_kernel, shape((shards, per_peer, lanes), BF16))(back, keep, taken)
    final = exchange(last, shards)

    total = call(total_kernel, shape((GROUP, per_peer, lanes), BF16))(final)
    gathered = exchange(total, GROUP).reshape(GROUP * per_peer, lanes)
    other = lax.ppermute(gathered, "rep", swap)
    feat_grad = call(feat_grad_kernel, shape((CHANNELS, length), BF16), flops=1 << 28)(
        final.reshape(length, lanes), z_slot
    )
    factor = float(lax.axis_size("rep") * shards * length) ** (-0.5)
    qkv_total, out_total, pool_total, gain_total = call(
        functools.partial(finish_kernel, factor),
        (
            shape((CHANNELS, 3 * CHANNELS), F32),
            shape((CHANNELS, CHANNELS), F32),
            shape((CHANNELS, lanes), F32),
            shape((1, CHANNELS), F32),
        ),
        in_specs=[scalar] + [block] * 4,
    )(core, gathered, other, qkv_t, gain)
    return (
        pooled[None],
        feat_grad[None],
        qkv_total.T,
        out_total,
        pool_total.T,
        gain_total.reshape(CHANNELS),
    )


def solution(mesh):
    return jax.shard_map(
        body,
        mesh=mesh,
        in_specs=(
            P("rep", None, "pts"),
            P("rep", "pts"),
            P("rep", "pts", None),
            P("rep", "pts"),
            P(),
            P(),
            P(),
            P(),
            P("rep", None, "pts"),
        ),
        out_specs=(P("rep", None, "pts"), P("rep", None, "pts"), P(), P(), P(), P()),
        check_vma=False,
    )
```

```python
import functools

import jax
import jax.numpy as jnp
from jax import lax
from jax.experimental import pallas as pl
from jax.experimental.pallas import tpu as pltpu
from jax.sharding import PartitionSpec as P

HEADS = 4
HEAD_DIM = 16
CHANNELS = 64
NORM_EPS = 1e-05
CHUNK = 256
GROUP = 64

F32 = jnp.float32
BF16 = jnp.bfloat16
I32 = jnp.int32


def dot(a, b):
    return lax.dot_general(a, b, (((1,), (0,)), ((), ())), preferred_element_type=F32)


def dot_nt(a, b):
    return lax.dot_general(a, b, (((1,), (1,)), ((), ())), preferred_element_type=F32)


def dot_tn(a, b):
    return lax.dot_general(a, b, (((0,), (0,)), ((), ())), preferred_element_type=F32)


def turned(a):
    return a.astype(F32).T


def iota(shape, dim):
    return lax.broadcasted_iota(I32, shape, dim)


def onehot(mask):
    return jnp.where(mask, 1.0, 0.0).astype(BF16)


def on_rows(row, count):
    return onehot(iota((count, row.shape[1]), 0) == row)


def on_columns(column, count):
    return onehot(iota((column.shape[0], count), 1) == column)


def rank_in_group(groups, count):
    length = groups.shape[1]
    member = on_rows(groups, count)
    upto = onehot(iota((128, 128), 0) <= iota((128, 128), 1))
    seen = jnp.zeros((count, 1), F32)
    ranks = []
    for start in range(0, length, 128):
        block = member[:, start : start + 128]
        running = dot(block, upto) + seen
        seen = running[:, 127:128]
        ranks.append(jnp.sum(block.astype(F32) * running, axis=0, keepdims=True) - 1.0)
    return jnp.concatenate(ranks, axis=1).astype(I32)


def send_kernel(
    pos_hbm,
    owner_hbm,
    cell_hbm,
    feats_hbm,
    pool_grad_hbm,
    qkv_t_hbm,
    out_w_hbm,
    pool_t_hbm,
    gain_hbm,
    out_ref,
    z_slot_ref,
    o_slot_ref,
    pool_grad_ref,
    qkv_t_ref,
    out_w_ref,
    pool_t_ref,
    gain_ref,
    pos_ref,
    owner_ref,
    cell_ref,
    feats_ref,
    sems,
):
    loads = [
        pltpu.make_async_copy(source, target, sems.at[number])
        for number, (source, target) in enumerate(
            (
                (pos_hbm, pos_ref),
                (owner_hbm, owner_ref),
                (cell_hbm, cell_ref),
                (feats_hbm, feats_ref),
                (pool_grad_hbm, pool_grad_ref),
                (qkv_t_hbm, qkv_t_ref),
                (out_w_hbm, out_w_ref),
                (pool_t_hbm, pool_t_ref),
                (gain_hbm, gain_ref),
            )
        )
    ]
    for load in loads:
        load.start()
    for load in loads[:3]:
        load.wait()
    length = pos_ref.shape[1]
    shards = out_ref.shape[0]
    per_peer = length // shards
    positions = pos_ref[...]
    owners = owner_ref[...]
    shift = length.bit_length() - 1
    target = lax.shift_right_logical(positions, shift)
    local = lax.bitwise_and(positions, length - 1)
    z_slot = target * per_peer + rank_in_group(target, shards)
    o_slot = owners * (2 * per_peer) + rank_in_group(owners, shards)
    z_slot_ref[...] = z_slot
    o_slot_ref[...] = o_slot
    row = iota((CHANNELS, length), 0)
    high = lax.shift_right_logical(local, 5).astype(F32)
    low = lax.bitwise_and(local, 31).astype(F32)
    place = jnp.where(row == 0, high, jnp.where(row == 1, low, 0.0)).astype(BF16)
    cell = (cell_ref[...] + 1).astype(F32)
    odd = lax.bitwise_and(o_slot, 1)
    cells = jnp.where(row - 2 == odd, cell, 0.0).astype(BF16)
    loads[3].wait()
    first = jnp.concatenate([feats_ref[...], place], axis=0)
    second = jnp.concatenate([jnp.zeros((CHANNELS, length), BF16), cells], axis=0)
    out = dot_nt(on_rows(z_slot, length), first)
    out = out + dot_nt(on_rows(lax.shift_right_logical(o_slot, 1), length), second)
    out_ref[...] = out.astype(BF16).reshape(out_ref.shape)
    for load in loads[4:]:
        load.wait()


def arrived_columns(arrived):
    side = arrived[:, CHANNELS:].astype(F32)
    place = (side[:, 0:1] * 32.0 + side[:, 1:2]).astype(I32)
    return place, side[:, 2:3].astype(I32) - 1, side[:, 3:4].astype(I32) - 1


def gain_column(gain_ref):
    gain = gain_ref[...]
    eye = iota((CHANNELS, CHANNELS), 0) == iota((CHANNELS, CHANNELS), 1)
    return jnp.sum(jnp.where(eye, gain, 0.0), axis=1, keepdims=True)


def layer_norm(floats, gain):
    centred = floats - jnp.mean(floats, axis=0, keepdims=True)
    inverse_std = lax.rsqrt(jnp.mean(centred * centred, axis=0, keepdims=True) + NORM_EPS)
    normed = centred * inverse_std
    return normed, inverse_std, (gain * normed).astype(BF16)


def cluster_counts(first, second):
    return jnp.maximum(
        jnp.sum(first.astype(F32) + second.astype(F32), axis=0, keepdims=True), 1.0
    )


def head_lanes(shape, head):
    return lax.shift_right_logical(iota(shape, 1), 4) == head


def forward_kernel(
    arrived_ref,
    o_slot_ref,
    qkv_t_ref,
    out_w_ref,
    pool_t_ref,
    gain_ref,
    pool_grad_ref,
    out_ref,
    attended_ref,
    probs_ref,
    slot_map_ref,
    hidden_ref,
    normed_ref,
    inverse_std_ref,
    query_ref,
    key_ref,
    value_ref,
    query_rows_ref,
):
    shards = out_ref.shape[0]
    length = arrived_ref.shape[0]
    clusters = pool_grad_ref.shape[1]
    per_peer = length // shards
    arrived = arrived_ref[...]
    place, first_cell, second_cell = arrived_columns(arrived)
    turned_rows = turned(arrived)[:CHANNELS].astype(BF16)
    floats = dot(turned_rows, on_columns(place, length))
    normed, inverse_std, hidden = layer_norm(floats, gain_column(gain_ref))
    qkv = dot_tn(qkv_t_ref[...], hidden).astype(BF16)
    query_rows_ref[...] = (turned(qkv[:CHANNELS]) * HEAD_DIM ** (-0.5)).astype(BF16)
    key_ref[...] = qkv[CHANNELS : 2 * CHANNELS]
    value_ref[:CHANNELS, :] = qkv[2 * CHANNELS :]
    value_ref[CHANNELS:, :] = jnp.ones((CHANNELS, length), BF16)
    half_slot = lax.shift_right_logical(o_slot_ref[...], 1)
    kept = {}

    def cluster_grads():
        first = on_columns(first_cell, clusters)
        second = on_columns(second_cell, clusters)
        denom = cluster_counts(first, second)
        grad_mean = (dot(pool_t_ref[...], pool_grad_ref[...]) / denom).astype(BF16)
        blank = jnp.zeros_like(grad_mean)
        kept["cells"] = (first, second)
        kept["means"] = (
            jnp.concatenate([grad_mean, blank], axis=0),
            jnp.concatenate([blank, grad_mean], axis=0),
        )

    def send_back(start, count):
        first, second = (one[start : start + count] for one in kept["cells"])
        back = dot_nt(first, kept["means"][0]) + dot_nt(second, kept["means"][1])
        peers = slice(start // per_peer, (start + count) // per_peer)
        out_ref[peers, per_peer:, :] = back.astype(BF16).reshape(-1, per_peer, 2 * CHANNELS)

    def map_slots(start, count):
        rows = iota((count, length), 0) + start
        slot_map_ref[start : start + count, :] = onehot(rows == half_slot)

    def hand_over():
        hidden_ref[...] = hidden
        normed_ref[...] = normed
        inverse_std_ref[...] = inverse_std
        query_ref[...] = qkv[:CHANNELS]

    chores = [hand_over, cluster_grads]
    quarter = length // 4
    chores += [functools.partial(send_back, k * quarter, quarter) for k in range(4)]
    eighth = length // 8
    chores += [functools.partial(map_slots, k * eighth, eighth) for k in range(8)]

    units = [(start, head) for start in range(0, length, CHUNK) for head in range(HEADS)]

    def scores(unit):
        start, head = unit
        queries = query_rows_ref[start : start + CHUNK, :].astype(F32)
        mask = head_lanes((CHUNK, CHANNELS), head)
        return dot(jnp.where(mask, queries, 0.0).astype(BF16), key_ref[...])

    def mix(unit):
        start, head = unit
        own = slice(head * HEAD_DIM, (head + 1) * HEAD_DIM)
        return dot_nt(value_ref[own, :], probs_ref[head, start : start + CHUNK, :])

    totals = []
    ready = scores(units[0])
    for number, (start, head) in enumerate(units):
        now = ready
        if number + 1 < len(units):
            ready = scores(units[number + 1])
        if number > 0:
            totals.append(mix(units[number - 1]))
        if number < len(chores):
            chores[number]()
        weights = jnp.exp(now)
        share = 1.0 / jnp.sum(weights, axis=1, keepdims=True)
        probs_ref[head, start : start + CHUNK, :] = (weights * share).astype(BF16)
    totals.append(mix(units[-1]))
    for number in range(0, len(units), HEADS):
        start = units[number][0]
        attended_ref[:, start : start + CHUNK] = jnp.concatenate(
            totals[number : number + HEADS], axis=0
        )
    attended = attended_ref[...]
    mixed = (floats + dot(out_w_ref[...], attended.astype(BF16))).astype(BF16).astype(F32)
    odd = lax.bitwise_and(o_slot_ref[...], 1) == 1
    pair = jnp.concatenate([jnp.where(odd, 0.0, mixed), jnp.where(odd, mixed, 0.0)], axis=0)
    picked = dot_nt(slot_map_ref[...], pair.astype(BF16))
    out_ref[:, :per_peer, :] = picked.astype(BF16).reshape(shards, per_peer, 2 * CHANNELS)


def backward_kernel(
    returned_ref,
    arrived_ref,
    o_slot_ref,
    qkv_t_ref,
    out_w_ref,
    pool_t_ref,
    gain_ref,
    pool_grad_ref,
    attended_ref,
    probs_ref,
    slot_map_ref,
    hidden_ref,
    normed_ref,
    inverse_std_ref,
    query_ref,
    key_ref,
    value_ref,
    out_ref,
    pooled_ref,
    upstream_ref,
    grad_out_ref,
    grad_query_ref,
    grad_key_ref,
    grad_value_ref,
    place_ref,
):
    shards = out_ref.shape[0]
    length = arrived_ref.shape[0]
    clusters = pool_grad_ref.shape[1]
    per_peer = length // shards
    blank = jnp.zeros((CHANNELS, length), BF16)
    odd = lax.bitwise_and(o_slot_ref[...], 1) == 1
    slots = turned(returned_ref[:, per_peer:, :].reshape(length, 2 * CHANNELS)).astype(BF16)
    both = dot(slots, slot_map_ref[...])
    grad_mixed = jnp.where(odd, both[CHANNELS:], both[:CHANNELS])
    grad_mixed_low = grad_mixed.astype(BF16)
    attended = attended_ref[...]
    grad_attended = dot_tn(out_w_ref[...], grad_mixed_low).astype(BF16)
    grad_out_ref[...] = grad_attended
    scaled = grad_attended.astype(F32) * HEAD_DIM ** (-0.5)
    delta = -jnp.sum((scaled * attended).reshape(HEADS, HEAD_DIM, length), axis=1)
    delta_high = delta.astype(BF16).astype(F32)
    rest = jnp.concatenate(
        [delta_high, delta - delta_high, jnp.zeros((CHANNELS - 2 * HEADS, length), F32)], axis=0
    )
    upstream_ref[...] = jnp.concatenate([scaled, rest], axis=0).T.astype(BF16)
    place, first_cell, second_cell = arrived_columns(arrived_ref[...])
    kept = {}

    def cells():
        kept["cells"] = (on_columns(first_cell, clusters), on_columns(second_cell, clusters))
        kept["denom"] = cluster_counts(*kept["cells"])

    def pool():
        rows = turned(returned_ref[:, :per_peer, :].reshape(length, 2 * CHANNELS)).astype(BF16)
        first, second = kept["cells"]
        sums = dot(rows[:CHANNELS], first) + dot(rows[CHANNELS:], second)
        kept["mean"] = (sums / kept["denom"]).astype(BF16)

    def pool_out():
        pooled_ref[...] = dot_tn(pool_t_ref[...], kept["mean"]).astype(BF16)
        empty = jnp.zeros((CHANNELS, clusters), BF16)
        kept["pool"] = [
            dot_nt(kept["mean"], jnp.concatenate([empty, half], axis=0))
            for half in (pool_grad_ref[:CHANNELS, :], pool_grad_ref[CHANNELS:, :])
        ]

    def out_grad():
        attended_low = attended.astype(BF16)
        kept["out"] = dot_nt(grad_mixed_low, jnp.concatenate([blank, attended_low], axis=0))

    def map_places(start, count):
        place_ref[start : start + count, :] = on_columns(place[start : start + count], length)

    chores = [cells, pool, pool_out, out_grad]
    eighth = length // 8
    chores += [functools.partial(map_places, k * eighth, eighth) for k in range(8)]

    units = [(start, head) for start in range(0, length, CHUNK) for head in range(HEADS)]
    lane = iota((CHUNK, 2 * CHANNELS), 1)

    def change(unit):
        start, head = unit
        mask = (
            (lax.shift_right_logical(lane, 4) == head)
            | (lane == CHANNELS + head)
            | (lane == CHANNELS + HEADS + head)
        )
        upstream = upstream_ref[start : start + CHUNK, :].astype(F32)
        return dot(jnp.where(mask, upstream, 0.0).astype(BF16), value_ref[...])

    totals = []
    ready = change(units[0])
    for number, (start, head) in enumerate(units):
        own = slice(head * HEAD_DIM, (head + 1) * HEAD_DIM)
        rows = slice(start, start + CHUNK)
        now = ready
        if number + 1 < len(units):
            ready = change(units[number + 1])
        if number < len(chores):
            chores[number]()
        probs = probs_ref[head, rows, :]
        more_values = dot(grad_out_ref[own, rows], probs)
        grad_scores = (probs.astype(F32) * now).astype(BF16)
        totals.append(dot_nt(key_ref[own, :], grad_scores))
        more_keys = dot(query_ref[own, rows], grad_scores)
        if start == 0:
            grad_value_ref[own, :] = more_values
            grad_key_ref[own, :] = more_keys
        else:
            grad_value_ref[own, :] += more_values
            grad_key_ref[own, :] += more_keys
    for number in range(0, len(units), HEADS):
        start = units[number][0]
        grad_query_ref[:, start : start + CHUNK] = jnp.concatenate(
            totals[number : number + HEADS], axis=0
        )
    grad_qkv = jnp.concatenate(
        [grad_query_ref[...], grad_key_ref[...], grad_value_ref[...]], axis=0
    ).astype(BF16)
    grad_hidden = dot(qkv_t_ref[...], grad_qkv)
    hidden = hidden_ref[...]
    normed = normed_ref[...]
    qkv_parts = [
        dot_nt(hidden, jnp.concatenate([blank, grad_qkv[start : start + CHANNELS]], axis=0))
        for start in (0, CHANNELS, 2 * CHANNELS)
    ]
    grad_normed = grad_hidden * gain_column(gain_ref)
    grad_norm_in = inverse_std_ref[...] * (
        grad_normed
        - jnp.mean(grad_normed, axis=0, keepdims=True)
        - normed * jnp.mean(grad_normed * normed, axis=0, keepdims=True)
    )
    grad_rows = (grad_mixed + grad_norm_in).astype(BF16)
    back = dot_nt(place_ref[...], jnp.concatenate([grad_rows, blank], axis=0))
    parts = qkv_parts + [kept["out"]] + kept["pool"]
    unused = jnp.zeros((GROUP * per_peer - len(parts) * CHANNELS, 2 * CHANNELS), F32)
    side = jnp.concatenate(parts + [unused], axis=0)
    span = GROUP * per_peer
    for start in range(0, shards, GROUP):
        rows = back[start * per_peer : start * per_peer + span] + side
        out_ref[start : start + GROUP] = rows.astype(BF16).reshape(GROUP, per_peer, 2 * CHANNELS)


def total_kernel(arrived_ref, out_ref):
    out_ref[...] = jnp.sum(arrived_ref[...].astype(F32), axis=0)


def spread_kernel(own_ref, other_ref, out_ref):
    total = own_ref[...] + other_ref[...]
    high = total.astype(BF16).astype(F32)
    low = pltpu.roll(total - high, CHANNELS, 1)
    chosen = jnp.where(iota(total.shape, 1) >= CHANNELS, high, low)
    out_ref[...] = jnp.broadcast_to(chosen[None], out_ref.shape).astype(BF16)


def feat_grad_kernel(arrived_ref, z_slot_ref, out_ref):
    length = arrived_ref.shape[0]
    rows = turned(arrived_ref[...])[:CHANNELS].astype(BF16)
    out_ref[...] = dot(rows, on_rows(z_slot_ref[...], length)).astype(BF16)


def finish_kernel(
    factor,
    total_ref,
    qkv_t_ref,
    gain_in_ref,
    qkv_ref,
    out_ref,
    pool_ref,
    gain_ref,
):
    both = total_ref[...].astype(F32)
    both = (both[:, CHANNELS:] + both[:, :CHANNELS]) * factor
    piece = [both[k * CHANNELS : (k + 1) * CHANNELS] for k in range(6)]
    qkv = jnp.concatenate(piece[:3], axis=1)
    qkv_ref[...] = qkv
    out_ref[...] = piece[3]
    pool_ref[...] = jnp.concatenate(piece[4:], axis=1)
    column = jnp.sum(qkv * qkv_t_ref[...].astype(F32), axis=1, keepdims=True)
    eye = iota((CHANNELS, CHANNELS), 0) == iota((CHANNELS, CHANNELS), 1)
    gain_ref[...] = jnp.sum(jnp.where(eye, column, 0.0), axis=0, keepdims=True) / gain_in_ref[...]


def shape(dims, dtype):
    return jax.ShapeDtypeStruct(dims, dtype)


def call(kernel, outs, scratch=(), flops=0, **more):
    return pl.pallas_call(
        kernel,
        out_shape=outs,
        **more,
        scratch_shapes=list(scratch),
        compiler_params=pltpu.CompilerParams(vmem_limit_bytes=28 * 1024 * 1024),
        cost_estimate=pl.CostEstimate(flops=flops, bytes_accessed=1 << 20, transcendentals=0),
    )


def exchange(blocks):
    return lax.all_to_all(blocks, "pts", split_axis=0, concat_axis=0, tiled=True)


def body(
    feats,
    hilbert_of_z,
    pool_owner,
    pool_slot,
    qkv_weight,
    out_weight,
    pool_weight,
    norm_gain,
    pooled_grad,
):
    length = feats.shape[2]
    shards = lax.axis_size("pts")
    per_peer = length // shards
    clusters = pooled_grad.shape[2]
    lanes = 2 * CHANNELS
    qkv_t = qkv_weight.T
    pool_t = pool_weight.T
    gain = norm_gain.reshape(1, CHANNELS)
    upstream_pool = pooled_grad[0]

    arguments = tuple(
        pltpu.with_memory_space_constraint(one, pltpu.HBM)
        for one in (
        hilbert_of_z,
        pool_owner.reshape(1, length),
        pool_slot,
        feats[0],
        upstream_pool,
        qkv_t,
        out_weight,
        pool_t,
        gain,
        )
    )
    outgoing, z_slot, o_slot, upstream_pool, qkv_t, out_weight, pool_t, gain = call(
        send_kernel,
        (
            shape((shards, per_peer, lanes), BF16),
            shape((1, length), I32),
            shape((1, length), I32),
        )
        + tuple(shape(one.shape, one.dtype) for one in arguments[4:]),
        scratch=tuple(pltpu.VMEM(one.shape, one.dtype) for one in arguments[:4])
        + (pltpu.SemaphoreType.DMA((len(arguments),)),),
        flops=1 << 30,
        in_specs=[pl.BlockSpec(memory_space=pltpu.HBM)] * len(arguments),
    )(*arguments)
    arrived = exchange(outgoing).reshape(length, lanes)

    both_ways, *saved = call(
        forward_kernel,
        (
            shape((shards, 2 * per_peer, lanes), BF16),
            shape((CHANNELS, length), F32),
            shape((HEADS, length, length), BF16),
            shape((length, length), BF16),
            shape((CHANNELS, length), BF16),
            shape((CHANNELS, length), F32),
            shape((1, length), F32),
            shape((CHANNELS, length), BF16),
            shape((CHANNELS, length), BF16),
            shape((lanes, length), BF16),
        ),
        scratch=(pltpu.VMEM((length, CHANNELS), BF16),),
        flops=1 << 32,
    )(arrived, o_slot, qkv_t, out_weight, pool_t, gain, upstream_pool)
    returned = exchange(both_ways)

    last, pooled = call(
        backward_kernel,
        (shape((shards, per_peer, lanes), BF16), shape((2 * CHANNELS, clusters), BF16)),
        scratch=(
            pltpu.VMEM((length, lanes), BF16),
            pltpu.VMEM((CHANNELS, length), BF16),
            pltpu.VMEM((CHANNELS, length), F32),
            pltpu.VMEM((CHANNELS, length), F32),
            pltpu.VMEM((CHANNELS, length), F32),
            pltpu.VMEM((length, length), BF16),
        ),
        flops=1 << 33,
    )(
        returned,
        arrived,
        o_slot,
        qkv_t,
        out_weight,
        pool_t,
        gain,
        upstream_pool,
        *saved,
    )
    final = exchange(last)

    own = call(total_kernel, shape((per_peer, lanes), F32))(final)
    other = lax.ppermute(own, "rep", [(0, 1), (1, 0)])
    feat_grad = call(feat_grad_kernel, shape((CHANNELS, length), BF16), flops=1 << 30)(
        final.reshape(length, lanes), z_slot
    )
    other, feat_grad = lax.optimization_barrier((other, feat_grad))
    total = call(spread_kernel, shape((GROUP, per_peer, lanes), BF16))(own, other)
    gathered = lax.all_to_all(
        total,
        "pts",
        split_axis=0,
        concat_axis=0,
        tiled=True,
        axis_index_groups=[
            list(range(start, start + GROUP)) for start in range(0, shards, GROUP)
        ],
    ).reshape(GROUP * per_peer, lanes)
    factor = float(lax.axis_size("rep") * shards * length) ** (-0.5)
    qkv_total, out_total, pool_total, gain_total = call(
        functools.partial(finish_kernel, factor),
        (
            shape((CHANNELS, 3 * CHANNELS), F32),
            shape((CHANNELS, CHANNELS), F32),
            shape((CHANNELS, lanes), F32),
            shape((1, CHANNELS), F32),
        ),
    )(gathered, qkv_t, gain)
    return (
        pooled[None],
        feat_grad[None],
        qkv_total.T,
        out_total,
        pool_total.T,
        gain_total.reshape(CHANNELS),
    )


def solution(mesh):
    return jax.shard_map(
        body,
        mesh=mesh,
        in_specs=(
            P("rep", None, "pts"),
            P("rep", "pts"),
            P("rep", "pts", None),
            P("rep", "pts"),
            P(),
            P(),
            P(),
            P(),
            P("rep", None, "pts"),
        ),
        out_specs=(P("rep", None, "pts"), P("rep", None, "pts"), P(), P(), P(), P()),
        check_vma=False,
    )
```

```python
import functools

import jax
import jax.numpy as jnp
from jax import lax
from jax.experimental import pallas as pl
from jax.experimental.pallas import tpu as pltpu
from jax.sharding import PartitionSpec as P

HEADS = 4
HEAD_DIM = 16
CHANNELS = 64
NORM_EPS = 1e-05
CHUNK = 256
AHEAD = 1
LAG = 2
LATE = 0
GROUP = 64

F32 = jnp.float32
BF16 = jnp.bfloat16
I32 = jnp.int32


def dot(a, b):
    return lax.dot_general(a, b, (((1,), (0,)), ((), ())), preferred_element_type=F32)


def dot_nt(a, b):
    return lax.dot_general(a, b, (((1,), (1,)), ((), ())), preferred_element_type=F32)


def dot_tn(a, b):
    return lax.dot_general(a, b, (((0,), (0,)), ((), ())), preferred_element_type=F32)


def turned(a):
    return a.astype(F32).T


def iota(shape, dim):
    return lax.broadcasted_iota(I32, shape, dim)


def onehot(mask):
    return jnp.where(mask, 1.0, 0.0).astype(BF16)


def on_rows(row, count):
    return onehot(iota((count, row.shape[1]), 0) == row)


def on_columns(column, count):
    return onehot(iota((column.shape[0], count), 1) == column)


def rank_in_group(groups, count):
    length = groups.shape[1]
    member = on_rows(groups, count)
    upto = onehot(iota((128, 128), 0) <= iota((128, 128), 1))
    entry, block = iota((length, 128), 0), iota((length, 128), 1)
    seen = dot(member, onehot(lax.shift_right_logical(entry, 7) < block))
    ranks = []
    for number in range(length // 128):
        part = member[:, number * 128 : (number + 1) * 128]
        running = dot(part, upto) + seen[:, number : number + 1]
        ranks.append(jnp.sum(part.astype(F32) * running, axis=0, keepdims=True) - 1.0)
    return jnp.concatenate(ranks, axis=1).astype(I32), member


def send_kernel(
    pos_hbm,
    owner_hbm,
    cell_hbm,
    feats_hbm,
    pool_grad_hbm,
    qkv_t_hbm,
    out_w_hbm,
    pool_t_hbm,
    gain_hbm,
    out_ref,
    z_slot_ref,
    o_slot_ref,
    pool_grad_ref,
    qkv_t_ref,
    out_w_ref,
    pool_t_ref,
    gain_ref,
    pos_ref,
    owner_ref,
    cell_ref,
    feats_ref,
    sems,
):
    loads = [
        pltpu.make_async_copy(source, target, sems.at[number])
        for number, (source, target) in enumerate(
            (
                (pos_hbm, pos_ref),
                (owner_hbm, owner_ref),
                (cell_hbm, cell_ref),
                (feats_hbm, feats_ref),
                (pool_grad_hbm, pool_grad_ref),
                (qkv_t_hbm, qkv_t_ref),
                (out_w_hbm, out_w_ref),
                (pool_t_hbm, pool_t_ref),
                (gain_hbm, gain_ref),
            )
        )
    ]
    for load in loads:
        load.start()
    for load in loads[:3]:
        load.wait()
    length = pos_ref.shape[1]
    shards = out_ref.shape[0]
    per_peer = length // shards
    positions = pos_ref[...]
    owners = owner_ref[...]
    shift = length.bit_length() - 1
    target = lax.shift_right_logical(positions, shift)
    local = lax.bitwise_and(positions, length - 1)
    z_rank, _ = rank_in_group(target, shards)
    o_rank, owned = rank_in_group(owners, shards)
    z_slot = target * per_peer + z_rank
    o_slot = owners * (2 * per_peer) + o_rank
    z_slot_ref[...] = z_slot
    o_slot_ref[...] = o_slot
    row = iota((CHANNELS, length), 0)
    high = lax.shift_right_logical(local, 5).astype(F32)
    low = lax.bitwise_and(local, 31).astype(F32)
    place = jnp.where(row == 0, high, jnp.where(row == 1, low, 0.0)).astype(BF16)
    cell = (cell_ref[...] + 1).astype(F32)
    rank = iota((2 * per_peer, length), 0)
    cells = dot_nt(owned, jnp.where(rank == o_rank, cell, 0.0).astype(BF16)).astype(BF16)
    peer = lax.shift_right_logical(iota((length, shards), 0), per_peer.bit_length() - 1)
    listed = dot(onehot(peer == iota((length, shards), 1)), cells)
    row = iota(listed.shape, 0)
    place_in_list = iota(listed.shape, 1)
    mine = lax.shift_right_logical(place_in_list, 1) == lax.bitwise_and(row, per_peer - 1)
    listed = jnp.where(mine, listed, 0.0).astype(BF16)
    lane = iota((2 * per_peer, 2 * CHANNELS), 1)
    parity = lax.bitwise_and(iota((2 * per_peer, 2 * CHANNELS), 0), 1)
    out = dot(listed, onehot(lane == parity + CHANNELS + 2))
    loads[3].wait()
    first = jnp.concatenate([feats_ref[...], place], axis=0)
    out = out + dot_nt(on_rows(z_slot, length), first)
    out_ref[...] = out.astype(BF16).reshape(out_ref.shape)
    for load in loads[4:]:
        load.wait()


def arrived_columns(arrived):
    side = arrived[:, CHANNELS:].astype(F32)
    place = (side[:, 0:1] * 32.0 + side[:, 1:2]).astype(I32)
    return place, side[:, 2:3].astype(I32) - 1, side[:, 3:4].astype(I32) - 1


def gain_column(gain_ref):
    gain = gain_ref[...]
    eye = iota((CHANNELS, CHANNELS), 0) == iota((CHANNELS, CHANNELS), 1)
    return jnp.sum(jnp.where(eye, gain, 0.0), axis=1, keepdims=True)


def layer_norm(floats, gain):
    centred = floats - jnp.mean(floats, axis=0, keepdims=True)
    inverse_std = lax.rsqrt(jnp.mean(centred * centred, axis=0, keepdims=True) + NORM_EPS)
    normed = centred * inverse_std
    return normed, inverse_std, (gain * normed).astype(BF16)


def cluster_counts(first, second):
    return jnp.maximum(
        jnp.sum(first.astype(F32) + second.astype(F32), axis=0, keepdims=True), 1.0
    )


def forward_kernel(
    arrived_ref,
    o_slot_ref,
    qkv_t_ref,
    out_w_ref,
    pool_t_ref,
    gain_ref,
    pool_grad_ref,
    out_ref,
    attended_ref,
    probs_ref,
    slot_map_ref,
    hidden_ref,
    normed_ref,
    inverse_std_ref,
    query_ref,
    key_ref,
    value_ref,
    scaled_query_ref,
):
    shards = out_ref.shape[0]
    length = arrived_ref.shape[0]
    clusters = pool_grad_ref.shape[1]
    per_peer = length // shards
    arrived = arrived_ref[...]
    place, first_cell, second_cell = arrived_columns(arrived)
    floats = dot_tn(arrived, on_columns(place, length))[:CHANNELS]
    normed, inverse_std, hidden = layer_norm(floats, gain_column(gain_ref))
    qkv = dot_tn(qkv_t_ref[...], hidden).astype(BF16)
    scaled_query_ref[...] = (qkv[:CHANNELS].astype(F32) * HEAD_DIM ** (-0.5)).astype(BF16)
    key_ref[...] = qkv[CHANNELS : 2 * CHANNELS]
    value_ref[...] = qkv[2 * CHANNELS :]
    half_slot = lax.shift_right_logical(o_slot_ref[...], 1)
    kept = {}

    def cluster_grads():
        first = on_columns(first_cell, clusters)
        second = on_columns(second_cell, clusters)
        denom = cluster_counts(first, second)
        grad_mean = (dot(pool_t_ref[...], pool_grad_ref[...]) / denom).astype(BF16)
        blank = jnp.zeros_like(grad_mean)
        kept["cells"] = (first, second)
        kept["means"] = (
            jnp.concatenate([grad_mean, blank], axis=0),
            jnp.concatenate([blank, grad_mean], axis=0),
        )

    def send_back(start, count):
        first, second = (one[start : start + count] for one in kept["cells"])
        back = dot_nt(first, kept["means"][0]) + dot_nt(second, kept["means"][1])
        peers = slice(start // per_peer, (start + count) // per_peer)
        out_ref[peers, per_peer:, :] = back.astype(BF16).reshape(-1, per_peer, 2 * CHANNELS)

    def map_slots(start, count):
        rows = iota((count, length), 0) + start
        slot_map_ref[start : start + count, :] = onehot(rows == half_slot)

    def hand_over():
        hidden_ref[...] = hidden
        normed_ref[...] = normed
        inverse_std_ref[...] = inverse_std
        query_ref[...] = qkv[:CHANNELS]

    chores = [hand_over, cluster_grads]
    quarter = length // 4
    chores += [functools.partial(send_back, k * quarter, quarter) for k in range(4)]
    eighth = length // 8
    chores += [functools.partial(map_slots, k * eighth, eighth) for k in range(8)]

    units = [(start, head) for start in range(0, length, CHUNK) for head in range(HEADS)]

    def scores(unit):
        start, head = unit
        own = slice(head * HEAD_DIM, (head + 1) * HEAD_DIM)
        return dot_tn(scaled_query_ref[own, start : start + CHUNK], key_ref[own, :])

    def mix(unit):
        start, head = unit
        own = slice(head * HEAD_DIM, (head + 1) * HEAD_DIM)
        return dot_nt(value_ref[own, :], probs_ref[head, start : start + CHUNK, :])

    totals = []
    ready = [scores(unit) for unit in units[:AHEAD]]
    for number, (start, head) in enumerate(units):
        if number + AHEAD < len(units):
            ready.append(scores(units[number + AHEAD]))
        if number >= LAG:
            totals.append(mix(units[number - LAG]))
        for chore in chores[number :: len(units)]:
            chore()
        weights = jnp.exp(ready.pop(0))
        share = 1.0 / jnp.sum(weights, axis=1, keepdims=True)
        probs_ref[head, start : start + CHUNK, :] = (weights * share).astype(BF16)
    totals += [mix(unit) for unit in units[len(units) - LAG :]]
    for number in range(0, len(units), HEADS):
        start = units[number][0]
        attended_ref[:, start : start + CHUNK] = jnp.concatenate(
            totals[number : number + HEADS], axis=0
        )
    attended = attended_ref[...]
    mixed = (floats + dot(out_w_ref[...], attended.astype(BF16))).astype(BF16).astype(F32)
    odd = lax.bitwise_and(o_slot_ref[...], 1) == 1
    pair = jnp.concatenate([jnp.where(odd, 0.0, mixed), jnp.where(odd, mixed, 0.0)], axis=0)
    picked = dot_nt(slot_map_ref[...], pair.astype(BF16))
    out_ref[:, :per_peer, :] = picked.astype(BF16).reshape(shards, per_peer, 2 * CHANNELS)


def backward_kernel(
    returned_ref,
    arrived_ref,
    o_slot_ref,
    qkv_t_ref,
    out_w_ref,
    pool_t_ref,
    gain_ref,
    pool_grad_ref,
    attended_ref,
    probs_ref,
    slot_map_ref,
    hidden_ref,
    normed_ref,
    inverse_std_ref,
    query_ref,
    key_ref,
    value_ref,
    out_ref,
    pooled_ref,
    upstream_ref,
    grad_out_ref,
    grad_query_ref,
    grad_key_ref,
    grad_value_ref,
    place_ref,
):
    shards = out_ref.shape[0]
    length = arrived_ref.shape[0]
    clusters = pool_grad_ref.shape[1]
    per_peer = length // shards
    blank = jnp.zeros((CHANNELS, length), BF16)
    odd = lax.bitwise_and(o_slot_ref[...], 1) == 1
    both = dot_tn(returned_ref[:, per_peer:, :].reshape(length, 2 * CHANNELS), slot_map_ref[...])
    grad_mixed = jnp.where(odd, both[CHANNELS:], both[:CHANNELS])
    grad_mixed_low = grad_mixed.astype(BF16)
    attended = attended_ref[...]
    grad_attended = dot_tn(out_w_ref[...], grad_mixed_low).astype(BF16)
    grad_out_ref[...] = grad_attended
    scaled = grad_attended.astype(F32) * HEAD_DIM ** (-0.5)
    delta = -jnp.sum((scaled * attended).reshape(HEADS, HEAD_DIM, length), axis=1)
    delta_high = delta.astype(BF16).astype(F32)
    for head in range(HEADS):
        own = slice(head * HEAD_DIM, (head + 1) * HEAD_DIM)
        high, whole = delta_high[head : head + 1], delta[head : head + 1]
        row = iota((HEAD_DIM, length), 0)
        extra = jnp.where(row == 0, high, jnp.where(row == 1, whole - high, 0.0))
        upstream_ref[head] = jnp.concatenate([scaled[own], extra], axis=0).astype(BF16)
    place, first_cell, second_cell = arrived_columns(arrived_ref[...])
    kept = {}

    def cells():
        kept["cells"] = (on_columns(first_cell, clusters), on_columns(second_cell, clusters))
        kept["denom"] = cluster_counts(*kept["cells"])

    def pool():
        rows = returned_ref[:, :per_peer, :].reshape(length, 2 * CHANNELS)
        first, second = kept["cells"]
        sums = dot_tn(rows, first)[:CHANNELS] + dot_tn(rows, second)[CHANNELS:]
        kept["mean"] = (sums / kept["denom"]).astype(BF16)

    def pool_out():
        pooled_ref[...] = dot_tn(pool_t_ref[...], kept["mean"]).astype(BF16)
        empty = jnp.zeros((CHANNELS, clusters), BF16)
        kept["pool"] = [
            dot_nt(kept["mean"], jnp.concatenate([empty, half], axis=0))
            for half in (pool_grad_ref[:CHANNELS, :], pool_grad_ref[CHANNELS:, :])
        ]

    def out_grad():
        attended_low = attended.astype(BF16)
        kept["out"] = dot_nt(grad_mixed_low, jnp.concatenate([blank, attended_low], axis=0))

    def map_places(start, count):
        place_ref[start : start + count, :] = on_columns(place[start : start + count], length)

    chores = [cells, pool, pool_out, out_grad]
    eighth = length // 8
    chores += [functools.partial(map_places, k * eighth, eighth) for k in range(8)]

    units = [(start, head) for head in range(HEADS) for start in range(0, length, CHUNK)]

    def change(unit):
        start, head = unit
        own = slice(head * HEAD_DIM, (head + 1) * HEAD_DIM)
        values = jnp.concatenate([value_ref[own, :], jnp.ones((HEAD_DIM, length), BF16)], axis=0)
        return dot_tn(upstream_ref[head, :, start : start + CHUNK], values)

    def use(unit, grad_scores):
        start, head = unit
        own = slice(head * HEAD_DIM, (head + 1) * HEAD_DIM)
        rows = slice(start, start + CHUNK)
        grad_query_ref[own, rows] = dot_nt(key_ref[own, :], grad_scores)
        more = dot(query_ref[own, rows], grad_scores)
        grad_key_ref[own, :] = more if start == 0 else grad_key_ref[own, :] + more

    waiting = []
    ready = [change(unit) for unit in units[:AHEAD]]
    for number, (start, head) in enumerate(units):
        own = slice(head * HEAD_DIM, (head + 1) * HEAD_DIM)
        rows = slice(start, start + CHUNK)
        if number + AHEAD < len(units):
            ready.append(change(units[number + AHEAD]))
        if len(waiting) > LATE:
            use(*waiting.pop(0))
        for chore in chores[number :: len(units)]:
            chore()
        probs = probs_ref[head, rows, :]
        more = dot(grad_out_ref[own, rows], probs)
        grad_value_ref[own, :] = more if start == 0 else grad_value_ref[own, :] + more
        waiting.append(((start, head), (probs.astype(F32) * ready.pop(0)).astype(BF16)))
    for one in waiting:
        use(*one)
    grad_qkv = jnp.concatenate(
        [grad_query_ref[...], grad_key_ref[...], grad_value_ref[...]], axis=0
    ).astype(BF16)
    grad_hidden = dot(qkv_t_ref[...], grad_qkv)
    hidden = hidden_ref[...]
    normed = normed_ref[...]
    qkv_parts = [
        dot_nt(hidden, jnp.concatenate([blank, grad_qkv[start : start + CHANNELS]], axis=0))
        for start in (0, CHANNELS, 2 * CHANNELS)
    ]
    grad_normed = grad_hidden * gain_column(gain_ref)
    grad_norm_in = inverse_std_ref[...] * (
        grad_normed
        - jnp.mean(grad_normed, axis=0, keepdims=True)
        - normed * jnp.mean(grad_normed * normed, axis=0, keepdims=True)
    )
    grad_rows = (grad_mixed + grad_norm_in).astype(BF16)
    back = dot_nt(place_ref[...], jnp.concatenate([grad_rows, blank], axis=0))
    parts = qkv_parts + [kept["out"]] + kept["pool"]
    unused = jnp.zeros((GROUP * per_peer - len(parts) * CHANNELS, 2 * CHANNELS), F32)
    side = jnp.concatenate(parts + [unused], axis=0)
    span = GROUP * per_peer
    for start in range(0, shards, GROUP):
        rows = back[start * per_peer : start * per_peer + span] + side
        out_ref[start : start + GROUP] = rows.astype(BF16).reshape(GROUP, per_peer, 2 * CHANNELS)


def total_kernel(arrived_ref, out_ref):
    out_ref[...] = jnp.sum(arrived_ref[...].astype(F32), axis=0)


def spread_kernel(own_ref, other_ref, out_ref):
    total = own_ref[...] + other_ref[...]
    high = total.astype(BF16).astype(F32)
    low = pltpu.roll(total - high, CHANNELS, 1)
    chosen = jnp.where(iota(total.shape, 1) >= CHANNELS, high, low)
    out_ref[...] = jnp.broadcast_to(chosen[None], out_ref.shape).astype(BF16)


def feat_grad_kernel(arrived_ref, z_slot_ref, out_ref):
    length = arrived_ref.shape[0]
    rows = turned(arrived_ref[...])[:CHANNELS].astype(BF16)
    out_ref[...] = dot(rows, on_rows(z_slot_ref[...], length)).astype(BF16)


def finish_kernel(
    factor,
    total_ref,
    qkv_t_ref,
    gain_in_ref,
    qkv_ref,
    out_ref,
    pool_ref,
    gain_ref,
):
    both = total_ref[...].astype(F32)
    both = (both[:, CHANNELS:] + both[:, :CHANNELS]) * factor
    piece = [both[k * CHANNELS : (k + 1) * CHANNELS] for k in range(6)]
    qkv = jnp.concatenate(piece[:3], axis=1)
    qkv_ref[...] = qkv
    out_ref[...] = piece[3]
    pool_ref[...] = jnp.concatenate(piece[4:], axis=1)
    column = jnp.sum(qkv * qkv_t_ref[...].astype(F32), axis=1, keepdims=True)
    eye = iota((CHANNELS, CHANNELS), 0) == iota((CHANNELS, CHANNELS), 1)
    gain_ref[...] = jnp.sum(jnp.where(eye, column, 0.0), axis=0, keepdims=True) / gain_in_ref[...]


def shape(dims, dtype):
    return jax.ShapeDtypeStruct(dims, dtype)


def call(kernel, outs, scratch=(), flops=0, **more):
    return pl.pallas_call(
        kernel,
        out_shape=outs,
        **more,
        scratch_shapes=list(scratch),
        compiler_params=pltpu.CompilerParams(vmem_limit_bytes=28 * 1024 * 1024),
        cost_estimate=pl.CostEstimate(flops=flops, bytes_accessed=1 << 20, transcendentals=0),
    )


def exchange(blocks):
    return lax.all_to_all(blocks, "pts", split_axis=0, concat_axis=0, tiled=True)


def body(
    feats,
    hilbert_of_z,
    pool_owner,
    pool_slot,
    qkv_weight,
    out_weight,
    pool_weight,
    norm_gain,
    pooled_grad,
):
    length = feats.shape[2]
    shards = lax.axis_size("pts")
    per_peer = length // shards
    clusters = pooled_grad.shape[2]
    lanes = 2 * CHANNELS
    qkv_t = qkv_weight.T
    pool_t = pool_weight.T
    gain = norm_gain.reshape(1, CHANNELS)
    upstream_pool = pooled_grad[0]

    arguments = tuple(
        pltpu.with_memory_space_constraint(one, pltpu.HBM)
        for one in (
        hilbert_of_z,
        pool_owner.reshape(1, length),
        pool_slot,
        feats[0],
        upstream_pool,
        qkv_t,
        out_weight,
        pool_t,
        gain,
        )
    )
    outgoing, z_slot, o_slot, upstream_pool, qkv_t, out_weight, pool_t, gain = call(
        send_kernel,
        (
            shape((shards, per_peer, lanes), BF16),
            shape((1, length), I32),
            shape((1, length), I32),
        )
        + tuple(shape(one.shape, one.dtype) for one in arguments[4:]),
        scratch=tuple(pltpu.VMEM(one.shape, one.dtype) for one in arguments[:4])
        + (pltpu.SemaphoreType.DMA((len(arguments),)),),
        flops=1 << 30,
        in_specs=[pl.BlockSpec(memory_space=pltpu.HBM)] * len(arguments),
    )(*arguments)
    arrived = exchange(outgoing).reshape(length, lanes)

    both_ways, *saved = call(
        forward_kernel,
        (
            shape((shards, 2 * per_peer, lanes), BF16),
            shape((CHANNELS, length), F32),
            shape((HEADS, length, length), BF16),
            shape((length, length), BF16),
            shape((CHANNELS, length), BF16),
            shape((CHANNELS, length), F32),
            shape((1, length), F32),
            shape((CHANNELS, length), BF16),
            shape((CHANNELS, length), BF16),
            shape((CHANNELS, length), BF16),
        ),
        scratch=(pltpu.VMEM((CHANNELS, length), BF16),),
        flops=1 << 32,
    )(arrived, o_slot, qkv_t, out_weight, pool_t, gain, upstream_pool)
    returned = exchange(both_ways)

    last, pooled = call(
        backward_kernel,
        (shape((shards, per_peer, lanes), BF16), shape((2 * CHANNELS, clusters), BF16)),
        scratch=(
            pltpu.VMEM((HEADS, 2 * HEAD_DIM, length), BF16),
            pltpu.VMEM((CHANNELS, length), BF16),
            pltpu.VMEM((CHANNELS, length), F32),
            pltpu.VMEM((CHANNELS, length), F32),
            pltpu.VMEM((CHANNELS, length), F32),
            pltpu.VMEM((length, length), BF16),
        ),
        flops=1 << 33,
    )(
        returned,
        arrived,
        o_slot,
        qkv_t,
        out_weight,
        pool_t,
        gain,
        upstream_pool,
        *saved,
    )
    final = exchange(last)

    own = call(total_kernel, shape((per_peer, lanes), F32))(final)
    other = lax.ppermute(own, "rep", [(0, 1), (1, 0)])
    feat_grad = call(feat_grad_kernel, shape((CHANNELS, length), BF16), flops=1 << 30)(
        final.reshape(length, lanes), z_slot
    )
    other, feat_grad = lax.optimization_barrier((other, feat_grad))
    total = call(spread_kernel, shape((GROUP, per_peer, lanes), BF16))(own, other)
    gathered = lax.all_to_all(
        total,
        "pts",
        split_axis=0,
        concat_axis=0,
        tiled=True,
        axis_index_groups=[
            list(range(start, start + GROUP)) for start in range(0, shards, GROUP)
        ],
    ).reshape(GROUP * per_peer, lanes)
    factor = float(lax.axis_size("rep") * shards * length) ** (-0.5)
    qkv_total, out_total, pool_total, gain_total = call(
        functools.partial(finish_kernel, factor),
        (
            shape((CHANNELS, 3 * CHANNELS), F32),
            shape((CHANNELS, CHANNELS), F32),
            shape((CHANNELS, lanes), F32),
            shape((1, CHANNELS), F32),
        ),
    )(gathered, qkv_t, gain)
    return (
        pooled[None],
        feat_grad[None],
        qkv_total.T,
        out_total,
        pool_total.T,
        gain_total.reshape(CHANNELS),
    )


def solution(mesh):
    return jax.shard_map(
        body,
        mesh=mesh,
        in_specs=(
            P("rep", None, "pts"),
            P("rep", "pts"),
            P("rep", "pts", None),
            P("rep", "pts"),
            P(),
            P(),
            P(),
            P(),
            P("rep", None, "pts"),
        ),
        out_specs=(P("rep", None, "pts"), P("rep", None, "pts"), P(), P(), P(), P()),
        check_vma=False,
    )
```

```python
import functools

import jax
import jax.numpy as jnp
from jax import lax
from jax.experimental import pallas as pl
from jax.experimental.pallas import tpu as pltpu
from jax.sharding import PartitionSpec as P

HEADS = 4
HEAD_DIM = 16
CHANNELS = 64
NORM_EPS = 1e-05
CHUNK = 256
AHEAD = 1
LAG = 2
LATE = 0
GROUP = 64

F32 = jnp.float32
BF16 = jnp.bfloat16
I32 = jnp.int32


def dot(a, b):
    return lax.dot_general(a, b, (((1,), (0,)), ((), ())), preferred_element_type=F32)


def dot_nt(a, b):
    return lax.dot_general(a, b, (((1,), (1,)), ((), ())), preferred_element_type=F32)


def dot_tn(a, b):
    return lax.dot_general(a, b, (((0,), (0,)), ((), ())), preferred_element_type=F32)


def turned(a):
    return a.astype(F32).T


def iota(shape, dim):
    return lax.broadcasted_iota(I32, shape, dim)


def onehot(mask):
    return jnp.where(mask, 1.0, 0.0).astype(BF16)


def on_rows(row, count):
    return onehot(iota((count, row.shape[1]), 0) == row)


def on_columns(column, count):
    return onehot(iota((column.shape[0], count), 1) == column)


def rank_in_group(groups, count):
    length = groups.shape[1]
    member = on_rows(groups, count)
    upto = onehot(iota((128, 128), 0) <= iota((128, 128), 1))
    entry, block = iota((length, 128), 0), iota((length, 128), 1)
    seen = dot(member, onehot(lax.shift_right_logical(entry, 7) < block))
    ranks = []
    for number in range(length // 128):
        part = member[:, number * 128 : (number + 1) * 128]
        running = dot(part, upto) + seen[:, number : number + 1]
        ranks.append(jnp.sum(part.astype(F32) * running, axis=0, keepdims=True) - 1.0)
    return jnp.concatenate(ranks, axis=1).astype(I32), member


def send_kernel(
    pos_hbm,
    owner_hbm,
    cell_hbm,
    feats_hbm,
    pool_grad_hbm,
    qkv_t_hbm,
    out_w_hbm,
    pool_t_hbm,
    gain_hbm,
    out_ref,
    z_slot_ref,
    o_slot_ref,
    pool_grad_ref,
    qkv_t_ref,
    out_w_ref,
    pool_t_ref,
    gain_ref,
    pos_ref,
    owner_ref,
    cell_ref,
    feats_ref,
    sems,
):
    loads = [
        pltpu.make_async_copy(source, target, sems.at[number])
        for number, (source, target) in enumerate(
            (
                (pos_hbm, pos_ref),
                (owner_hbm, owner_ref),
                (cell_hbm, cell_ref),
                (feats_hbm, feats_ref),
                (pool_grad_hbm, pool_grad_ref),
                (qkv_t_hbm, qkv_t_ref),
                (out_w_hbm, out_w_ref),
                (pool_t_hbm, pool_t_ref),
                (gain_hbm, gain_ref),
            )
        )
    ]
    for load in loads:
        load.start()
    for load in loads[:3]:
        load.wait()
    length = pos_ref.shape[1]
    shards = out_ref.shape[0]
    per_peer = length // shards
    positions = pos_ref[...]
    owners = owner_ref[...]
    shift = length.bit_length() - 1
    target = lax.shift_right_logical(positions, shift)
    local = lax.bitwise_and(positions, length - 1)
    z_rank, _ = rank_in_group(target, shards)
    o_rank, owned = rank_in_group(owners, shards)
    z_slot = target * per_peer + z_rank
    o_slot = owners * (2 * per_peer) + o_rank
    z_slot_ref[...] = z_slot
    o_slot_ref[...] = o_slot
    row = iota((CHANNELS, length), 0)
    high = lax.shift_right_logical(local, 5).astype(F32)
    low = lax.bitwise_and(local, 31).astype(F32)
    place = jnp.where(row == 0, high, jnp.where(row == 1, low, 0.0)).astype(BF16)
    cell = (cell_ref[...] + 1).astype(F32)
    rank = iota((2 * per_peer, length), 0)
    cells = dot_nt(owned, jnp.where(rank == o_rank, cell, 0.0).astype(BF16)).astype(BF16)
    peer = lax.shift_right_logical(iota((length, shards), 0), per_peer.bit_length() - 1)
    listed = dot(onehot(peer == iota((length, shards), 1)), cells)
    row = iota(listed.shape, 0)
    place_in_list = iota(listed.shape, 1)
    mine = lax.shift_right_logical(place_in_list, 1) == lax.bitwise_and(row, per_peer - 1)
    listed = jnp.where(mine, listed, 0.0).astype(BF16)
    lane = iota((2 * per_peer, 2 * CHANNELS), 1)
    parity = lax.bitwise_and(iota((2 * per_peer, 2 * CHANNELS), 0), 1)
    out = dot(listed, onehot(lane == parity + CHANNELS + 2))
    loads[3].wait()
    first = jnp.concatenate([feats_ref[...], place], axis=0)
    out = out + dot_nt(on_rows(z_slot, length), first)
    out_ref[...] = out.astype(BF16).reshape(out_ref.shape)
    for load in loads[4:]:
        load.wait()


def arrived_columns(arrived):
    side = arrived[:, CHANNELS:].astype(F32)
    place = (side[:, 0:1] * 32.0 + side[:, 1:2]).astype(I32)
    return place, side[:, 2:3].astype(I32) - 1, side[:, 3:4].astype(I32) - 1


def gain_column(gain_ref):
    gain = gain_ref[...]
    eye = iota((CHANNELS, CHANNELS), 0) == iota((CHANNELS, CHANNELS), 1)
    return jnp.sum(jnp.where(eye, gain, 0.0), axis=1, keepdims=True)


def layer_norm(floats, gain):
    centred = floats - jnp.mean(floats, axis=0, keepdims=True)
    inverse_std = lax.rsqrt(jnp.mean(centred * centred, axis=0, keepdims=True) + NORM_EPS)
    normed = centred * inverse_std
    return normed, inverse_std, (gain * normed).astype(BF16)


def cluster_counts(first, second):
    return jnp.maximum(
        jnp.sum(first.astype(F32) + second.astype(F32), axis=0, keepdims=True), 1.0
    )


def forward_kernel(
    arrived_ref,
    o_slot_ref,
    qkv_t_ref,
    out_w_ref,
    pool_t_ref,
    gain_ref,
    pool_grad_ref,
    out_ref,
    attended_ref,
    probs_ref,
    slot_map_ref,
    hidden_ref,
    normed_ref,
    inverse_std_ref,
    query_ref,
    key_ref,
    value_ref,
    scaled_query_ref,
):
    shards = out_ref.shape[0]
    length = arrived_ref.shape[0]
    clusters = pool_grad_ref.shape[1]
    per_peer = length // shards
    arrived = arrived_ref[...]
    place, first_cell, second_cell = arrived_columns(arrived)
    floats = dot_tn(arrived, on_columns(place, length))[:CHANNELS]
    normed, inverse_std, hidden = layer_norm(floats, gain_column(gain_ref))
    qkv = dot_tn(qkv_t_ref[...], hidden).astype(BF16)
    scaled_query_ref[...] = (qkv[:CHANNELS].astype(F32) * HEAD_DIM ** (-0.5)).astype(BF16)
    key_ref[...] = qkv[CHANNELS : 2 * CHANNELS]
    value_ref[...] = qkv[2 * CHANNELS :]
    half_slot = lax.shift_right_logical(o_slot_ref[...], 1)
    kept = {}

    def cluster_grads():
        first = on_columns(first_cell, clusters)
        second = on_columns(second_cell, clusters)
        denom = cluster_counts(first, second)
        grad_mean = (dot(pool_t_ref[...], pool_grad_ref[...]) / denom).astype(BF16)
        blank = jnp.zeros_like(grad_mean)
        kept["cells"] = (first, second)
        kept["means"] = (
            jnp.concatenate([grad_mean, blank], axis=0),
            jnp.concatenate([blank, grad_mean], axis=0),
        )

    def send_back(start, count):
        first, second = (one[start : start + count] for one in kept["cells"])
        back = dot_nt(first, kept["means"][0]) + dot_nt(second, kept["means"][1])
        peers = slice(start // per_peer, (start + count) // per_peer)
        out_ref[peers, per_peer:, :] = back.astype(BF16).reshape(-1, per_peer, 2 * CHANNELS)

    def map_slots(start, count):
        rows = iota((count, length), 0) + start
        slot_map_ref[start : start + count, :] = onehot(rows == half_slot)

    def hand_over():
        hidden_ref[...] = hidden
        normed_ref[...] = normed
        inverse_std_ref[...] = inverse_std
        query_ref[...] = qkv[:CHANNELS]

    chores = [hand_over, cluster_grads]
    quarter = length // 4
    chores += [functools.partial(send_back, k * quarter, quarter) for k in range(4)]
    eighth = length // 8
    chores += [functools.partial(map_slots, k * eighth, eighth) for k in range(8)]

    units = [(start, head) for start in range(0, length, CHUNK) for head in range(HEADS)]

    def scores(unit):
        start, head = unit
        own = slice(head * HEAD_DIM, (head + 1) * HEAD_DIM)
        return dot_tn(scaled_query_ref[own, start : start + CHUNK], key_ref[own, :])

    def mix(unit):
        start, head = unit
        own = slice(head * HEAD_DIM, (head + 1) * HEAD_DIM)
        return dot_nt(value_ref[own, :], probs_ref[head, start : start + CHUNK, :])

    totals = []
    ready = [scores(unit) for unit in units[:AHEAD]]
    for number, (start, head) in enumerate(units):
        if number + AHEAD < len(units):
            ready.append(scores(units[number + AHEAD]))
        if number >= LAG:
            totals.append(mix(units[number - LAG]))
        for chore in chores[number :: len(units)]:
            chore()
        weights = jnp.exp(ready.pop(0))
        share = 1.0 / jnp.sum(weights, axis=1, keepdims=True)
        probs_ref[head, start : start + CHUNK, :] = (weights * share).astype(BF16)
    totals += [mix(unit) for unit in units[len(units) - LAG :]]
    for number in range(0, len(units), HEADS):
        start = units[number][0]
        attended_ref[:, start : start + CHUNK] = jnp.concatenate(
            totals[number : number + HEADS], axis=0
        )
    attended = attended_ref[...]
    mixed = (floats + dot(out_w_ref[...], attended.astype(BF16))).astype(BF16).astype(F32)
    odd = lax.bitwise_and(o_slot_ref[...], 1) == 1
    pair = jnp.concatenate([jnp.where(odd, 0.0, mixed), jnp.where(odd, mixed, 0.0)], axis=0)
    picked = dot_nt(slot_map_ref[...], pair.astype(BF16))
    out_ref[:, :per_peer, :] = picked.astype(BF16).reshape(shards, per_peer, 2 * CHANNELS)


def backward_kernel(
    returned_ref,
    arrived_ref,
    o_slot_ref,
    qkv_t_ref,
    out_w_ref,
    pool_t_ref,
    gain_ref,
    pool_grad_ref,
    attended_ref,
    probs_ref,
    slot_map_ref,
    hidden_ref,
    normed_ref,
    inverse_std_ref,
    query_ref,
    key_ref,
    value_ref,
    out_ref,
    pooled_hbm,
    pooled_ref,
    pooled_sem,
    upstream_ref,
    grad_out_ref,
    grad_query_ref,
    grad_key_ref,
    grad_value_ref,
    place_ref,
):
    shards = out_ref.shape[0]
    length = arrived_ref.shape[0]
    clusters = pool_grad_ref.shape[1]
    per_peer = length // shards
    blank = jnp.zeros((CHANNELS, length), BF16)
    odd = lax.bitwise_and(o_slot_ref[...], 1) == 1
    both = dot_tn(returned_ref[:, per_peer:, :].reshape(length, 2 * CHANNELS), slot_map_ref[...])
    grad_mixed = jnp.where(odd, both[CHANNELS:], both[:CHANNELS])
    grad_mixed_low = grad_mixed.astype(BF16)
    attended = attended_ref[...]
    grad_attended = dot_tn(out_w_ref[...], grad_mixed_low).astype(BF16)
    grad_out_ref[...] = grad_attended
    scaled = grad_attended.astype(F32) * HEAD_DIM ** (-0.5)
    delta = -jnp.sum((scaled * attended).reshape(HEADS, HEAD_DIM, length), axis=1)
    delta_high = delta.astype(BF16).astype(F32)
    for head in range(HEADS):
        own = slice(head * HEAD_DIM, (head + 1) * HEAD_DIM)
        high, whole = delta_high[head : head + 1], delta[head : head + 1]
        row = iota((HEAD_DIM, length), 0)
        extra = jnp.where(row == 0, high, jnp.where(row == 1, whole - high, 0.0))
        upstream_ref[head] = jnp.concatenate([scaled[own], extra], axis=0).astype(BF16)
    place, first_cell, second_cell = arrived_columns(arrived_ref[...])
    pooled_copy = pltpu.make_async_copy(pooled_ref, pooled_hbm, pooled_sem)
    kept = {}

    def cells():
        kept["cells"] = (on_columns(first_cell, clusters), on_columns(second_cell, clusters))
        kept["denom"] = cluster_counts(*kept["cells"])

    def pool():
        rows = returned_ref[:, :per_peer, :].reshape(length, 2 * CHANNELS)
        first, second = kept["cells"]
        sums = dot_tn(rows, first)[:CHANNELS] + dot_tn(rows, second)[CHANNELS:]
        kept["mean"] = (sums / kept["denom"]).astype(BF16)

    def pool_out():
        pooled_ref[...] = dot_tn(pool_t_ref[...], kept["mean"]).astype(BF16)
        pooled_copy.start()
        empty = jnp.zeros((CHANNELS, clusters), BF16)
        kept["pool"] = [
            dot_nt(kept["mean"], jnp.concatenate([empty, half], axis=0))
            for half in (pool_grad_ref[:CHANNELS, :], pool_grad_ref[CHANNELS:, :])
        ]

    def out_grad():
        attended_low = attended.astype(BF16)
        kept["out"] = dot_nt(grad_mixed_low, jnp.concatenate([blank, attended_low], axis=0))

    def map_places(start, count):
        place_ref[start : start + count, :] = on_columns(place[start : start + count], length)

    chores = [cells, pool, pool_out, out_grad]
    eighth = length // 8
    chores += [functools.partial(map_places, k * eighth, eighth) for k in range(8)]

    units = [(start, head) for head in range(HEADS) for start in range(0, length, CHUNK)]

    def change(unit):
        start, head = unit
        own = slice(head * HEAD_DIM, (head + 1) * HEAD_DIM)
        values = jnp.concatenate([value_ref[own, :], jnp.ones((HEAD_DIM, length), BF16)], axis=0)
        return dot_tn(upstream_ref[head, :, start : start + CHUNK], values)

    def use(unit, grad_scores):
        start, head = unit
        own = slice(head * HEAD_DIM, (head + 1) * HEAD_DIM)
        rows = slice(start, start + CHUNK)
        grad_query_ref[own, rows] = dot_nt(key_ref[own, :], grad_scores)
        more = dot(query_ref[own, rows], grad_scores)
        grad_key_ref[own, :] = more if start == 0 else grad_key_ref[own, :] + more

    waiting = []
    ready = [change(unit) for unit in units[:AHEAD]]
    for number, (start, head) in enumerate(units):
        own = slice(head * HEAD_DIM, (head + 1) * HEAD_DIM)
        rows = slice(start, start + CHUNK)
        if number + AHEAD < len(units):
            ready.append(change(units[number + AHEAD]))
        if len(waiting) > LATE:
            use(*waiting.pop(0))
        for chore in chores[number :: len(units)]:
            chore()
        probs = probs_ref[head, rows, :]
        more = dot(grad_out_ref[own, rows], probs)
        grad_value_ref[own, :] = more if start == 0 else grad_value_ref[own, :] + more
        waiting.append(((start, head), (probs.astype(F32) * ready.pop(0)).astype(BF16)))
    for one in waiting:
        use(*one)
    grad_qkv = jnp.concatenate(
        [grad_query_ref[...], grad_key_ref[...], grad_value_ref[...]], axis=0
    ).astype(BF16)
    grad_hidden = dot(qkv_t_ref[...], grad_qkv)
    hidden = hidden_ref[...]
    normed = normed_ref[...]
    qkv_parts = [
        dot_nt(hidden, jnp.concatenate([blank, grad_qkv[start : start + CHANNELS]], axis=0))
        for start in (0, CHANNELS, 2 * CHANNELS)
    ]
    grad_normed = grad_hidden * gain_column(gain_ref)
    grad_norm_in = inverse_std_ref[...] * (
        grad_normed
        - jnp.mean(grad_normed, axis=0, keepdims=True)
        - normed * jnp.mean(grad_normed * normed, axis=0, keepdims=True)
    )
    grad_rows = (grad_mixed + grad_norm_in).astype(BF16)
    back = dot_nt(place_ref[...], jnp.concatenate([grad_rows, blank], axis=0))
    parts = qkv_parts + [kept["out"]] + kept["pool"]
    unused = jnp.zeros((GROUP * per_peer - len(parts) * CHANNELS, 2 * CHANNELS), F32)
    side = jnp.concatenate(parts + [unused], axis=0)
    span = GROUP * per_peer
    for start in range(0, shards, GROUP):
        rows = back[start * per_peer : start * per_peer + span] + side
        out_ref[start : start + GROUP] = rows.astype(BF16).reshape(GROUP, per_peer, 2 * CHANNELS)
    pooled_copy.wait()


def total_kernel(arrived_ref, out_ref):
    out_ref[...] = jnp.sum(arrived_ref[...].astype(F32), axis=0)


def spread_kernel(own_ref, other_ref, out_ref):
    total = own_ref[...] + other_ref[...]
    half = total.shape[0] // 2
    lower = pltpu.roll(total, CHANNELS, 1)[half:]
    chosen = jnp.where(iota(lower.shape, 1) >= CHANNELS, total[:half], lower)
    out_ref[...] = jnp.broadcast_to(chosen[None], out_ref.shape).astype(BF16)


def feat_grad_kernel(arrived_ref, z_slot_ref, out_ref):
    length = arrived_ref.shape[0]
    rows = turned(arrived_ref[...])[:CHANNELS].astype(BF16)
    out_ref[...] = dot(rows, on_rows(z_slot_ref[...], length)).astype(BF16)


def finish_kernel(
    factor,
    total_ref,
    qkv_t_ref,
    gain_in_ref,
    feat_ref,
    qkv_ref,
    out_ref,
    pool_ref,
    gain_ref,
    feat_hbm,
    feat_sem,
):
    feat_copy = pltpu.make_async_copy(feat_ref, feat_hbm, feat_sem)
    feat_copy.start()
    both = total_ref[...].astype(F32) * factor
    both = jnp.concatenate([both[:, :, CHANNELS:], both[:, :, :CHANNELS]], axis=1)
    both = both.reshape(both.shape[0] * both.shape[1], CHANNELS)
    piece = [both[k * CHANNELS : (k + 1) * CHANNELS] for k in range(6)]
    qkv = jnp.concatenate(piece[:3], axis=1)
    qkv_ref[...] = qkv
    out_ref[...] = piece[3]
    pool_ref[...] = jnp.concatenate(piece[4:], axis=1)
    column = jnp.sum(qkv * qkv_t_ref[...].astype(F32), axis=1, keepdims=True)
    eye = iota((CHANNELS, CHANNELS), 0) == iota((CHANNELS, CHANNELS), 1)
    gain_ref[...] = jnp.sum(jnp.where(eye, column, 0.0), axis=0, keepdims=True) / gain_in_ref[...]
    feat_copy.wait()


def shape(dims, dtype):
    return jax.ShapeDtypeStruct(dims, dtype)


def call(kernel, outs, scratch=(), flops=0, **more):
    return pl.pallas_call(
        kernel,
        out_shape=outs,
        **more,
        scratch_shapes=list(scratch),
        compiler_params=pltpu.CompilerParams(vmem_limit_bytes=28 * 1024 * 1024),
        cost_estimate=pl.CostEstimate(flops=flops, bytes_accessed=1 << 20, transcendentals=0),
    )


def exchange(blocks):
    return lax.all_to_all(blocks, "pts", split_axis=0, concat_axis=0, tiled=True)


def body(
    feats,
    hilbert_of_z,
    pool_owner,
    pool_slot,
    qkv_weight,
    out_weight,
    pool_weight,
    norm_gain,
    pooled_grad,
):
    length = feats.shape[2]
    shards = lax.axis_size("pts")
    per_peer = length // shards
    clusters = pooled_grad.shape[2]
    lanes = 2 * CHANNELS
    qkv_t = qkv_weight.T
    pool_t = pool_weight.T
    gain = norm_gain.reshape(1, CHANNELS)
    upstream_pool = pooled_grad[0]

    arguments = tuple(
        pltpu.with_memory_space_constraint(one, pltpu.HBM)
        for one in (
        hilbert_of_z,
        pool_owner.reshape(1, length),
        pool_slot,
        feats[0],
        upstream_pool,
        qkv_t,
        out_weight,
        pool_t,
        gain,
        )
    )
    outgoing, z_slot, o_slot, upstream_pool, qkv_t, out_weight, pool_t, gain = call(
        send_kernel,
        (
            shape((shards, per_peer, lanes), BF16),
            shape((1, length), I32),
            shape((1, length), I32),
        )
        + tuple(shape(one.shape, one.dtype) for one in arguments[4:]),
        scratch=tuple(pltpu.VMEM(one.shape, one.dtype) for one in arguments[:4])
        + (pltpu.SemaphoreType.DMA((len(arguments),)),),
        flops=1 << 30,
        in_specs=[pl.BlockSpec(memory_space=pltpu.HBM)] * len(arguments),
    )(*arguments)
    arrived = exchange(outgoing).reshape(length, lanes)

    both_ways, *saved = call(
        forward_kernel,
        (
            shape((shards, 2 * per_peer, lanes), BF16),
            shape((CHANNELS, length), F32),
            shape((HEADS, length, length), BF16),
            shape((length, length), BF16),
            shape((CHANNELS, length), BF16),
            shape((CHANNELS, length), F32),
            shape((1, length), F32),
            shape((CHANNELS, length), BF16),
            shape((CHANNELS, length), BF16),
            shape((CHANNELS, length), BF16),
        ),
        scratch=(pltpu.VMEM((CHANNELS, length), BF16),),
        flops=1 << 32,
    )(arrived, o_slot, qkv_t, out_weight, pool_t, gain, upstream_pool)
    returned = exchange(both_ways)

    block = pl.BlockSpec(memory_space=pltpu.VMEM)
    outside = pl.BlockSpec(memory_space=pl.ANY)
    last, pooled = call(
        backward_kernel,
        (shape((shards, per_peer, lanes), BF16), shape((2 * CHANNELS, clusters), BF16)),
        out_specs=(block, outside),
        scratch=(
            pltpu.VMEM((2 * CHANNELS, clusters), BF16),
            pltpu.SemaphoreType.DMA,
            pltpu.VMEM((HEADS, 2 * HEAD_DIM, length), BF16),
            pltpu.VMEM((CHANNELS, length), BF16),
            pltpu.VMEM((CHANNELS, length), F32),
            pltpu.VMEM((CHANNELS, length), F32),
            pltpu.VMEM((CHANNELS, length), F32),
            pltpu.VMEM((length, length), BF16),
        ),
        flops=1 << 33,
    )(
        returned,
        arrived,
        o_slot,
        qkv_t,
        out_weight,
        pool_t,
        gain,
        upstream_pool,
        *saved,
    )
    final = exchange(last)

    own = call(total_kernel, shape((per_peer, lanes), F32))(final)
    other = lax.ppermute(own, "rep", [(0, 1), (1, 0)])
    feat_grad = call(feat_grad_kernel, shape((CHANNELS, length), BF16), flops=1 << 30)(
        final.reshape(length, lanes), z_slot
    )
    other, feat_grad = lax.optimization_barrier((other, feat_grad))
    total = call(spread_kernel, shape((GROUP, per_peer // 2, lanes), BF16))(own, other)
    gathered = lax.all_to_all(
        total,
        "pts",
        split_axis=0,
        concat_axis=0,
        tiled=True,
        axis_index_groups=[
            list(range(start, start + GROUP)) for start in range(0, shards, GROUP)
        ],
    )
    factor = float(lax.axis_size("rep") * shards * length) ** (-0.5)
    qkv_total, out_total, pool_total, gain_total, feat_grad = call(
        functools.partial(finish_kernel, factor),
        (
            shape((CHANNELS, 3 * CHANNELS), F32),
            shape((CHANNELS, CHANNELS), F32),
            shape((CHANNELS, lanes), F32),
            shape((1, CHANNELS), F32),
            shape((CHANNELS, length), BF16),
        ),
        out_specs=(block, block, block, block, outside),
        scratch=(pltpu.SemaphoreType.DMA,),
    )(gathered, qkv_t, gain, feat_grad)
    return (
        pooled[None],
        feat_grad[None],
        qkv_total.T,
        out_total,
        pool_total.T,
        gain_total.reshape(CHANNELS),
    )


def solution(mesh):
    return jax.shard_map(
        body,
        mesh=mesh,
        in_specs=(
            P("rep", None, "pts"),
            P("rep", "pts"),
            P("rep", "pts", None),
            P("rep", "pts"),
            P(),
            P(),
            P(),
            P(),
            P("rep", None, "pts"),
        ),
        out_specs=(P("rep", None, "pts"), P("rep", None, "pts"), P(), P(), P(), P()),
        check_vma=False,
    )
```

```python
import functools

import jax
import jax.numpy as jnp
from jax import lax
from jax.experimental import pallas as pl
from jax.experimental.pallas import tpu as pltpu
from jax.sharding import PartitionSpec as P

HEADS = 4
HEAD_DIM = 16
CHANNELS = 64
NORM_EPS = 1e-05
CHUNK = 256
AHEAD = 1
LAG = 2
LATE = 0
GROUP = 64

F32 = jnp.float32
BF16 = jnp.bfloat16
I32 = jnp.int32


def dot(a, b):
    return lax.dot_general(a, b, (((1,), (0,)), ((), ())), preferred_element_type=F32)


def dot_nt(a, b):
    return lax.dot_general(a, b, (((1,), (1,)), ((), ())), preferred_element_type=F32)


def dot_tn(a, b):
    return lax.dot_general(a, b, (((0,), (0,)), ((), ())), preferred_element_type=F32)


def turned(a):
    return a.astype(F32).T


def iota(shape, dim):
    return lax.broadcasted_iota(I32, shape, dim)


def onehot(mask):
    return jnp.where(mask, 1.0, 0.0).astype(BF16)


def on_rows(row, count):
    return onehot(iota((count, row.shape[1]), 0) == row)


def on_columns(column, count):
    return onehot(iota((column.shape[0], count), 1) == column)


def rank_in_group(groups, count):
    length = groups.shape[1]
    member = on_rows(groups, count)
    upto = onehot(iota((128, 128), 0) <= iota((128, 128), 1))
    entry, block = iota((length, 128), 0), iota((length, 128), 1)
    seen = dot(member, onehot(lax.shift_right_logical(entry, 7) < block))
    ranks = []
    for number in range(length // 128):
        part = member[:, number * 128 : (number + 1) * 128]
        running = dot(part, upto) + seen[:, number : number + 1]
        ranks.append(jnp.sum(part.astype(F32) * running, axis=0, keepdims=True) - 1.0)
    return jnp.concatenate(ranks, axis=1).astype(I32), member


def send_kernel(
    pos_hbm,
    owner_hbm,
    cell_hbm,
    feats_hbm,
    pool_grad_hbm,
    qkv_t_hbm,
    out_w_hbm,
    pool_t_hbm,
    gain_hbm,
    out_ref,
    z_slot_ref,
    o_slot_ref,
    pool_grad_ref,
    qkv_t_ref,
    out_w_ref,
    pool_t_ref,
    gain_ref,
    pos_ref,
    owner_ref,
    cell_ref,
    feats_ref,
    sems,
):
    loads = [
        pltpu.make_async_copy(source, target, sems.at[number])
        for number, (source, target) in enumerate(
            (
                (pos_hbm, pos_ref),
                (owner_hbm, owner_ref),
                (cell_hbm, cell_ref),
                (feats_hbm, feats_ref),
                (pool_grad_hbm, pool_grad_ref),
                (qkv_t_hbm, qkv_t_ref),
                (out_w_hbm, out_w_ref),
                (pool_t_hbm, pool_t_ref),
                (gain_hbm, gain_ref),
            )
        )
    ]
    for load in loads:
        load.start()
    for load in loads[:3]:
        load.wait()
    length = pos_ref.shape[1]
    shards = out_ref.shape[0]
    per_peer = length // shards
    positions = pos_ref[...]
    owners = owner_ref[...]
    shift = length.bit_length() - 1
    target = lax.shift_right_logical(positions, shift)
    local = lax.bitwise_and(positions, length - 1)
    z_rank, _ = rank_in_group(target, shards)
    o_rank, owned = rank_in_group(owners, shards)
    z_slot = target * per_peer + z_rank
    o_slot = owners * (2 * per_peer) + o_rank
    z_slot_ref[...] = z_slot
    o_slot_ref[...] = o_slot
    row = iota((CHANNELS, length), 0)
    high = lax.shift_right_logical(local, 5).astype(F32)
    low = lax.bitwise_and(local, 31).astype(F32)
    place = jnp.where(row == 0, high, jnp.where(row == 1, low, 0.0)).astype(BF16)
    cell = (cell_ref[...] + 1).astype(F32)
    rank = iota((2 * per_peer, length), 0)
    cells = dot_nt(owned, jnp.where(rank == o_rank, cell, 0.0).astype(BF16)).astype(BF16)
    peer = lax.shift_right_logical(iota((length, shards), 0), per_peer.bit_length() - 1)
    listed = dot(onehot(peer == iota((length, shards), 1)), cells)
    row = iota(listed.shape, 0)
    place_in_list = iota(listed.shape, 1)
    mine = lax.shift_right_logical(place_in_list, 1) == lax.bitwise_and(row, per_peer - 1)
    listed = jnp.where(mine, listed, 0.0).astype(BF16)
    lane = iota((2 * per_peer, 2 * CHANNELS), 1)
    parity = lax.bitwise_and(iota((2 * per_peer, 2 * CHANNELS), 0), 1)
    out = dot(listed, onehot(lane == parity + CHANNELS + 2))
    loads[3].wait()
    first = jnp.concatenate([feats_ref[...], place], axis=0)
    out = out + dot_nt(on_rows(z_slot, length), first)
    out_ref[...] = out.astype(BF16).reshape(out_ref.shape)
    for load in loads[4:]:
        load.wait()


def arrived_columns(arrived):
    side = arrived[:, CHANNELS:].astype(F32)
    place = (side[:, 0:1] * 32.0 + side[:, 1:2]).astype(I32)
    return place, side[:, 2:3].astype(I32) - 1, side[:, 3:4].astype(I32) - 1


def gain_column(gain_ref):
    gain = gain_ref[...]
    eye = iota((CHANNELS, CHANNELS), 0) == iota((CHANNELS, CHANNELS), 1)
    return jnp.sum(jnp.where(eye, gain, 0.0), axis=1, keepdims=True)


def layer_norm(floats, gain):
    centred = floats - jnp.mean(floats, axis=0, keepdims=True)
    inverse_std = lax.rsqrt(jnp.mean(centred * centred, axis=0, keepdims=True) + NORM_EPS)
    normed = centred * inverse_std
    return normed, inverse_std, (gain * normed).astype(BF16)


def cluster_counts(first, second):
    return jnp.maximum(
        jnp.sum(first.astype(F32) + second.astype(F32), axis=0, keepdims=True), 1.0
    )


def forward_kernel(
    arrived_ref,
    o_slot_ref,
    qkv_t_ref,
    out_w_ref,
    pool_t_ref,
    gain_ref,
    pool_grad_ref,
    out_ref,
    attended_ref,
    probs_ref,
    slot_map_ref,
    hidden_ref,
    normed_ref,
    inverse_std_ref,
    query_ref,
    key_ref,
    value_ref,
    scaled_query_ref,
):
    shards = out_ref.shape[0]
    length = arrived_ref.shape[0]
    clusters = pool_grad_ref.shape[1]
    per_peer = length // shards
    arrived = arrived_ref[...]
    place, first_cell, second_cell = arrived_columns(arrived)
    floats = dot_tn(arrived, on_columns(place, length))[:CHANNELS]
    normed, inverse_std, hidden = layer_norm(floats, gain_column(gain_ref))
    qkv = dot_tn(qkv_t_ref[...], hidden).astype(BF16)
    scaled_query_ref[...] = (qkv[:CHANNELS].astype(F32) * HEAD_DIM ** (-0.5)).astype(BF16)
    key_ref[...] = qkv[CHANNELS : 2 * CHANNELS]
    value_ref[...] = qkv[2 * CHANNELS :]
    half_slot = lax.shift_right_logical(o_slot_ref[...], 1)
    kept = {}

    def cluster_grads():
        first = on_columns(first_cell, clusters)
        second = on_columns(second_cell, clusters)
        denom = cluster_counts(first, second)
        grad_mean = (dot(pool_t_ref[...], pool_grad_ref[...]) / denom).astype(BF16)
        blank = jnp.zeros_like(grad_mean)
        kept["cells"] = (first, second)
        kept["means"] = (
            jnp.concatenate([grad_mean, blank], axis=0),
            jnp.concatenate([blank, grad_mean], axis=0),
        )

    def send_back(start, count):
        first, second = (one[start : start + count] for one in kept["cells"])
        back = dot_nt(first, kept["means"][0]) + dot_nt(second, kept["means"][1])
        peers = slice(start // per_peer, (start + count) // per_peer)
        out_ref[peers, per_peer:, :] = back.astype(BF16).reshape(-1, per_peer, 2 * CHANNELS)

    def map_slots(start, count):
        rows = iota((count, length), 0) + start
        slot_map_ref[start : start + count, :] = onehot(rows == half_slot)

    def hand_over():
        hidden_ref[...] = hidden
        normed_ref[...] = normed
        inverse_std_ref[...] = inverse_std
        query_ref[...] = qkv[:CHANNELS]

    chores = [hand_over, cluster_grads]
    quarter = length // 4
    chores += [functools.partial(send_back, k * quarter, quarter) for k in range(4)]
    eighth = length // 8
    chores += [functools.partial(map_slots, k * eighth, eighth) for k in range(8)]

    units = [(start, head) for start in range(0, length, CHUNK) for head in range(HEADS)]

    def scores(unit):
        start, head = unit
        own = slice(head * HEAD_DIM, (head + 1) * HEAD_DIM)
        return dot_tn(scaled_query_ref[own, start : start + CHUNK], key_ref[own, :])

    def mix(unit):
        start, head = unit
        own = slice(head * HEAD_DIM, (head + 1) * HEAD_DIM)
        return dot_nt(value_ref[own, :], probs_ref[head, start : start + CHUNK, :])

    totals = []
    ready = [scores(unit) for unit in units[:AHEAD]]
    for number, (start, head) in enumerate(units):
        if number + AHEAD < len(units):
            ready.append(scores(units[number + AHEAD]))
        if number >= LAG:
            totals.append(mix(units[number - LAG]))
        for chore in chores[number :: len(units)]:
            chore()
        weights = jnp.exp(ready.pop(0))
        share = 1.0 / jnp.sum(weights, axis=1, keepdims=True)
        probs_ref[head, start : start + CHUNK, :] = (weights * share).astype(BF16)
    totals += [mix(unit) for unit in units[len(units) - LAG :]]
    for number in range(0, len(units), HEADS):
        start = units[number][0]
        attended_ref[:, start : start + CHUNK] = jnp.concatenate(
            totals[number : number + HEADS], axis=0
        )
    attended = attended_ref[...]
    mixed = (floats + dot(out_w_ref[...], attended.astype(BF16))).astype(BF16).astype(F32)
    odd = lax.bitwise_and(o_slot_ref[...], 1) == 1
    pair = jnp.concatenate([jnp.where(odd, 0.0, mixed), jnp.where(odd, mixed, 0.0)], axis=0)
    picked = dot_nt(slot_map_ref[...], pair.astype(BF16))
    out_ref[:, :per_peer, :] = picked.astype(BF16).reshape(shards, per_peer, 2 * CHANNELS)


def backward_kernel(
    returned_ref,
    arrived_ref,
    o_slot_ref,
    qkv_t_ref,
    out_w_ref,
    pool_t_ref,
    gain_ref,
    pool_grad_ref,
    attended_ref,
    probs_ref,
    slot_map_ref,
    hidden_ref,
    normed_ref,
    inverse_std_ref,
    query_ref,
    key_ref,
    value_ref,
    out_ref,
    pooled_hbm,
    pooled_ref,
    pooled_sem,
    upstream_ref,
    grad_out_ref,
    grad_query_ref,
    grad_key_ref,
    grad_value_ref,
    place_ref,
):
    shards = out_ref.shape[0]
    length = arrived_ref.shape[0]
    clusters = pool_grad_ref.shape[1]
    per_peer = length // shards
    blank = jnp.zeros((CHANNELS, length), BF16)
    odd = lax.bitwise_and(o_slot_ref[...], 1) == 1
    both = dot_tn(returned_ref[:, per_peer:, :].reshape(length, 2 * CHANNELS), slot_map_ref[...])
    grad_mixed = jnp.where(odd, both[CHANNELS:], both[:CHANNELS])
    grad_mixed_low = grad_mixed.astype(BF16)
    attended = attended_ref[...]
    grad_attended = dot_tn(out_w_ref[...], grad_mixed_low).astype(BF16)
    grad_out_ref[...] = grad_attended
    scaled = grad_attended.astype(F32) * HEAD_DIM ** (-0.5)
    delta = -jnp.sum((scaled * attended).reshape(HEADS, HEAD_DIM, length), axis=1)
    delta_high = delta.astype(BF16).astype(F32)
    for head in range(HEADS):
        own = slice(head * HEAD_DIM, (head + 1) * HEAD_DIM)
        high, whole = delta_high[head : head + 1], delta[head : head + 1]
        row = iota((HEAD_DIM, length), 0)
        extra = jnp.where(row == 0, high, jnp.where(row == 1, whole - high, 0.0))
        upstream_ref[head] = jnp.concatenate([scaled[own], extra], axis=0).astype(BF16)
    place, first_cell, second_cell = arrived_columns(arrived_ref[...])
    pooled_copy = pltpu.make_async_copy(pooled_ref, pooled_hbm, pooled_sem)
    kept = {}

    def cells():
        kept["cells"] = (on_columns(first_cell, clusters), on_columns(second_cell, clusters))
        kept["denom"] = cluster_counts(*kept["cells"])

    def pool():
        rows = returned_ref[:, :per_peer, :].reshape(length, 2 * CHANNELS)
        first, second = kept["cells"]
        sums = dot_tn(rows, first)[:CHANNELS] + dot_tn(rows, second)[CHANNELS:]
        kept["mean"] = (sums / kept["denom"]).astype(BF16)

    def pool_out():
        pooled_ref[...] = dot_tn(pool_t_ref[...], kept["mean"]).astype(BF16)
        pooled_copy.start()
        empty = jnp.zeros((CHANNELS, clusters), BF16)
        kept["pool"] = [
            dot_nt(kept["mean"], jnp.concatenate([empty, half], axis=0))
            for half in (pool_grad_ref[:CHANNELS, :], pool_grad_ref[CHANNELS:, :])
        ]

    def out_grad():
        attended_low = attended.astype(BF16)
        kept["out"] = dot_nt(grad_mixed_low, jnp.concatenate([blank, attended_low], axis=0))

    def map_places(start, count):
        place_ref[start : start + count, :] = on_columns(place[start : start + count], length)

    chores = [cells, pool, pool_out, out_grad]
    eighth = length // 8
    chores += [functools.partial(map_places, k * eighth, eighth) for k in range(8)]

    units = [(start, head) for head in range(HEADS) for start in range(0, length, CHUNK)]

    def change(unit):
        start, head = unit
        own = slice(head * HEAD_DIM, (head + 1) * HEAD_DIM)
        values = jnp.concatenate([value_ref[own, :], jnp.ones((HEAD_DIM, length), BF16)], axis=0)
        return dot_tn(upstream_ref[head, :, start : start + CHUNK], values)

    def use(unit, grad_scores):
        start, head = unit
        own = slice(head * HEAD_DIM, (head + 1) * HEAD_DIM)
        rows = slice(start, start + CHUNK)
        grad_query_ref[own, rows] = dot_nt(key_ref[own, :], grad_scores)
        more = dot(query_ref[own, rows], grad_scores)
        grad_key_ref[own, :] = more if start == 0 else grad_key_ref[own, :] + more

    waiting = []
    ready = [change(unit) for unit in units[:AHEAD]]
    for number, (start, head) in enumerate(units):
        own = slice(head * HEAD_DIM, (head + 1) * HEAD_DIM)
        rows = slice(start, start + CHUNK)
        if number + AHEAD < len(units):
            ready.append(change(units[number + AHEAD]))
        if len(waiting) > LATE:
            use(*waiting.pop(0))
        for chore in chores[number :: len(units)]:
            chore()
        probs = probs_ref[head, rows, :]
        more = dot(grad_out_ref[own, rows], probs)
        grad_value_ref[own, :] = more if start == 0 else grad_value_ref[own, :] + more
        waiting.append(((start, head), (probs.astype(F32) * ready.pop(0)).astype(BF16)))
    for one in waiting:
        use(*one)
    grad_qkv = jnp.concatenate(
        [grad_query_ref[...], grad_key_ref[...], grad_value_ref[...]], axis=0
    ).astype(BF16)
    grad_hidden = dot(qkv_t_ref[...], grad_qkv)
    hidden = hidden_ref[...]
    normed = normed_ref[...]
    qkv_parts = [
        dot_nt(hidden, jnp.concatenate([blank, grad_qkv[start : start + CHANNELS]], axis=0))
        for start in (0, CHANNELS, 2 * CHANNELS)
    ]
    grad_normed = grad_hidden * gain_column(gain_ref)
    grad_norm_in = inverse_std_ref[...] * (
        grad_normed
        - jnp.mean(grad_normed, axis=0, keepdims=True)
        - normed * jnp.mean(grad_normed * normed, axis=0, keepdims=True)
    )
    grad_rows = (grad_mixed + grad_norm_in).astype(BF16)
    back = dot_nt(place_ref[...], jnp.concatenate([grad_rows, blank], axis=0))
    parts = qkv_parts + [kept["out"]] + kept["pool"]
    unused = jnp.zeros((GROUP * per_peer - len(parts) * CHANNELS, 2 * CHANNELS), F32)
    side = jnp.concatenate(parts + [unused], axis=0)
    span = GROUP * per_peer
    for start in range(0, shards, GROUP):
        rows = back[start * per_peer : start * per_peer + span] + side
        out_ref[start : start + GROUP] = rows.astype(BF16).reshape(GROUP, per_peer, 2 * CHANNELS)
    pooled_copy.wait()


def total_kernel(arrived_ref, out_ref):
    out_ref[...] = jnp.sum(arrived_ref[...].astype(F32), axis=0)


def spread_kernel(own_ref, other_ref, out_ref):
    total = own_ref[...] + other_ref[...]
    half = total.shape[0] // 2
    lower = pltpu.roll(total, CHANNELS, 1)[half:]
    chosen = jnp.where(iota(lower.shape, 1) >= CHANNELS, total[:half], lower)
    out_ref[...] = jnp.broadcast_to(chosen[None], out_ref.shape).astype(BF16)


def feat_grad_kernel(arrived_ref, z_slot_ref, out_ref):
    length = arrived_ref.shape[0]
    z_map = on_rows(z_slot_ref[...], length)
    out_ref[...] = dot_tn(arrived_ref[...], z_map)[:CHANNELS].astype(BF16)


def finish_kernel(
    factor,
    total_ref,
    qkv_t_ref,
    gain_in_ref,
    qkv_ref,
    out_ref,
    pool_ref,
    gain_ref,
):
    both = total_ref[...].astype(F32) * factor
    both = jnp.concatenate([both[:, :, CHANNELS:], both[:, :, :CHANNELS]], axis=1)
    both = both.reshape(both.shape[0] * both.shape[1], CHANNELS)
    piece = [both[k * CHANNELS : (k + 1) * CHANNELS] for k in range(6)]
    qkv = jnp.concatenate(piece[:3], axis=1)
    qkv_ref[...] = qkv
    out_ref[...] = piece[3]
    pool_ref[...] = jnp.concatenate(piece[4:], axis=1)
    column = jnp.sum(qkv * qkv_t_ref[...].astype(F32), axis=1, keepdims=True)
    eye = iota((CHANNELS, CHANNELS), 0) == iota((CHANNELS, CHANNELS), 1)
    gain_ref[...] = jnp.sum(jnp.where(eye, column, 0.0), axis=0, keepdims=True) / gain_in_ref[...]


def shape(dims, dtype):
    return jax.ShapeDtypeStruct(dims, dtype)


def call(kernel, outs, scratch=(), flops=0, **more):
    return pl.pallas_call(
        kernel,
        out_shape=outs,
        **more,
        scratch_shapes=list(scratch),
        compiler_params=pltpu.CompilerParams(vmem_limit_bytes=28 * 1024 * 1024),
        cost_estimate=pl.CostEstimate(flops=flops, bytes_accessed=1 << 20, transcendentals=0),
    )


def exchange(blocks):
    return lax.all_to_all(blocks, "pts", split_axis=0, concat_axis=0, tiled=True)


def body(
    feats,
    hilbert_of_z,
    pool_owner,
    pool_slot,
    qkv_weight,
    out_weight,
    pool_weight,
    norm_gain,
    pooled_grad,
):
    length = feats.shape[2]
    shards = lax.axis_size("pts")
    per_peer = length // shards
    clusters = pooled_grad.shape[2]
    lanes = 2 * CHANNELS
    qkv_t = qkv_weight.T
    pool_t = pool_weight.T
    gain = norm_gain.reshape(1, CHANNELS)
    upstream_pool = pooled_grad[0]

    arguments = tuple(
        pltpu.with_memory_space_constraint(one, pltpu.HBM)
        for one in (
        hilbert_of_z,
        pool_owner.reshape(1, length),
        pool_slot,
        feats[0],
        upstream_pool,
        qkv_t,
        out_weight,
        pool_t,
        gain,
        )
    )
    outgoing, z_slot, o_slot, upstream_pool, qkv_t, out_weight, pool_t, gain = call(
        send_kernel,
        (
            shape((shards, per_peer, lanes), BF16),
            shape((1, length), I32),
            shape((1, length), I32),
        )
        + tuple(shape(one.shape, one.dtype) for one in arguments[4:]),
        scratch=tuple(pltpu.VMEM(one.shape, one.dtype) for one in arguments[:4])
        + (pltpu.SemaphoreType.DMA((len(arguments),)),),
        flops=1 << 30,
        in_specs=[pl.BlockSpec(memory_space=pltpu.HBM)] * len(arguments),
    )(*arguments)
    arrived = exchange(outgoing).reshape(length, lanes)

    both_ways, *saved = call(
        forward_kernel,
        (
            shape((shards, 2 * per_peer, lanes), BF16),
            shape((CHANNELS, length), F32),
            shape((HEADS, length, length), BF16),
            shape((length, length), BF16),
            shape((CHANNELS, length), BF16),
            shape((CHANNELS, length), F32),
            shape((1, length), F32),
            shape((CHANNELS, length), BF16),
            shape((CHANNELS, length), BF16),
            shape((CHANNELS, length), BF16),
        ),
        scratch=(pltpu.VMEM((CHANNELS, length), BF16),),
        flops=1 << 32,
    )(arrived, o_slot, qkv_t, out_weight, pool_t, gain, upstream_pool)
    returned = exchange(both_ways)

    block = pl.BlockSpec(memory_space=pltpu.VMEM)
    outside = pl.BlockSpec(memory_space=pl.ANY)
    last, pooled = call(
        backward_kernel,
        (shape((shards, per_peer, lanes), BF16), shape((2 * CHANNELS, clusters), BF16)),
        out_specs=(block, outside),
        scratch=(
            pltpu.VMEM((2 * CHANNELS, clusters), BF16),
            pltpu.SemaphoreType.DMA,
            pltpu.VMEM((HEADS, 2 * HEAD_DIM, length), BF16),
            pltpu.VMEM((CHANNELS, length), BF16),
            pltpu.VMEM((CHANNELS, length), F32),
            pltpu.VMEM((CHANNELS, length), F32),
            pltpu.VMEM((CHANNELS, length), F32),
            pltpu.VMEM((length, length), BF16),
        ),
        flops=1 << 33,
    )(
        returned,
        arrived,
        o_slot,
        qkv_t,
        out_weight,
        pool_t,
        gain,
        upstream_pool,
        *saved,
    )
    final = exchange(last)

    own = call(total_kernel, shape((per_peer, lanes), F32))(final)
    other = lax.ppermute(own, "rep", [(0, 1), (1, 0)])
    feat_grad = call(feat_grad_kernel, shape((CHANNELS, length), BF16), flops=1 << 30)(
        final.reshape(length, lanes), z_slot
    )
    other, feat_grad = lax.optimization_barrier((other, feat_grad))
    total = call(spread_kernel, shape((GROUP, per_peer // 2, lanes), BF16))(own, other)
    gathered = lax.all_to_all(
        total,
        "pts",
        split_axis=0,
        concat_axis=0,
        tiled=True,
        axis_index_groups=[
            list(range(start, start + GROUP)) for start in range(0, shards, GROUP)
        ],
    )
    factor = float(lax.axis_size("rep") * shards * length) ** (-0.5)
    qkv_total, out_total, pool_total, gain_total = call(
        functools.partial(finish_kernel, factor),
        (
            shape((CHANNELS, 3 * CHANNELS), F32),
            shape((CHANNELS, CHANNELS), F32),
            shape((CHANNELS, lanes), F32),
            shape((1, CHANNELS), F32),
        ),
    )(gathered, qkv_t, gain)
    return (
        pooled[None],
        feat_grad[None],
        qkv_total.T,
        out_total,
        pool_total.T,
        gain_total.reshape(CHANNELS),
    )


def solution(mesh):
    return jax.shard_map(
        body,
        mesh=mesh,
        in_specs=(
            P("rep", None, "pts"),
            P("rep", "pts"),
            P("rep", "pts", None),
            P("rep", "pts"),
            P(),
            P(),
            P(),
            P(),
            P("rep", None, "pts"),
        ),
        out_specs=(P("rep", None, "pts"), P("rep", None, "pts"), P(), P(), P(), P()),
        check_vma=False,
    )
```
